32 devices in a mesh: seq: 16 (over z, y, core), head: 2 (over x).
Axes of the slice: x: 2, y: 2, z: 4, core: 2. Of those that a mesh axis runs over, the one named last changes fastest.
Arguments:
- inputs: bfloat16 [6, 2048, 768], P(None, 'seq'), may hold values from -6 to 6
- attend_weight: bfloat16 [3, 768, 768], P(None, 'seq', 'head'), may hold values from -0.21875 to 0.21875
- merge_weight: bfloat16 [768, 768], P('head', 'seq'), may hold values from -0.21875 to 0.21875
- expand_weight: bfloat16 [768, 3072], P('seq', 'head'), may hold values from -0.21875 to 0.21875
- reduce_weight: bfloat16 [3072, 768], P('head', 'seq'), may hold values from -0.109375 to 0.109375
- gain_first: float32 [768], replicated, may hold values from 0.1 to 1.9
- gain_heads: float32 [768], P('head'), may hold values from 0.1 to 1.9
- gain_second: float32 [768], replicated, may hold values from 0.1 to 1.9
- gain_hidden: float32 [3072], P('head'), may hold values from 0.1 to 1.9
- cotangent: bfloat16 [6, 2048, 768], P(None, 'seq'), may hold values from -6 to 6
- lengths: int32 [6], replicated, may hold values from 1024 to 2048, as said below
- local_span: int32 [6], replicated, may hold values from 32 to 128, as said below
- dilation: int32 [6], replicated, may hold values from 8 to 16, as said below
Outputs:
- block_out: bfloat16 [6, 2048, 768], P(None, 'seq')
- grad_inputs: bfloat16 [6, 2048, 768], P(None, 'seq')
- grad_attend: float32 [3, 768, 768], P(None, 'seq', 'head')
- grad_merge: float32 [768, 768], P('head', 'seq')
- grad_expand: float32 [768, 3072], P('seq', 'head')
- grad_reduce: float32 [3072, 768], P('head', 'seq')
- grad_first: float32 [768], replicated
- grad_heads: float32 [768], P('head')
- grad_second: float32 [768], replicated
- grad_hidden: float32 [3072], P('head')
The draws below stay inside these ranges and needn't reach their ends.
Inputs may be any that keep to these rules, and one draw needn't show every extreme that they name: `lengths`: some row is full, 2048 tokens long. `local_span`: each value divides 128; 128, 64 and 32 each occur. `dilation`: each value is 8 or 16; both occur.
All inputs are finite; a program needn't handle non-finite values.
Results may differ from the reference program's by a relative error of at most 0.02.
Values may be sent and summed in bfloat16 or wider, within the bound.
No kernel may reach another device: no remote copies, remote signals or barrier semaphores. Data moves between devices by JAX's collectives and lax.ppermute only.
A program may use at most 192 MiB of HBM per device.

```python
import jax
import jax.numpy as jnp
from jax import lax

D = 768
HEADS = 12
HD = 64
FF = 3072
ROWS = 6
STRETCH = 128
DILATION_SMALL = 8
ROW_POSITIONS = 2048


def draw_lengths(key, part):
    key = jax.random.fold_in(key, 11)
    key_base, key_full = jax.random.split(key)
    base_len = jax.random.randint(key_base, (ROWS,), ROW_POSITIONS // 2, ROW_POSITIONS + 1)
    full_row = jax.random.randint(key_full, (), 0, ROWS)
    return jnp.where(jnp.arange(ROWS) == full_row, ROW_POSITIONS, base_len).astype(jnp.int32)


def draw_local_span(key, part):
    key = jax.random.fold_in(key, 12)
    order_index = jax.random.permutation(key, ROWS) % 3
    return (STRETCH // jnp.power(2, order_index)).astype(jnp.int32)


def draw_dilation(key, part):
    key = jax.random.fold_in(key, 13)
    order_index = jax.random.permutation(key, ROWS) % 2
    return (DILATION_SMALL * (1 + order_index)).astype(jnp.int32)


def strengthened(drawn, own_key, source, target, parts, factor):
    owner, partner = [(jnp.arange(drawn.shape[position]) // (drawn.shape[position] // parts)).reshape([-1 if axis == position else 1 for axis in range(drawn.ndim)]) for position in (source, target)]
    chosen = jax.random.permutation(own_key, parts)[partner]
    strong = (owner == chosen) | (owner == (partner + parts // 2) % parts)
    return jnp.where(strong, factor * drawn, drawn)


def shard_levels(rng, dims, cuts, least, largest):
    def one(dim, shards_of):
        heights = jax.random.uniform(jax.random.fold_in(jax.random.fold_in(rng, 6), dim), (shards_of,), jnp.float32, least / len(cuts), largest / len(cuts))
        return jnp.repeat(jnp.exp(heights), dims[dim] // shards_of).reshape((-1,) + (1,) * (len(dims) - dim - 1))

    loudness = one(*cuts[0])
    for cut in cuts[1:]:
        loudness = loudness * one(*cut)
    return loudness


def normal_values(own_key, shape, scale, bound, cuts=(), dtype=jnp.bfloat16):
    result = scale * jax.random.normal(own_key, shape, jnp.float32)
    if cuts:
        result = result * shard_levels(own_key, shape, cuts, -0.22, 0.18)
    return jnp.clip(result, -bound, bound).astype(dtype)


def heavy_noise(key, dims, scale, bound, pieces, heavy, kind=jnp.bfloat16):
    drawn = scale * jax.random.normal(key, dims, jnp.float32)
    if pieces:
        drawn = drawn * shard_levels(key, dims, pieces, -0.22, 0.18)
    return jnp.clip(strengthened(drawn, jax.random.fold_in(key, 3), *heavy), -bound, bound).astype(kind)


def setup_inputs(seed: int = 0) -> dict:
    arg_keys = jax.random.split(jax.random.key(seed), 14)
    inputs = normal_values(arg_keys[0], (ROWS, ROW_POSITIONS, D), 1.0, 6.0, ((1, 16),))
    attend_weight = normal_values(arg_keys[1], (3, D, D), D ** -0.5, 0.21875, ((1, 16), (2, 2)))
    merge_weight = normal_values(arg_keys[2], (D, D), D ** -0.5, 0.21875, ((0, 2), (1, 16)))
    expand_weight = normal_values(arg_keys[3], (D, FF), D ** -0.5, 0.21875, ((0, 16), (1, 2)))
    reduce_weight = normal_values(arg_keys[4], (FF, D), FF ** -0.5, 0.109375, ((0, 2), (1, 16)))
    gain_first = jnp.clip(1.0 + 0.18 * jax.random.normal(arg_keys[5], (D,), jnp.float32), 0.1, 1.9)
    gain_heads = jnp.clip(1.0 + 0.18 * jax.random.normal(arg_keys[6], (D,), jnp.float32), 0.1, 1.9)
    gain_second = jnp.clip(1.0 + 0.18 * jax.random.normal(arg_keys[7], (D,), jnp.float32), 0.1, 1.9)
    gain_hidden = jnp.clip(1.0 + 0.18 * jax.random.normal(arg_keys[8], (FF,), jnp.float32), 0.1, 1.9)
    cotangent = heavy_noise(arg_keys[9], (ROWS, ROW_POSITIONS, D), 1.0, 6.0, ((1, 16),), (1, 2, 16, 2.0))
    lengths = draw_lengths(jax.random.fold_in(arg_keys[13], 71), 0)
    local_span = draw_local_span(jax.random.fold_in(arg_keys[13], 71), 0)
    dilation = draw_dilation(jax.random.fold_in(arg_keys[13], 71), 0)
    return {"inputs": inputs, "attend_weight": attend_weight, "merge_weight": merge_weight, "expand_weight": expand_weight, "reduce_weight": reduce_weight, "gain_first": gain_first, "gain_heads": gain_heads, "gain_second": gain_second, "gain_hidden": gain_hidden, "cotangent": cotangent, "lengths": lengths, "local_span": local_span, "dilation": dilation}


NORM_EPSILON = 1e-05
MASKED_SCORE = -1e+30
PRECISE = lax.Precision.HIGHEST

@jax.custom_vjp
def low(v):
    return lax.optimization_barrier(v.astype(jnp.bfloat16)).astype(jnp.float32)

@jax.custom_vjp
def low_back(v):
    return v

def low_keep(v):
    return (low(v), None)

def low_pass(kept, grad):
    return (grad,)

def back_keep(v):
    return (v, None)

def back_low(kept, grad):
    return (low(grad),)
low.defvjp(low_keep, low_pass)
low_back.defvjp(back_keep, back_low)

def normed(values, gain_row):
    center = lax.optimization_barrier(jnp.mean(values, axis=-1, keepdims=True))
    spread = lax.optimization_barrier(jnp.mean(values * values, axis=-1, keepdims=True)) - center * center
    return (values - center) * lax.rsqrt(spread + NORM_EPSILON) * gain_row

def matmul(left, right):
    return jnp.dot(left, right, precision=PRECISE)

def row_layer(row_in, local_len, dilate_by, weights):
    attend, merging, expand, reducing, gain_first, gain_heads, gain_second, gain_hidden = weights
    score_scale = HD ** (-0.5)
    first_in = low(normed(row_in, gain_first))
    projected = low(low_back(jnp.einsum('td,edf->etf', first_in, attend, precision=PRECISE)))
    queries = projected[0].reshape(ROW_POSITIONS, HEADS, HD)
    keys_all = projected[1].reshape(ROW_POSITIONS, HEADS, HD)
    values_all = projected[2].reshape(ROW_POSITIONS, HEADS, HD)
    blocks = ROW_POSITIONS // STRETCH
    query_blk = queries.reshape(blocks, STRETCH, HEADS, HD)
    key_blk = keys_all.reshape(blocks, STRETCH, HEADS, HD)
    value_blk = values_all.reshape(blocks, STRETCH, HEADS, HD)
    places = jnp.arange(STRETCH)
    within = (places[:, None] // local_len == places[None, :] // local_len) & (places[None, :] <= places[:, None])
    score_near = low_back(jnp.einsum('bihd,bjhd->bhij', query_blk, key_blk, precision=PRECISE) * score_scale)
    score_near = jnp.where(within, score_near, MASKED_SCORE)
    peak_near = lax.optimization_barrier(jnp.max(score_near, axis=-1))
    log_near = peak_near + jnp.log(lax.optimization_barrier(jnp.sum(jnp.exp(score_near - peak_near[..., None]), axis=-1)))
    log_row = jnp.transpose(log_near, (1, 0, 2)).reshape(HEADS, ROW_POSITIONS)
    head_ids = jnp.arange(HEADS)
    slot_index = jnp.arange(ROW_POSITIONS // DILATION_SMALL)
    slot_place = (head_ids % dilate_by)[:, None] + dilate_by * slot_index[None, :]
    slot_live = slot_index < ROW_POSITIONS // dilate_by
    slot_clamp = jnp.minimum(slot_place, ROW_POSITIONS - 1)
    slot_drop = jnp.where(slot_live[None, :], slot_place, ROW_POSITIONS)
    query_far = queries[slot_clamp, head_ids[:, None]]
    key_far = keys_all[slot_clamp, head_ids[:, None]]
    value_far = values_all[slot_clamp, head_ids[:, None]]
    score_far = low_back(jnp.einsum('had,hbd->hab', query_far, key_far, precision=PRECISE) * score_scale)
    allowed = slot_live[:, None] & slot_live[None, :] & (slot_index[None, :] <= slot_index[:, None])
    score_far = jnp.where(allowed[None], score_far, MASKED_SCORE)
    peak_far = lax.optimization_barrier(jnp.max(score_far, axis=-1))
    log_far = peak_far + jnp.log(lax.optimization_barrier(jnp.sum(jnp.exp(score_far - peak_far[..., None]), axis=-1)))
    log_slot = jnp.logaddexp(log_row[head_ids[:, None], slot_clamp], log_far)
    log_full = log_row.at[head_ids[:, None], slot_drop].set(log_slot, mode='drop')
    log_blk = jnp.transpose(log_full.reshape(HEADS, blocks, STRETCH), (1, 0, 2))
    weight_near = low(jnp.exp(score_near - log_blk[..., None]))
    weight_far = low(jnp.exp(score_far - log_slot[..., None]))
    mixed_near = jnp.einsum('bhij,bjhd->bihd', weight_near, value_blk, precision=PRECISE).reshape(ROW_POSITIONS, HEADS, HD)
    mixed_far = jnp.einsum('hab,hbd->had', weight_far, value_far, precision=PRECISE)
    attended = mixed_near.at[slot_drop, head_ids[:, None]].add(mixed_far, mode='drop')
    attended = low_back(attended.reshape(ROW_POSITIONS, D))
    heads_in = low(normed(attended, gain_heads))
    residual = row_in + low_back(matmul(heads_in, merging))
    second_in = low(normed(residual, gain_second))
    hidden_pre = low_back(matmul(second_in, expand))
    hidden_in = low(normed(jax.nn.gelu(hidden_pre, approximate=False), gain_hidden))
    return residual + matmul(hidden_in, reducing)

def reference(inputs, attend_weight, merge_weight, expand_weight, reduce_weight, gain_first, gain_heads, gain_second, gain_hidden, cotangent, lengths, local_span, dilation):
    floats = tuple((tensor.astype(jnp.float32) for tensor in (inputs, attend_weight, merge_weight, expand_weight, reduce_weight, gain_first, gain_heads, gain_second, gain_hidden)))

    def forward(row_inputs, *weights):

        def for_each_row(row_items):
            return row_layer(row_items[0], row_items[1], row_items[2], weights)
        return lax.map(jax.checkpoint(for_each_row), (row_inputs, local_span, dilation))
    outputs, pullback = jax.vjp(forward, *floats)
    in_length = jnp.arange(ROW_POSITIONS)[None, :] < lengths[:, None]
    seed_grad = jnp.where(in_length[..., None], cotangent.astype(jnp.float32), jnp.float32(0.0))
    gradients = pullback(seed_grad)
    return (outputs.astype(jnp.bfloat16), gradients[0].astype(jnp.bfloat16), gradients[1], gradients[2], gradients[3], gradients[4], gradients[5], gradients[6], gradients[7], gradients[8])
```

```python
from functools import partial

import jax
import jax.numpy as jnp
from jax import lax
from jax.experimental import pallas as pl
from jax.experimental.pallas import tpu as pltpu
from jax.sharding import PartitionSpec as P

HD = 64
DILATION_SMALL = 8
NORM_EPSILON = 1e-05
MASKED_SCORE = -1e30
SCALE = HD ** (-0.5)
F32 = jnp.float32
BF16 = jnp.bfloat16
ANY = pl.BlockSpec(memory_space=pl.ANY)
SMEM = pl.BlockSpec(memory_space=pltpu.SMEM)
VMEM_LIMIT = 56 * 1024 * 1024


def nn(left, right):
    return lax.dot_general(left, right, (((1,), (0,)), ((), ())), preferred_element_type=F32)


def nt(left, right):
    return lax.dot_general(left, right, (((1,), (1,)), ((), ())), preferred_element_type=F32)


def tn(left, right):
    return lax.dot_general(left, right, (((0,), (0,)), ((), ())), preferred_element_type=F32)


def row_norm(values):
    center = jnp.mean(values, axis=-1, keepdims=True)
    spread = jnp.mean(values * values, axis=-1, keepdims=True) - center * center
    inverse = lax.rsqrt(spread + NORM_EPSILON)
    return (values - center) * inverse, inverse


def row_norm_back(incoming, normal, inverse, gain_row):
    scaled = incoming * gain_row
    first_mean = jnp.mean(scaled, axis=-1, keepdims=True)
    second_mean = jnp.mean(scaled * normal, axis=-1, keepdims=True)
    return inverse * (scaled - first_mean - normal * second_mean)


def three_parts(values):
    high = values.astype(BF16)
    rest = values - high.astype(F32)
    middle = rest.astype(BF16)
    low = (rest - middle.astype(F32)).astype(BF16)
    return high, middle, low


def gelu_parts(values):
    expo = jnp.exp(values * values * -0.5)
    term = 1.0 / (1.0 + (0.3275911 * 0.7071067811865476) * jnp.abs(values))
    poly = term * (
        0.254829592
        + term
        * (-0.284496736 + term * (1.421413741 + term * (-1.453152027 + term * 1.061405429)))
    )
    tail = 0.5 * poly * expo
    phi = jnp.where(values >= 0.0, 1.0 - tail, tail)
    return values * phi, phi + values * expo * 0.3989422804014327


def iota(shape, dim):
    return lax.broadcasted_iota(jnp.int32, shape, dim)


def exchange(value, seq_mask, head_mask):
    seq_size, head_size = lax.axis_size("seq"), lax.axis_size("head")
    pairs = [
        (s * head_size + h, (s ^ seq_mask) * head_size + (h ^ head_mask))
        for s in range(seq_size)
        for h in range(head_size)
    ]
    return lax.ppermute(value, ("seq", "head"), pairs)


def far_stages(seq_size):
    unit, left, stages = 4, seq_size // 4, []
    while left > 1:
        radix = 4 if left % 4 == 0 else 2
        stages.append((unit, radix))
        unit, left = unit * radix, left // radix
    return stages


def shard_masks(seq_size):
    return [
        4 * z + 2 * y + core for core in range(2) for y in range(2) for z in range(seq_size // 4)
    ]


def gather_chunk(shard):
    seq_size = lax.axis_size("seq")
    rows, width = shard.shape
    half = width // 2
    held = shard[None]
    for unit, radix in far_stages(seq_size):
        held = jnp.stack([held] + [exchange(held, unit * i, 0) for i in range(1, radix)])
        held = held.reshape(-1, rows, width)
    part_a, part_b = held[..., :half], held[..., half:]
    next_a, next_b = exchange(part_a, 0, 1), exchange(part_b, 2, 0)
    part_a, part_b = jnp.stack([part_a, next_a]), jnp.stack([part_b, next_b])
    next_a, next_b = exchange(part_a, 2, 0), exchange(part_b, 0, 1)
    part_a = jnp.stack([part_a, next_a], axis=1)
    part_b = jnp.stack([part_b, next_b], axis=0)
    own = jnp.stack([part_a, part_b])
    other = exchange(own, 1, 0)
    shape = (2, 2, seq_size // 2 * rows, half)
    return own.reshape(shape), other.reshape(shape)


def scatter_chunk(own, other):
    seq_size = lax.axis_size("seq")
    half_count, head_size, rows_all, half = own.shape
    rows = rows_all * 2 // seq_size
    shape = (half_count, head_size, 2, seq_size // 4, rows, half)
    got = exchange(other, 1, 0).reshape(shape)
    own = own.reshape(shape)
    total = own.astype(F32) + got.astype(F32)
    part_a, part_b = total[0], total[1]
    next_a = exchange(part_a[:, 1].astype(BF16), 2, 0)
    next_b = exchange(part_b[1].astype(BF16), 0, 1)
    part_a = part_a[:, 0] + next_a.astype(F32)
    part_b = part_b[0] + next_b.astype(F32)
    next_a = exchange(part_a[1].astype(BF16), 0, 1)
    next_b = exchange(part_b[1].astype(BF16), 2, 0)
    held = jnp.stack(
        [part_a[0] + next_a.astype(F32), part_b[0] + next_b.astype(F32)], axis=1
    )
    for unit, radix in reversed(far_stages(seq_size)):
        held = held.reshape(radix, -1, *held.shape[1:])
        low = held.astype(BF16)
        kept = held[0]
        for i in range(1, radix):
            kept = kept + exchange(low[i], unit * i, 0).astype(F32)
        held = kept
    return held[0]


def copies_of(pairs, sems):
    return [
        pltpu.make_async_copy(source, target, sems.at[i]) for i, (source, target) in enumerate(pairs)
    ]


def attend_copies(own, other, pair_w, value_w, sems):
    half_rows = own.shape[2]
    width = value_w.shape[2]
    pairs = []
    for hh in range(2):
        for c, source in enumerate((own, other)):
            rows = pl.ds(c * half_rows, half_rows)
            pairs.append((source.at[0, hh], pair_w.at[hh, rows]))
            pairs.append((source.at[1, hh, :, pl.ds(0, width)], value_w.at[hh, rows]))
    return copies_of(pairs, sems)


def head_columns(head, per_group, width):
    group, inside = divmod(head, per_group)
    start = group * 3 * width + inside * HD
    return [slice(start + e * width, start + e * width + HD) for e in range(3)]


def slot_select(offset, groups, positions):
    shape = (groups, positions)
    return (iota(shape, 1) == DILATION_SMALL * iota(shape, 0) + offset).astype(BF16)


def project_kernel(
    offs, x_ref, bias_ref, gain_ref, own, other, first_ref, qkv_ref, slot_ref, out_ref, lse_ref,
    pair_w, value_w, sems,
):
    positions, model = x_ref.shape[1:]
    width = value_w.shape[2]
    heads = model // HD
    per_group = heads // 2

    @pl.when(pl.program_id(0) == 0)
    def _():
        copies = attend_copies(own, other, pair_w, value_w, sems)
        for copy in copies:
            copy.start()
        for copy in copies:
            copy.wait()

    normal, _ = row_norm(x_ref[0].astype(F32))
    first = (normal * gain_ref[...]).astype(BF16)
    first_ref[0] = first
    for hh in range(2):
        start = hh * 3 * width
        qkv_ref[0, :, start : start + 2 * width] = nn(first, pair_w[hh]).astype(BF16)
        qkv_ref[0, :, start + 2 * width : start + 3 * width] = nn(first, value_w[hh]).astype(BF16)
    bias = bias_ref[0]
    lane = iota((positions, 2 * HD), 1)
    groups = positions // DILATION_SMALL
    for pair in range(heads // 2):
        outs, logs = [], []
        for head in (2 * pair, 2 * pair + 1):
            cq, ck, cv = head_columns(head, per_group, width)
            query, key, value = qkv_ref[0, :, cq], qkv_ref[0, :, ck], qkv_ref[0, :, cv]
            chosen = slot_select(offs[head], groups, positions)
            slot_ref[head] = nn(chosen, jnp.concatenate([query, key, value], axis=1)).astype(BF16)
            score = nt(query, key) * SCALE + bias
            peak = jnp.max(score, axis=-1, keepdims=True)
            expo = jnp.exp(score - peak)
            total = jnp.sum(expo, axis=-1, keepdims=True)
            outs.append(nn(expo.astype(BF16), value) / total)
            logs.append(peak + jnp.log(total))
        columns = slice(2 * pair * HD, 2 * (pair + 1) * HD)
        out_ref[0, :, columns] = jnp.concatenate(outs, axis=1)
        lse_ref[0, :, columns] = jnp.where(lane < HD, logs[0], logs[1])


def far_masks(parity, row_start, row_count, slots):
    row = row_start + iota((row_count, slots), 0)
    column = iota((row_count, slots), 1)
    live_row = (parity == 0) | ((row & 1) == parity - 1)
    live_column = (parity == 0) | ((column & 1) == parity - 1)
    return (column <= row) & live_column, live_row


def for_blocks(count, body):
    if count == 1:
        body(0)
    else:
        lax.fori_loop(0, count, lambda b, carry: (body(b), carry)[1], 0)


def far_kernel(parity_ref, qkv_ref, out_ref, kv_scr):
    devices, _, groups, _ = qkv_ref.shape
    slots = devices * groups
    block = min(slots, 256)
    per_block = block // groups
    parity = parity_ref[pl.program_id(0)]
    kv_scr[...] = qkv_ref[:, 0].reshape(slots, 3 * HD)[:, HD:]

    def body(index):
        piece = pl.ds(index * per_block, per_block)
        query = qkv_ref[piece, 0].reshape(block, 3 * HD)[:, :HD]
        key, value = kv_scr[:, :HD], kv_scr[:, HD:]
        allowed, live = far_masks(parity, index * block, block, slots)
        score = jnp.where(allowed, nt(query, key) * SCALE, MASKED_SCORE)
        peak = jnp.max(score, axis=-1, keepdims=True)
        expo = jnp.exp(score - peak)
        total = jnp.sum(expo, axis=-1, keepdims=True)
        out = nn(expo.astype(BF16), value) / total
        log = jnp.where(live[:, :1], peak + jnp.log(total), MASKED_SCORE)
        high, middle, low = three_parts(log)
        lane = iota((block, 2 * HD), 1)
        tile = jnp.concatenate([out, out], axis=1)
        tile = jnp.where(lane == HD, high.astype(F32), tile)
        tile = jnp.where(lane == HD + 1, middle.astype(F32), tile)
        tile = jnp.where(lane == HD + 2, low.astype(F32), tile)
        out_ref[piece, 0] = tile.astype(BF16).reshape(per_block, groups, 2 * HD)

    for_blocks(slots // block, body)


def middle_kernel(
    offs, x_ref, near_ref, log_ref, far_ref, seed_ref, gain_heads, gain_second, gain_hidden,
    place_ref, own_1, other_1, own_2, other_2, own_3, other_3,
    block_ref, heads_ref, second_ref, hidden_ref, pre_ref, resid_ref, low_ref, att_ref, lse_ref,
    dot_ref, slot_ref, grad_heads, grad_second, grad_hidden,
    merge_w, expand_w, reduce_w, act_scr, slope_scr, grad_scr, sems,
):
    positions, model = x_ref.shape[1:]
    half_rows, half = own_2.shape[2], own_2.shape[3]
    width = merge_w.shape[2]
    heads = model // HD
    groups = positions // DILATION_SMALL
    hidden_width = 4 * half
    step = pl.program_id(0)
    merge_pairs, expand_pairs, reduce_pairs = [], [], []
    for hh in range(2):
        for c, (one, two, three) in enumerate(((own_1, own_2, own_3), (other_1, other_2, other_3))):
            rows = pl.ds(c * half_rows, half_rows)
            merge_pairs.append((one.at[1, hh, :, pl.ds(half - width, width)], merge_w.at[hh, rows]))
            for part in range(2):
                expand_pairs.append((two.at[part, hh], expand_w.at[2 * hh + part, rows]))
                reduce_pairs.append((three.at[part, hh], reduce_w.at[2 * hh + part, rows]))
    copies = copies_of(merge_pairs + expand_pairs + reduce_pairs, sems)

    def await_copies(start, count):
        @pl.when(step == 0)
        def _():
            for copy in copies[start : start + count]:
                copy.wait()

    @pl.when(step == 0)
    def _():
        for copy in copies:
            copy.start()
        grad_heads[...] = jnp.zeros_like(grad_heads)
        grad_second[...] = jnp.zeros_like(grad_second)
        grad_hidden[...] = jnp.zeros_like(grad_hidden)

    lane = iota((positions, 2 * HD), 1)
    place = iota((positions, 2 * HD), 0)
    for pair in range(heads // 2):
        spread, logs = [], []
        for head in (2 * pair, 2 * pair + 1):
            chosen = slot_select(offs[head], groups, positions)
            tile = tn(chosen, far_ref[head])
            log = jnp.sum(
                jnp.where((lane >= HD) & (lane < HD + 3), tile, 0.0), axis=-1, keepdims=True
            )
            here = (place & (DILATION_SMALL - 1)) == offs[head]
            spread.append(tile[:, :HD])
            logs.append(jnp.where(here, log, MASKED_SCORE))
        columns = slice(2 * pair * HD, 2 * (pair + 1) * HD)
        log_near = log_ref[0, :, columns]
        log_far = jnp.where(lane < HD, logs[0], logs[1])
        peak = jnp.maximum(log_near, log_far)
        weight_near, weight_far = jnp.exp(log_near - peak), jnp.exp(log_far - peak)
        total = weight_near + weight_far
        lse_ref[0, :, columns] = peak + jnp.log(total)
        act_scr[:, columns] = (
            near_ref[0, :, columns] * weight_near + jnp.concatenate(spread, axis=1) * weight_far
        ) / total
    attended = act_scr[:, :model]
    normal_heads, inverse_heads = row_norm(attended)
    heads_in = (normal_heads * gain_heads[...]).astype(BF16)
    heads_ref[0] = heads_in
    await_copies(0, 4)
    merged = [nt(heads_in[:, hh * width : (hh + 1) * width], merge_w[hh]) for hh in range(2)]
    residual = x_ref[0].astype(F32) + (merged[0] + merged[1])
    normal_two, inverse_two = row_norm(residual)
    second_in = (normal_two * gain_second[...]).astype(BF16)
    second_ref[0] = second_in
    dot_ref[0] = attended
    await_copies(4, 8)
    total_one = jnp.zeros((positions, 1), F32)
    total_two = jnp.zeros((positions, 1), F32)
    for block in range(4):
        columns = slice(block * half, (block + 1) * half)
        act, slope = gelu_parts(nn(second_in, expand_w[block]))
        act_scr[:, columns] = act
        slope_scr[:, columns] = slope
        total_one += jnp.sum(act, axis=-1, keepdims=True)
        total_two += jnp.sum(act * act, axis=-1, keepdims=True)
    center = total_one / hidden_width
    inverse = lax.rsqrt(total_two / hidden_width - center * center + NORM_EPSILON)
    await_copies(12, 8)
    seed = seed_ref[0]
    total_one = jnp.zeros((positions, 1), F32)
    total_two = jnp.zeros((positions, 1), F32)
    block_out = jnp.zeros((positions, model), F32)
    for block in range(4):
        columns = slice(block * half, (block + 1) * half)
        normal = (act_scr[:, columns] - center) * inverse
        act_scr[:, columns] = normal
        gain = gain_hidden[:, columns]
        hidden_in = (normal * gain).astype(BF16)
        hidden_ref[0, :, columns] = hidden_in
        block_out += nt(hidden_in, reduce_w[block])
        grad = nn(seed, reduce_w[block])
        through = grad * normal
        grad_hidden[:, columns] += jnp.sum(through, axis=0, keepdims=True)
        total_one += jnp.sum(grad * gain, axis=-1, keepdims=True)
        total_two += jnp.sum(through * gain, axis=-1, keepdims=True)
        grad_scr[:, columns] = grad
    block_ref[0] = nt((residual + block_out).astype(BF16), place_ref[...]).astype(BF16)
    total_one = total_one / hidden_width
    total_two = total_two / hidden_width
    grad_second_in = jnp.zeros((positions, model), F32)
    for block in range(4):
        columns = slice(block * half, (block + 1) * half)
        grad = grad_scr[:, columns] * gain_hidden[:, columns]
        grad = inverse * (grad - total_one - act_scr[:, columns] * total_two)
        grad_pre = (grad * slope_scr[:, columns]).astype(BF16)
        pre_ref[0, :, columns] = grad_pre
        grad_second_in += nt(grad_pre, expand_w[block])
    grad_second[...] += jnp.sum(grad_second_in * normal_two, axis=0, keepdims=True)
    resid = seed.astype(F32) + row_norm_back(
        grad_second_in, normal_two, inverse_two, gain_second[...]
    )
    resid_ref[0] = resid
    resid_low = resid.astype(BF16)
    low_ref[0] = resid_low
    grad_heads_in = jnp.concatenate([nn(resid_low, merge_w[hh]) for hh in range(2)], axis=1)
    attended = dot_ref[0]
    normal_heads, inverse_heads = row_norm(attended)
    grad_heads[...] += jnp.sum(grad_heads_in * normal_heads, axis=0, keepdims=True)
    grad_att = row_norm_back(
        grad_heads_in, normal_heads, inverse_heads, gain_heads[...]
    ).astype(BF16)
    att_ref[0] = grad_att
    product = grad_att.astype(F32) * attended
    same = (iota((2 * HD, 2 * HD), 0) // HD == iota((2 * HD, 2 * HD), 1) // HD).astype(BF16)
    slot_lane = iota((groups, 2 * HD), 1)
    for pair in range(heads // 2):
        columns = slice(2 * pair * HD, 2 * (pair + 1) * HD)
        dots = sum(nn(part, same) for part in three_parts(product[:, columns]))
        dot_ref[0, :, columns] = dots
        lse = lse_ref[0, :, columns]
        for inside, head in enumerate((2 * pair, 2 * pair + 1)):
            chosen = slot_select(offs[head], groups, positions)
            part = slice(inside * HD, (inside + 1) * HD)
            grad_slot = nn(chosen, att_ref[0, :, head * HD : (head + 1) * HD])
            tile = jnp.concatenate([grad_slot, grad_slot], axis=1)
            for index, piece in enumerate(
                three_parts(lse[:, part]) + three_parts(dots[:, part])
            ):
                value = nn(chosen, piece)
                tile = jnp.where(
                    slot_lane == HD + index, jnp.concatenate([value, value], axis=1), tile
                )
            slot_ref[head] = tile.astype(BF16)


def far_back_kernel(parity_ref, qkv_ref, grad_ref, out_ref, kv_scr, total_scr):
    devices, _, groups, _ = qkv_ref.shape
    slots = devices * groups
    block = min(slots, 256)
    per_block = block // groups
    parity = parity_ref[pl.program_id(0)]
    kv_scr[...] = qkv_ref[:, 0].reshape(slots, 3 * HD)[:, HD:]
    total_scr[...] = jnp.zeros_like(total_scr)

    def body(index):
        piece = pl.ds(index * per_block, per_block)
        query = qkv_ref[piece, 0].reshape(block, 3 * HD)[:, :HD]
        tile = grad_ref[piece, 0].reshape(block, 2 * HD)
        key, value = kv_scr[:, :HD], kv_scr[:, HD:]
        grad = tile[:, :HD]
        stats = tile[:, HD:].astype(F32)
        log = stats[:, 0:1] + stats[:, 1:2] + stats[:, 2:3]
        dots = stats[:, 3:4] + stats[:, 4:5] + stats[:, 5:6]
        allowed, live = far_masks(parity, index * block, block, slots)
        score = jnp.where(allowed & live, nt(query, key) * SCALE - log, MASKED_SCORE)
        weight = jnp.exp(score)
        grad_score = (weight * (nt(grad, value) - dots)).astype(BF16)
        grad_query = nn(grad_score, key) * SCALE
        total_scr[:, :HD] += tn(grad_score, query) * SCALE
        total_scr[:, HD:] += tn(weight.astype(BF16), grad)
        out_ref[piece, 0, :, :HD] = grad_query.astype(BF16).reshape(per_block, groups, HD)

    for_blocks(slots // block, body)
    out_ref[:, 0, :, HD:] = total_scr[...].astype(BF16).reshape(devices, groups, 2 * HD)


def near_back_kernel(offs, bias_ref, qkv_ref, att_ref, lse_ref, dot_ref, far_ref, out_ref):
    positions, model = att_ref.shape[1:]
    heads = model // HD
    per_group = heads // 2
    width = per_group * HD
    groups = positions // DILATION_SMALL
    bias = bias_ref[0]
    for head in range(heads):
        cq, ck, cv = head_columns(head, per_group, width)
        query, key, value = qkv_ref[0, :, cq], qkv_ref[0, :, ck], qkv_ref[0, :, cv]
        own = slice(head * HD, (head + 1) * HD)
        grad = att_ref[0, :, own]
        log = lse_ref[0, :, head * HD : head * HD + 1]
        dots = dot_ref[0, :, head * HD : head * HD + 1]
        weight = jnp.exp(nt(query, key) * SCALE + bias - log)
        grad_score = (weight * (nt(grad, value) - dots)).astype(BF16)
        chosen = slot_select(offs[head], groups, positions)
        far = tn(chosen, far_ref[head])
        out_ref[0, :, cq] = (nn(grad_score, key) * SCALE + far[:, :HD]).astype(BF16)
        out_ref[0, :, ck] = (tn(grad_score, query) * SCALE + far[:, HD : 2 * HD]).astype(BF16)
        out_ref[0, :, cv] = (tn(weight.astype(BF16), grad) + far[:, 2 * HD :]).astype(BF16)


def product_kernel(left_ref, right_ref, out_ref):
    out_ref[0, 0, 0] = tn(left_ref[...], right_ref[...]).astype(BF16)


def attend_grad_kernel(first_ref, low_ref, qkv_ref, heads_ref, out_ref):
    width = heads_ref.shape[1]
    first = first_ref[...]
    out_ref[0, 0, 0] = tn(first, qkv_ref[:, : 2 * width]).astype(BF16)
    out_ref[0, 1, 0, :, :width] = tn(first, qkv_ref[:, 2 * width :]).astype(BF16)
    out_ref[0, 1, 0, :, width:] = tn(low_ref[...], heads_ref[...]).astype(BF16)


def input_grad_kernel(
    x_ref, qkv_ref, resid_ref, gain_ref, place_ref, own, other, grad_ref, gain_grad,
    pair_w, value_w, sems,
):
    width = value_w.shape[2]

    @pl.when(pl.program_id(0) == 0)
    def _():
        copies = attend_copies(own, other, pair_w, value_w, sems)
        for copy in copies:
            copy.start()
        for copy in copies:
            copy.wait()
        gain_grad[...] = jnp.zeros_like(gain_grad)

    normal, inverse = row_norm(x_ref[0].astype(F32))
    grad_first = jnp.zeros(normal.shape, F32)
    for hh in range(2):
        start = hh * 3 * width
        grad_first += nt(qkv_ref[0, :, start : start + 2 * width], pair_w[hh])
        grad_first += nt(qkv_ref[0, :, start + 2 * width : start + 3 * width], value_w[hh])
    gain_grad[...] += jnp.sum(grad_first * normal, axis=0, keepdims=True)
    grad = resid_ref[0] + row_norm_back(grad_first, normal, inverse, gain_ref[...])
    grad_ref[0] = nt(grad.astype(BF16), place_ref[...]).astype(BF16)


def by_row(*tail):
    return pl.BlockSpec((1, *tail), lambda r: (r, *(0 for _ in tail)))


def whole(*shape):
    return pl.BlockSpec(shape, lambda *_: tuple(0 for _ in shape))


def sds(shape, dtype):
    return jax.ShapeDtypeStruct(shape, dtype)


def call(kernel, grid, in_specs, out_specs, out_shape, scratch=(), flops=0, moved=0):
    return pl.pallas_call(
        kernel,
        grid=grid,
        in_specs=in_specs,
        out_specs=out_specs,
        out_shape=out_shape,
        scratch_shapes=list(scratch),
        compiler_params=pltpu.CompilerParams(
            dimension_semantics=("arbitrary",) * len(grid), vmem_limit_bytes=VMEM_LIMIT
        ),
        cost_estimate=pl.CostEstimate(flops=flops, bytes_accessed=moved, transcendentals=0),
    )


def per_device(
    inputs,
    attend_weight,
    merge_weight,
    expand_weight,
    reduce_weight,
    gain_first,
    gain_heads,
    gain_second,
    gain_hidden,
    cotangent,
    lengths,
    local_span,
    dilation,
):
    seq_size, head_size = lax.axis_size("seq"), lax.axis_size("head")
    row_count, positions, model = inputs.shape
    rows = row_count // head_size
    tokens = rows * positions
    shard_rows, width = attend_weight.shape[1:]
    heads = width * head_size // HD
    group_heads = heads // head_size
    hidden_here = expand_weight.shape[1]
    hidden_width = hidden_here * head_size
    half = hidden_here // 2
    half_rows = model // 2
    groups = positions // DILATION_SMALL
    pairs = rows * heads
    owned = -(-pairs // seq_size)
    padded = owned * seq_size
    seq_index, head_index = lax.axis_index("seq"), lax.axis_index("head")

    chunk_1 = jnp.concatenate(
        [attend_weight[0], attend_weight[1], attend_weight[2], merge_weight.T], axis=1
    )
    own_1, other_1 = gather_chunk(chunk_1)
    own_2, other_2 = gather_chunk(expand_weight)
    own_3, other_3 = gather_chunk(reduce_weight.T)
    both_gains = jnp.concatenate([gain_heads, gain_hidden])
    partner_gains = exchange(both_gains.reshape(-1, 128), 0, 1).reshape(-1)
    gain_heads_all = jnp.concatenate([gain_heads, partner_gains[:width]])[None]
    gain_hidden_all = jnp.concatenate([gain_hidden, partner_gains[width:]])[None]

    masks = jnp.array(shard_masks(seq_size), jnp.int32)
    block_of = seq_index ^ masks
    feature_of = (block_of[:, None] * shard_rows + jnp.arange(shard_rows)).reshape(-1)
    place = (jnp.arange(model)[:, None] == feature_of[None, :]).astype(BF16)

    def to_own_order(gain):
        return jnp.take(gain.reshape(seq_size, shard_rows), block_of, axis=0).reshape(1, model)

    gain_one, gain_two = to_own_order(gain_first), to_own_order(gain_second)
    row_start = head_index * rows

    def own_rows(tensor):
        return lax.dynamic_slice_in_dim(tensor, row_start, rows, axis=0)

    in_own_order = partial(jnp.einsum, "rtd,de->rte", preferred_element_type=F32)
    x_own = in_own_order(own_rows(inputs), place).astype(BF16)
    places = jnp.arange(positions)
    in_length = (seq_index * positions + places)[None, :] < own_rows(lengths)[:, None]
    seed = jnp.where(in_length[..., None], own_rows(cotangent), jnp.zeros((), BF16))
    seed = in_own_order(seed, place).astype(BF16)
    span_block = places[None, :] // own_rows(local_span)[:, None]
    within = (span_block[:, :, None] == span_block[:, None, :]) & (
        places[None, :] <= places[:, None]
    )
    bias = jnp.where(within, 0.0, MASKED_SCORE).astype(F32)

    local_head = jnp.arange(heads)
    head_ids = (head_index ^ (local_head // group_heads)) * group_heads + local_head % group_heads
    offsets = (head_ids % DILATION_SMALL).astype(jnp.int32)
    pair_ids = jnp.minimum(seq_index * owned + jnp.arange(owned), pairs - 1)
    pair_rate = own_rows(dilation)[pair_ids // heads]
    pair_head = head_ids[pair_ids % heads]
    parity = jnp.where(
        pair_rate == DILATION_SMALL, 0, 1 + (pair_head % pair_rate) // DILATION_SMALL
    ).astype(jnp.int32)

    attend_scratch = [
        pltpu.VMEM((2, model, 2 * width), BF16),
        pltpu.VMEM((2, model, width), BF16),
        pltpu.SemaphoreType.DMA((8,)),
    ]
    first_in, qkv, slots, near, log_near = call(
        project_kernel,
        (rows,),
        [SMEM, by_row(positions, model), by_row(positions, positions), whole(1, model), ANY, ANY],
        [
            by_row(positions, model),
            by_row(positions, 3 * model),
            pl.BlockSpec((heads, groups, 3 * HD), lambda r: (r, 0, 0)),
            by_row(positions, model),
            by_row(positions, model),
        ],
        [
            sds((rows, positions, model), BF16),
            sds((rows, positions, 3 * model), BF16),
            sds((padded, groups, 3 * HD), BF16),
            sds((rows, positions, model), F32),
            sds((rows, positions, model), F32),
        ],
        attend_scratch,
        flops=2 * tokens * model * 3 * model,
        moved=16 * tokens * model,
    )(offsets, x_own, bias, gain_one, own_1, other_1)

    def to_owners(value):
        value = value.reshape(seq_size, owned, groups, value.shape[-1])
        return lax.all_to_all(value, "seq", 0, 0, tiled=True)

    def from_owners(value):
        value = lax.all_to_all(value, "seq", 0, 0, tiled=True)
        return value.reshape(padded, groups, value.shape[-1])

    def by_pair(size):
        return pl.BlockSpec((seq_size, 1, groups, size), lambda i: (0, i, 0, 0))

    def owned_shape(size):
        return sds((seq_size, owned, groups, size), BF16)

    slot_count = seq_size * groups
    kv_scratch = pltpu.VMEM((slot_count, 2 * HD), BF16)
    far_qkv = to_owners(slots)
    far_out = call(
        far_kernel,
        (owned,),
        [SMEM, by_pair(3 * HD)],
        by_pair(2 * HD),
        owned_shape(2 * HD),
        [kv_scratch],
        flops=4 * owned * slot_count**2 * HD,
        moved=owned * slot_count * HD * 10,
    )(parity, far_qkv)
    far_here = from_owners(far_out)

    def of_row(size):
        return pl.BlockSpec((heads, groups, size), lambda r: (r, 0, 0))

    model_row, hidden_row = by_row(positions, model), by_row(positions, hidden_width)
    model_shape = (rows, positions, model)
    hidden_shape = (rows, positions, hidden_width)
    (
        block_mine, heads_in, second_in, hidden_in, grad_pre, grad_resid, resid_low, grad_att,
        log_all, row_dot, grad_slots, grad_heads, grad_second, grad_hidden,
    ) = call(
        middle_kernel,
        (rows,),
        [
            SMEM, model_row, model_row, model_row, of_row(2 * HD), model_row, whole(1, model),
            whole(1, model), whole(1, hidden_width), whole(model, model),
            ANY, ANY, ANY, ANY, ANY, ANY,
        ],
        [
            model_row, model_row, model_row, hidden_row, hidden_row, model_row, model_row,
            model_row, model_row, model_row, of_row(2 * HD), whole(1, model), whole(1, model),
            whole(1, hidden_width),
        ],
        [
            sds(model_shape, BF16), sds(model_shape, BF16), sds(model_shape, BF16),
            sds(hidden_shape, BF16), sds(hidden_shape, BF16), sds(model_shape, F32),
            sds(model_shape, BF16), sds(model_shape, BF16), sds(model_shape, F32),
            sds(model_shape, F32), sds((padded, groups, 2 * HD), BF16), sds((1, model), F32),
            sds((1, model), F32), sds((1, hidden_width), F32),
        ],
        [
            pltpu.VMEM((2, model, width), BF16),
            pltpu.VMEM((4, model, half), BF16),
            pltpu.VMEM((4, model, half), BF16),
            pltpu.VMEM((positions, hidden_width), F32),
            pltpu.VMEM((positions, hidden_width), F32),
            pltpu.VMEM((positions, hidden_width), F32),
            pltpu.SemaphoreType.DMA((20,)),
        ],
        flops=8 * tokens * model * hidden_width,
        moved=4 * model * hidden_width,
    )(
        offsets, x_own, near, log_near, far_here, seed, gain_heads_all, gain_two,
        gain_hidden_all, place, own_1, other_1, own_2, other_2, own_3, other_3,
    )

    def flat(tensor):
        return tensor.reshape(tokens, tensor.shape[-1])

    def weight_grad(left, right):
        return call(
            product_kernel,
            (2, 2, 2),
            [
                pl.BlockSpec((tokens, half_rows), lambda c, x, p: (0, c)),
                pl.BlockSpec((tokens, half), lambda c, x, p: (0, 2 * x + p)),
            ],
            pl.BlockSpec((1, 1, 1, half_rows, half), lambda c, x, p: (c, p, x, 0, 0)),
            sds((2, 2, 2, half_rows, half), BF16),
            flops=2 * tokens * model * hidden_width,
            moved=2 * model * hidden_width,
        )(flat(left), flat(right))

    reduce_parts = weight_grad(seed, hidden_in)
    grad_reduce = scatter_chunk(reduce_parts[0], reduce_parts[1])
    expand_parts = weight_grad(second_in, grad_pre)
    grad_expand = scatter_chunk(expand_parts[0], expand_parts[1])

    def both_rows(mine):
        other = exchange(mine, 0, 1)
        first = jnp.where(head_index == 0, mine, other)
        second = jnp.where(head_index == 0, other, mine)
        return jnp.concatenate([first, second])

    block_out = both_rows(block_mine)

    far_grads = to_owners(grad_slots)
    far_back = call(
        far_back_kernel,
        (owned,),
        [SMEM, by_pair(3 * HD), by_pair(2 * HD)],
        by_pair(3 * HD),
        owned_shape(3 * HD),
        [kv_scratch, pltpu.VMEM((slot_count, 2 * HD), F32)],
        flops=10 * owned * slot_count**2 * HD,
        moved=owned * slot_count * HD * 16,
    )(parity, far_qkv, far_grads)
    back_here = from_owners(far_back)
    grad_qkv = call(
        near_back_kernel,
        (rows,),
        [
            SMEM, by_row(positions, positions), by_row(positions, 3 * model), model_row,
            model_row, model_row, of_row(3 * HD),
        ],
        by_row(positions, 3 * model),
        sds((rows, positions, 3 * model), BF16),
        flops=10 * tokens * positions * model,
        moved=20 * tokens * model,
    )(offsets, bias, qkv, grad_att, log_all, row_dot, back_here)

    def left_spec(size):
        return pl.BlockSpec((tokens, size), lambda c, x: (0, c))

    def right_spec(size):
        return pl.BlockSpec((tokens, size), lambda c, x: (0, x))

    attend_parts = call(
        attend_grad_kernel,
        (2, 2),
        [left_spec(half_rows), left_spec(half_rows), right_spec(3 * width), right_spec(width)],
        pl.BlockSpec((1, 2, 1, half_rows, 2 * width), lambda c, x: (c, 0, x, 0, 0)),
        sds((2, 2, 2, half_rows, 2 * width), BF16),
        flops=2 * tokens * model * 4 * model,
        moved=8 * model * model,
    )(flat(first_in), flat(resid_low), flat(grad_qkv), flat(heads_in))
    grad_attend = scatter_chunk(attend_parts[0], attend_parts[1])

    grad_mine, grad_first = call(
        input_grad_kernel,
        (rows,),
        [
            model_row, by_row(positions, 3 * model), model_row, whole(1, model),
            whole(model, model), ANY, ANY,
        ],
        [model_row, whole(1, model)],
        [sds(model_shape, BF16), sds((1, model), F32)],
        attend_scratch,
        flops=2 * tokens * model * 3 * model,
        moved=8 * model * model,
    )(x_own, grad_qkv, grad_resid, gain_one, place, own_1, other_1)
    grad_inputs = both_rows(grad_mine)

    inverse_masks = [0] * seq_size
    for index, mask in enumerate(shard_masks(seq_size)):
        inverse_masks[mask] = index
    found = jnp.array(inverse_masks, jnp.int32)[seq_index ^ jnp.arange(seq_size)]

    def to_common_order(grad):
        return jnp.take(grad.reshape(seq_size, shard_rows), found, axis=0).reshape(-1)

    shared = [to_common_order(grad_first), to_common_order(grad_second)]
    kept = jnp.concatenate(shared + [grad_heads[0, :width], grad_hidden[0, :hidden_here]])
    sent = jnp.concatenate(shared + [grad_heads[0, width:], grad_hidden[0, hidden_here:]])
    total = kept.reshape(-1, 128) + exchange(sent.reshape(-1, 128), 0, 1)
    mask = 1
    while mask < seq_size:
        total = total + exchange(total, mask, 0)
        mask *= 2
    total = total.reshape(-1)

    return (
        block_out,
        grad_inputs,
        jnp.stack(
            [grad_attend[0, :, :width], grad_attend[0, :, width:], grad_attend[1, :, :width]]
        ),
        grad_attend[1, :, width:].T,
        jnp.concatenate([grad_expand[0], grad_expand[1]], axis=1),
        jnp.concatenate([grad_reduce[0], grad_reduce[1]], axis=1).T,
        total[:model],
        total[2 * model : 2 * model + width],
        total[model : 2 * model],
        total[2 * model + width :],
    )


def solution(mesh):
    placed = (
        P(None, "seq", None),
        P(None, "seq", "head"),
        P("head", "seq"),
        P("seq", "head"),
        P("head", "seq"),
        P(),
        P("head"),
        P(),
        P("head"),
        P(None, "seq", None),
        P(),
        P(),
        P(),
    )
    return jax.shard_map(
        per_device,
        mesh=mesh,
        in_specs=placed,
        out_specs=(
            P(None, "seq", None),
            P(None, "seq", None),
            P(None, "seq", "head"),
            P("head", "seq"),
            P("seq", "head"),
            P("head", "seq"),
            P(),
            P("head"),
            P(),
            P("head"),
        ),
        check_vma=False,
    )
```

```python
from functools import partial

import jax
import jax.numpy as jnp
from jax import lax
from jax.experimental import pallas as pl
from jax.experimental.pallas import tpu as pltpu
from jax.sharding import PartitionSpec as P

HD = 64
DILATION_SMALL = 8
NORM_EPSILON = 1e-05
MASKED_SCORE = -1e30
SCALE = HD ** (-0.5)
F32 = jnp.float32
BF16 = jnp.bfloat16
ANY = pl.BlockSpec(memory_space=pl.ANY)
SMEM = pl.BlockSpec(memory_space=pltpu.SMEM)
VMEM_LIMIT = 56 * 1024 * 1024


def nn(left, right):
    return lax.dot_general(left, right, (((1,), (0,)), ((), ())), preferred_element_type=F32)


def nt(left, right):
    return lax.dot_general(left, right, (((1,), (1,)), ((), ())), preferred_element_type=F32)


def tn(left, right):
    return lax.dot_general(left, right, (((0,), (0,)), ((), ())), preferred_element_type=F32)


def row_norm(values):
    center = jnp.mean(values, axis=-1, keepdims=True)
    spread = jnp.mean(values * values, axis=-1, keepdims=True) - center * center
    inverse = lax.rsqrt(spread + NORM_EPSILON)
    return (values - center) * inverse, inverse


def row_norm_back(incoming, normal, inverse, gain_row):
    scaled = incoming * gain_row
    first_mean = jnp.mean(scaled, axis=-1, keepdims=True)
    second_mean = jnp.mean(scaled * normal, axis=-1, keepdims=True)
    return inverse * (scaled - first_mean - normal * second_mean)


def three_parts(values):
    high = values.astype(BF16)
    rest = values - high.astype(F32)
    middle = rest.astype(BF16)
    low = (rest - middle.astype(F32)).astype(BF16)
    return high, middle, low


def gelu_parts(values):
    expo = jnp.exp(values * values * -0.5)
    term = 1.0 / (1.0 + (0.3275911 * 0.7071067811865476) * jnp.abs(values))
    poly = term * (
        0.254829592
        + term
        * (-0.284496736 + term * (1.421413741 + term * (-1.453152027 + term * 1.061405429)))
    )
    tail = 0.5 * poly * expo
    phi = jnp.where(values >= 0.0, 1.0 - tail, tail)
    return values * phi, phi + values * expo * 0.3989422804014327


def iota(shape, dim):
    return lax.broadcasted_iota(jnp.int32, shape, dim)


def permute(value, target):
    seq_size, head_size = lax.axis_size("seq"), lax.axis_size("head")
    pairs = []
    for s in range(seq_size):
        for h in range(head_size):
            to_seq, to_head = target(s, h)
            pairs.append((s * head_size + h, to_seq * head_size + to_head))
    return lax.ppermute(value, ("seq", "head"), pairs)


def exchange(value, seq_mask, head_mask):
    return permute(value, lambda s, h: (s ^ seq_mask, h ^ head_mask))


def exchange_near(value, turn):
    return permute(value, lambda s, h: (s, h ^ 1) if (s & 1) == turn else (s ^ 2, h))


def far_stages(seq_size):
    unit, left, stages = 4, seq_size // 4, []
    while left > 1:
        radix = 4 if left % 4 == 0 else 2
        stages.append((unit, radix))
        unit, left = unit * radix, left // radix
    return stages


def join(pieces, earlier=(), splits=None):
    rows, width = pieces[0].shape
    count = len(pieces)
    splits = splits or (width,)
    starts = [sum(splits[:i]) for i in range(len(splits))]
    if rows % 16:
        whole_array = jnp.concatenate(pieces)
        out = [whole_array[:, start : start + size] for start, size in zip(starts, splits)]
        return out if len(splits) > 1 else out[0]

    def kernel(*refs):
        refs = refs[len(earlier) :]
        sources, targets, sems = refs[:count], refs[count:-1], refs[-1]
        copies = [
            pltpu.make_async_copy(
                source.at[:, pl.ds(start, size)], target.at[pl.ds(i * rows, rows)], sems.at[i, j]
            )
            for i, source in enumerate(sources)
            for j, (target, start, size) in enumerate(zip(targets, starts, splits))
        ]
        start_all(copies)
        wait_all(copies)

    out = pl.pallas_call(
        kernel,
        in_specs=[ANY] * len(earlier) + [pl.BlockSpec(memory_space=pltpu.VMEM)] * count,
        out_specs=[ANY] * len(splits),
        out_shape=[jax.ShapeDtypeStruct((count * rows, size), pieces[0].dtype) for size in splits],
        scratch_shapes=[pltpu.SemaphoreType.DMA((count, len(splits)))],
        cost_estimate=pl.CostEstimate(flops=2_000_000_000, bytes_accessed=0, transcendentals=0),
    )(*earlier, *pieces)
    return out if len(splits) > 1 else out[0]


def gate(value, *earlier):
    def kernel(*refs):
        pass

    return pl.pallas_call(
        kernel,
        in_specs=[ANY] * (len(earlier) + 1),
        out_specs=ANY,
        out_shape=jax.ShapeDtypeStruct(value.shape, value.dtype),
        input_output_aliases={len(earlier): 0},
        cost_estimate=pl.CostEstimate(flops=0, bytes_accessed=0, transcendentals=0),
    )(*earlier, value)


def after(value, earlier):
    zero = earlier[(0,) * earlier.ndim].astype(F32) * 0.0
    return value + zero.astype(value.dtype)


def gather_core(shard):
    core = lax.axis_index("seq") & 1
    half = shard.shape[0] // 2
    kept = lax.dynamic_slice_in_dim(shard, core * half, half)
    sent = lax.dynamic_slice_in_dim(shard, (1 - core) * half, half)
    return jnp.concatenate([kept, exchange(sent, 1, 0)])


def gather_far(held, earlier=()):
    for unit, radix in far_stages(lax.axis_size("seq")):
        pieces = [held] + [exchange(held, unit * i, 0) for i in range(1, radix)]
        held = join(pieces, earlier) if earlier else jnp.concatenate(pieces)
    return held


def scatter_first(kept, sent):
    got = exchange_near(sent, 1)
    block = kept.shape[1]

    def total(index):
        return kept[index] + got[index * block : (index + 1) * block].astype(F32)

    return total(0), total(1).astype(BF16), got


def scatter_second(kept, sent):
    got = exchange_near(sent, 0)
    total = kept + got[: kept.shape[0]].astype(F32)
    unit, radix = far_stages(lax.axis_size("seq"))[-1]
    total = total.reshape(radix, -1, total.shape[-1])
    return total[0], [total[i].astype(BF16) for i in range(1, radix)], got


def scatter_far(kept, sent):
    stages = far_stages(lax.axis_size("seq"))
    for stage in reversed(range(len(stages))):
        unit, radix = stages[stage]
        for i, piece in enumerate(sent):
            kept = kept + exchange(piece, unit * (i + 1), 0).astype(F32)
        if stage:
            held = kept.reshape(stages[stage - 1][1], -1, kept.shape[-1])
            kept, sent = held[0], [piece.astype(BF16) for piece in held[1:]]
    return kept


def to_rows(sums):
    high = lax.reduce_precision(sums, 8, 7)
    low = sums - high
    spare = jnp.zeros((GAIN_ROWS - 2 * sums.shape[0], sums.shape[1]), F32)
    return jnp.concatenate([high, low, spare]).astype(BF16)


def from_rows(rows, count):
    return rows[:count].astype(F32) + rows[count : 2 * count].astype(F32)


GAIN_ROWS = 16


def scatter_core(held):
    core = lax.axis_index("seq") & 1
    half = held.shape[0] // 2
    kept, got = held[:half], exchange(held[half:], 1, 0)
    first = jnp.where(core == 0, kept, got)
    second = jnp.where(core == 0, got, kept)
    return jnp.concatenate([first, second])


def stream_copies(pieces, columns, target, sems, core):
    block = target.shape[1] // 4
    blocks = [
        piece.at[pl.ds(start, block), columns]
        for piece in pieces
        for start in range(0, piece.shape[0], block)
    ]
    copies = []
    for index, source in enumerate(blocks):
        part, second, first = index // 4, index // 2 % 2, index % 2
        straight = (core ^ part) == 0
        x = jnp.where(straight, first, second)
        y = jnp.where(straight, second, first)
        row = pl.multiple_of((2 * part + y) * block, block)
        copies.append(
            pltpu.make_async_copy(source, target.at[x, pl.ds(row, block)], sems.at[index])
        )
    return copies


def start_all(copies):
    for copy in copies:
        copy.start()


def wait_all(copies):
    for copy in copies:
        copy.wait()


def pair_columns(pair, per_group, width):
    group, inside = divmod(2 * pair, per_group)
    start = group * 3 * width + inside * HD
    return [slice(start + e * width, start + e * width + 2 * HD) for e in range(3)]


def slot_select(offset, groups, positions):
    shape = (groups, positions)
    return (iota(shape, 1) == DILATION_SMALL * iota(shape, 0) + offset).astype(BF16)


def slot_spread(offs, pair, groups, positions, times=1):
    shape = (positions, 2 * groups * times)
    slot = iota(shape, 1) & (2 * groups - 1)
    offset = jnp.where(slot < groups, offs[2 * pair], offs[2 * pair + 1])
    return (iota(shape, 0) == DILATION_SMALL * (slot & (groups - 1)) + offset).astype(BF16)


def side_masks():
    lane = iota((1, 2 * HD), 1)
    return (lane < HD).astype(BF16), (lane >= HD).astype(BF16)


def beside(even, odd):
    nothing = jnp.zeros_like(even)
    return jnp.concatenate(
        [jnp.concatenate([even, nothing], axis=1), jnp.concatenate([nothing, odd], axis=1)], axis=0
    )


def project_kernel(
    core_ref, offs, x_ref, bias_ref, gain_ref, w0, w1, w2, w3, w4, w5, w6, w7,
    first_ref, qkv_ref, slot_ref, out_ref, lse_ref, weights, score_scr, first_scr, qkv_scr,
    sems,
):
    _, positions = bias_ref.shape[:2]
    model = x_ref.shape[1]
    width = weights.shape[2] // 3
    heads = model // HD
    per_group = heads // 2
    groups = positions // DILATION_SMALL
    r = pl.program_id(0)

    @pl.when(r == 0)
    def _():
        pieces = (w0, w1, w2, w3, w4, w5, w6, w7)
        copies = stream_copies(pieces, slice(None), weights, sems, core_ref[0])
        start_all(copies)
        normal, _ = row_norm(x_ref[...].astype(F32))
        first_scr[...] = (normal * gain_ref[...]).astype(BF16)
        wait_all(copies)
        for hh in range(2):
            columns = slice(hh * 3 * width, (hh + 1) * 3 * width)
            qkv_scr[:, columns] = nn(first_scr[...], weights[hh]).astype(BF16)

    low, high = side_masks()
    side = iota((positions, 2 * HD), 1) < HD
    here = pl.ds(pl.multiple_of(r * positions, positions), positions)
    first_ref[...] = first_scr[here]
    qkv_ref[...] = qkv_scr[here]
    bias = bias_ref[0]
    bias = jnp.concatenate([bias, bias], axis=0)
    for pair in range(heads // 2):
        cq, ck, cv = pair_columns(pair, per_group, width)
        query, key = qkv_ref[:, cq], qkv_ref[:, ck]
        both = jnp.concatenate([query * low, query * high], axis=0)
        score_scr[pair] = nt(both, key) * SCALE + bias
        every = jnp.concatenate([query, key, qkv_ref[:, cv]], axis=1)
        for inside in range(2):
            chosen = slot_select(offs[2 * pair + inside], groups, positions)
            slots = nn(chosen, every).astype(BF16)
            starts = [2 * HD * e + HD * inside for e in range(3)]
            slot_ref[2 * pair + inside] = jnp.concatenate(
                [slots[:, start : start + HD] for start in starts], axis=1
            )
    for pair in range(heads // 2):
        value = qkv_ref[:, pair_columns(pair, per_group, width)[2]]
        score = score_scr[pair]
        peak = jnp.max(score, axis=-1, keepdims=True)
        expo = jnp.exp(score - peak)
        total = jnp.sum(expo, axis=-1, keepdims=True)
        expo = expo.astype(BF16)
        out = nn(
            jnp.concatenate([expo[:positions], expo[positions:]], axis=1),
            jnp.concatenate([value * low, value * high], axis=0),
        )
        columns = slice(2 * pair * HD, 2 * (pair + 1) * HD)
        log, scale = peak + jnp.log(total), 1.0 / total
        out_ref[:, columns] = out * jnp.where(side, scale[:positions], scale[positions:])
        lse_ref[:, columns] = jnp.where(side, log[:positions], log[positions:])


def far_masks(parity, row_start, row_count, slots):
    row = row_start + iota((row_count, slots), 0)
    column = iota((row_count, slots), 1)
    live_row = (parity == 0) | ((row & 1) == parity - 1)
    live_column = (parity == 0) | ((column & 1) == parity - 1)
    return (column <= row) & live_column, live_row


def for_blocks(count, body):
    if count == 1:
        body(0)
    else:
        lax.fori_loop(0, count, lambda b, carry: (body(b), carry)[1], 0)


def far_kernel(parity_ref, qkv_ref, out_ref, kv_scr):
    devices, _, groups, _ = qkv_ref.shape
    slots = devices * groups
    block = min(slots, 256)
    per_block = block // groups
    parity = parity_ref[pl.program_id(0)]
    kv_scr[...] = qkv_ref[:, 0].reshape(slots, 3 * HD)[:, HD:]

    def body(index):
        piece = pl.ds(index * per_block, per_block)
        query = qkv_ref[piece, 0].reshape(block, 3 * HD)[:, :HD]
        key, value = kv_scr[:, :HD], kv_scr[:, HD:]
        allowed, live = far_masks(parity, index * block, block, slots)
        score = jnp.where(allowed, nt(query, key) * SCALE, MASKED_SCORE)
        peak = jnp.max(score, axis=-1, keepdims=True)
        expo = jnp.exp(score - peak)
        total = jnp.sum(expo, axis=-1, keepdims=True)
        out = nn(expo.astype(BF16), value) / total
        log = jnp.where(live[:, :1], peak + jnp.log(total), MASKED_SCORE)
        high, middle, low = three_parts(log)
        lane = iota((block, 2 * HD), 1)
        tile = jnp.concatenate([out, out], axis=1)
        tile = jnp.where(lane == HD, high.astype(F32), tile)
        tile = jnp.where(lane == HD + 1, middle.astype(F32), tile)
        tile = jnp.where(lane == HD + 2, low.astype(F32), tile)
        out_ref[piece, 0] = tile.astype(BF16).reshape(per_block, groups, 2 * HD)

    for_blocks(slots // block, body)


def join_kernel(offs, near_ref, log_ref, far_ref, gain_ref, att_ref, heads_ref, lse_ref):
    positions, model = near_ref.shape
    heads = model // HD
    groups = far_ref.shape[1]
    side = iota((positions, 2 * HD), 1) < HD
    place = iota((positions, 2 * HD), 0) & (DILATION_SMALL - 1)

    for pair in range(heads // 2):
        even, odd = far_ref[2 * pair], far_ref[2 * pair + 1]
        far_out = nn(
            slot_spread(offs, pair, groups, positions), beside(even[:, :HD], odd[:, :HD])
        )
        even, odd = even.astype(F32), odd.astype(F32)
        shape = (groups, HD)
        logs = [
            beside(
                jnp.broadcast_to(even[:, HD + i : HD + i + 1], shape),
                jnp.broadcast_to(odd[:, HD + i : HD + i + 1], shape),
            )
            for i in range(3)
        ]
        spread = slot_spread(offs, pair, groups, positions)
        log_far = sum(nn(spread, log.astype(BF16)) for log in logs)
        slot = jnp.where(side, offs[2 * pair], offs[2 * pair + 1])
        log_far = jnp.where(place == slot, log_far, MASKED_SCORE)
        columns = slice(2 * pair * HD, 2 * (pair + 1) * HD)
        log_near = log_ref[:, columns]
        peak = jnp.maximum(log_near, log_far)
        weight_near, weight_far = jnp.exp(log_near - peak), jnp.exp(log_far - peak)
        total = weight_near + weight_far
        lse_ref[:, columns] = pltpu.roll(peak + jnp.log(total), HD, 1)
        att_ref[:, columns] = (
            near_ref[:, columns] * weight_near + far_out * weight_far
        ) / total
    normal, _ = row_norm(att_ref[...])
    heads_ref[...] = (normal * gain_ref[...]).astype(BF16)


def column_block(index, block):
    return pl.ds(pl.multiple_of(index * block, block), block)


def weight_block(weights, index, block):
    per_group = weights.shape[2] // block
    inside = lax.rem(index, per_group)
    return weights[lax.div(index, per_group), :, column_block(inside, block)]


def block_copy(source, target, index, block, sems):
    columns = column_block(index, block)
    return pltpu.make_async_copy(source.at[:, columns], target.at[:, columns], sems.at[index])


HIDDEN_BLOCKS = 6


def forward_kernel(
    core_ref, x_ref, heads_ref, seed_ref, gain_second, gain_hidden, e0, e1, e2, e3,
    hidden_ref, second_ref, resid_ref, inverse_ref, normal_ref, slope_ref,
    merge_w, expand_w, act_scr, normal_scr, slope_scr, sems, out_sems,
):
    tokens, model = x_ref.shape
    hidden_here, width = expand_w.shape[2], merge_w.shape[2]
    hidden_width = 2 * hidden_here
    block = hidden_width // HIDDEN_BLOCKS
    core = core_ref[0]
    expand = (e0, e1, e2, e3)
    merge_copies = stream_copies(expand, pl.ds(hidden_here, width), merge_w, sems.at[0], core)
    expand_copies = stream_copies(expand, pl.ds(0, hidden_here), expand_w, sems.at[1], core)
    start_all(merge_copies)
    start_all(expand_copies)
    wait_all(merge_copies)
    heads_in = heads_ref[...]
    merged = [nt(heads_in[:, hh * width : (hh + 1) * width], merge_w[hh]) for hh in range(2)]
    residual = x_ref[...].astype(F32) + (merged[0] + merged[1])
    resid_ref[...] = residual
    normal_two, _ = row_norm(residual)
    second_in = (normal_two * gain_second[...]).astype(BF16)
    second_ref[...] = second_in
    hidden_ref[:, hidden_width:] = seed_ref[:, model // 2 :]
    wait_all(expand_copies)

    def expand_step(index, totals):
        columns = column_block(index, block)
        act, slope = gelu_parts(nn(second_ref[...], weight_block(expand_w, index, block)))
        act_scr[:, columns] = act
        slope_scr[:, columns] = slope.astype(BF16)
        block_copy(slope_scr, slope_ref, index, block, out_sems.at[0]).start()
        return (
            totals[0] + jnp.sum(act, axis=-1, keepdims=True),
            totals[1] + jnp.sum(act * act, axis=-1, keepdims=True),
        )

    nothing = jnp.zeros((tokens, 1), F32)
    total_one, total_two = lax.fori_loop(0, HIDDEN_BLOCKS, expand_step, (nothing, nothing))
    center = total_one / hidden_width
    inverse = lax.rsqrt(total_two / hidden_width - center * center + NORM_EPSILON)
    inverse_ref[...] = jnp.broadcast_to(inverse, inverse_ref.shape)

    def normal_step(index, carry):
        columns = column_block(index, block)
        normal = (act_scr[:, columns] - center) * inverse
        normal_scr[:, columns] = normal.astype(BF16)
        block_copy(normal_scr, normal_ref, index, block, out_sems.at[1]).start()
        hidden_ref[:, columns] = (normal * gain_hidden[:, columns]).astype(BF16)
        return carry

    lax.fori_loop(0, HIDDEN_BLOCKS, normal_step, 0)
    for index in range(HIDDEN_BLOCKS):
        block_copy(slope_scr, slope_ref, index, block, out_sems.at[0]).wait()
        block_copy(normal_scr, normal_ref, index, block, out_sems.at[1]).wait()


def output_kernel(
    core_ref, hidden_ref, resid_ref, place_ref, r0, r1, r2, r3, block_ref, reduce_w, sems
):
    hidden_here = reduce_w.shape[2]
    copies = stream_copies((r0, r1, r2, r3), slice(None), reduce_w, sems, core_ref[0])
    start_all(copies)
    wait_all(copies)
    block_out = nt(hidden_ref[:, :hidden_here], reduce_w[0]) + nt(
        hidden_ref[:, hidden_here : 2 * hidden_here], reduce_w[1]
    )
    block_out = resid_ref[...] + block_out
    block_ref[...] = nt(block_out.astype(BF16), place_ref[...]).astype(BF16)


def backward_kernel(
    core_ref, offs, att_ref, heads_ref, lse_ref, seed_ref, second_ref, resid_ref, inverse_ref,
    gain_heads, gain_second, gain_hidden, normal_ref, slope_ref,
    e0, e1, e2, e3, r0, r1, r2, r3,
    pre_ref, left_ref, out_ref, grad_ref, stats_ref, slot_ref, grad_heads, grad_second, grad_hidden,
    merge_w, expand_w, reduce_w, normal_scr, slope_scr, grad_scr, sems, in_sems,
):
    tokens, model = att_ref.shape
    hidden_here = r0.shape[1]
    half_model = model // 2
    width = merge_w.shape[2]
    heads = model // HD
    groups = slot_ref.shape[1]
    positions = groups * DILATION_SMALL
    hidden_width = 2 * hidden_here
    block = hidden_width // HIDDEN_BLOCKS
    core = core_ref[0]
    expand = (e0, e1, e2, e3)
    merge_copies = stream_copies(expand, pl.ds(hidden_here, width), merge_w, sems.at[0], core)
    expand_copies = stream_copies(expand, pl.ds(0, hidden_here), expand_w, sems.at[1], core)
    reduce_copies = stream_copies((r0, r1, r2, r3), slice(None), reduce_w, sems.at[2], core)
    start_all(reduce_copies)
    for index in range(HIDDEN_BLOCKS):
        block_copy(normal_ref, normal_scr, index, block, in_sems.at[0]).start()
        block_copy(slope_ref, slope_scr, index, block, in_sems.at[1]).start()
    start_all(expand_copies)
    start_all(merge_copies)
    start = hidden_width + model
    pre_ref[:, hidden_width:start] = heads_ref[...]
    pre_ref[:, start : start + half_model] = second_ref[:, half_model:]
    left_ref[:, :half_model] = second_ref[:, :half_model]
    inverse = inverse_ref[:, :1]
    wait_all(reduce_copies)

    def reduce_step(index, totals):
        columns = column_block(index, block)
        grad = nn(seed_ref[...], weight_block(reduce_w, index, block))
        block_copy(normal_ref, normal_scr, index, block, in_sems.at[0]).wait()
        through = grad * normal_scr[:, columns].astype(F32)
        gain = gain_hidden[:, columns]
        grad_hidden[:, columns] = jnp.sum(through, axis=0, keepdims=True)
        grad_scr[:, columns] = grad * gain
        return (
            totals[0] + jnp.sum(grad * gain, axis=-1, keepdims=True),
            totals[1] + jnp.sum(through * gain, axis=-1, keepdims=True),
        )

    nothing = jnp.zeros((tokens, 1), F32)
    total_one, total_two = lax.fori_loop(0, HIDDEN_BLOCKS, reduce_step, (nothing, nothing))
    mean_one = total_one / hidden_width
    mean_two = total_two / hidden_width

    def pre_step(index, carry):
        columns = column_block(index, block)
        block_copy(slope_ref, slope_scr, index, block, in_sems.at[1]).wait()
        normal = normal_scr[:, columns].astype(F32)
        grad = inverse * (grad_scr[:, columns] - mean_one - normal * mean_two)
        pre_ref[:, columns] = (grad * slope_scr[:, columns].astype(F32)).astype(BF16)
        return carry

    lax.fori_loop(0, HIDDEN_BLOCKS, pre_step, 0)
    wait_all(expand_copies)
    grad_second_in = nt(pre_ref[:, :hidden_here], expand_w[0]) + nt(
        pre_ref[:, hidden_here:hidden_width], expand_w[1]
    )
    normal_two, inverse_two = row_norm(resid_ref[...])
    grad_second[...] = jnp.sum(grad_second_in * normal_two, axis=0, keepdims=True)
    resid = seed_ref[...].astype(F32) + row_norm_back(
        grad_second_in, normal_two, inverse_two, gain_second[...]
    )
    out_ref[...] = resid
    resid_low = resid.astype(BF16)
    left_ref[:, half_model:] = resid_low[:, :half_model]
    pre_ref[:, start + half_model :] = resid_low[:, half_model:]
    wait_all(merge_copies)
    grad_heads_in = jnp.concatenate([nn(resid_low, merge_w[hh]) for hh in range(2)], axis=1)
    normal_heads, inverse_heads = row_norm(att_ref[...])
    grad_heads[...] = jnp.sum(grad_heads_in * normal_heads, axis=0, keepdims=True)
    grad_att = row_norm_back(
        grad_heads_in, normal_heads, inverse_heads, gain_heads[...]
    ).astype(BF16)
    grad_ref[...] = grad_att
    grad_scr[:, :model] = grad_att.astype(F32) * att_ref[...]
    across = (iota((2 * HD, 2 * HD), 0) // HD != iota((2 * HD, 2 * HD), 1) // HD).astype(BF16)
    lane = iota((positions, 2 * HD), 1)
    side, inside_lane = lane < HD, lane & (HD - 1)

    def for_row(r, carry):
        here = pl.ds(pl.multiple_of(r * positions, positions), positions)
        for pair in range(heads // 2):
            columns = slice(2 * pair * HD, 2 * (pair + 1) * HD)
            top, middle, _ = three_parts(grad_scr[here, columns])
            dots = nn(top, across) + nn(middle, across)
            stats = jnp.zeros((positions, 2 * HD), F32)
            for index, part in enumerate(three_parts(lse_ref[here, columns]) + three_parts(dots)):
                stats = jnp.where(inside_lane == index, part.astype(F32), stats)
            stats_ref[here, columns] = stats.astype(BF16)
            grad = grad_ref[here, columns].astype(F32)
            tile = jnp.where(side, grad, stats).astype(BF16)
            chosen = slot_select(offs[2 * pair], groups, positions)
            slot_ref[r * heads + 2 * pair] = nn(chosen, tile).astype(BF16)
            tile = jnp.where(side, stats, grad).astype(BF16)
            chosen = slot_select(offs[2 * pair + 1], groups, positions)
            tile = nn(chosen, tile)
            slot_ref[r * heads + 2 * pair + 1] = jnp.concatenate(
                [tile[:, HD:], tile[:, :HD]], axis=1
            ).astype(BF16)
        return carry

    lax.fori_loop(0, tokens // positions, for_row, 0)


def far_back_kernel(parity_ref, qkv_ref, grad_ref, out_ref, kv_scr, total_scr):
    devices, _, groups, _ = qkv_ref.shape
    slots = devices * groups
    block = min(slots, 256)
    per_block = block // groups
    parity = parity_ref[pl.program_id(0)]
    kv_scr[...] = qkv_ref[:, 0].reshape(slots, 3 * HD)[:, HD:]
    total_scr[...] = jnp.zeros_like(total_scr)

    def body(index):
        piece = pl.ds(index * per_block, per_block)
        query = qkv_ref[piece, 0].reshape(block, 3 * HD)[:, :HD]
        tile = grad_ref[piece, 0].reshape(block, 2 * HD)
        key, value = kv_scr[:, :HD], kv_scr[:, HD:]
        grad = tile[:, :HD]
        stats = tile[:, HD:].astype(F32)
        log = stats[:, 0:1] + stats[:, 1:2] + stats[:, 2:3]
        dots = stats[:, 3:4] + stats[:, 4:5] + stats[:, 5:6]
        allowed, live = far_masks(parity, index * block, block, slots)
        score = jnp.where(allowed & live, nt(query, key) * SCALE - log, MASKED_SCORE)
        weight = jnp.exp(score)
        grad_score = (weight * (nt(grad, value) - dots)).astype(BF16)
        grad_query = nn(grad_score, key) * SCALE
        total_scr[:, :HD] += tn(grad_score, query) * SCALE
        total_scr[:, HD:] += tn(weight.astype(BF16), grad)
        out_ref[piece, 0, :, :HD] = grad_query.astype(BF16).reshape(per_block, groups, HD)

    for_blocks(slots // block, body)
    out_ref[:, 0, :, HD:] = total_scr[...].astype(BF16).reshape(devices, groups, 2 * HD)


def near_back_kernel(bias_ref, qkv_ref, grad_ref, stats_ref, out_ref, weight_scr, score_scr):
    positions, model = grad_ref.shape
    heads = model // HD
    per_group = heads // 2
    width = per_group * HD
    low, high = side_masks()
    inside = iota((1, 2 * HD), 1) & (HD - 1)
    less_log = jnp.where(inside < 3, -1.0 / SCALE, 0.0).astype(BF16)
    less_dots = jnp.where((inside >= 3) & (inside < 6), -1.0, 0.0).astype(BF16)

    bias = bias_ref[0]
    for pair in range(heads // 2):
        cq, ck, cv = pair_columns(pair, per_group, width)
        own = slice(2 * pair * HD, 2 * (pair + 1) * HD)
        query, key, value = qkv_ref[:, cq], qkv_ref[:, ck], qkv_ref[:, cv]
        grad, stats = grad_ref[:, own], stats_ref[:, own]
        for side, (mine, other) in enumerate(((low, high), (high, low))):
            more = stats * other
            score = nt(query * mine + more, key * mine + less_log * other)
            weight = jnp.exp(score * SCALE + bias)
            through = nt(grad * mine + more, value * mine + less_dots * other)
            weight_scr[2 * pair + side] = weight.astype(BF16)
            score_scr[2 * pair + side] = (weight * through).astype(BF16)
    for pair in range(heads // 2):
        cq, ck, cv = pair_columns(pair, per_group, width)
        own = slice(2 * pair * HD, 2 * (pair + 1) * HD)
        query, key, grad = qkv_ref[:, cq], qkv_ref[:, ck], grad_ref[:, own]
        even, odd = score_scr[2 * pair], score_scr[2 * pair + 1]
        out_ref[:, cq] = (SCALE * nn(
            jnp.concatenate([even, odd], axis=1),
            jnp.concatenate([key * low, key * high], axis=0),
        )).astype(BF16)
        out_ref[:, ck] = (SCALE * tn(
            jnp.concatenate([even, odd], axis=0),
            jnp.concatenate([query * low, query * high], axis=0),
        )).astype(BF16)
        out_ref[:, cv] = (tn(
            jnp.concatenate([weight_scr[2 * pair], weight_scr[2 * pair + 1]], axis=0),
            jnp.concatenate([grad * low, grad * high], axis=0),
        )).astype(BF16)


def join_back_kernel(offs, near_ref, far_ref, first_ref, out_ref):
    positions, model = first_ref.shape
    heads = model // HD
    per_group = heads // 2
    width = per_group * HD
    groups = far_ref.shape[1]
    out_ref[:, 3 * model :] = first_ref[:, model // 2 :]

    for pair in range(heads // 2):
        even, odd = far_ref[2 * pair], far_ref[2 * pair + 1]
        spread = slot_spread(offs, pair, groups, positions)
        for e, columns in enumerate(pair_columns(pair, per_group, width)):
            part = slice(e * HD, (e + 1) * HD)
            far = nn(spread, beside(even[:, part], odd[:, part]))
            out_ref[:, columns] = (near_ref[:, columns].astype(F32) + far).astype(BF16)


def weight_grad_kernel(
    change, core_ref, left, right_0, right_1, left_got, right_0_got, right_1_got,
    *refs,
):
    kept_ref, sent_ref, left_scr = refs[-3:]
    block = kept_ref.shape[1]
    if len(refs) > 3:
        sent_ref[2 * block :] = refs[0][...]
    step = pl.program_id(0)

    @pl.when((step == 0) | (step == change))
    def _():
        left_scr[0] = left[...].T
        left_scr[1] = left_got[...].T

    product = [
        nn(left_scr[0], right[...]) + nn(left_scr[1], got[...])
        for right, got in ((right_0, right_0_got), (right_1, right_1_got))
    ]
    kept_ref[0] = product[0][:block]
    sent_ref[block : 2 * block] = product[1][block:].astype(BF16)
    low, high = product[0][block:], product[1][:block]

    @pl.when(core_ref[0] == 0)
    def _():
        kept_ref[1] = high
        sent_ref[:block] = low.astype(BF16)

    @pl.when(core_ref[0] != 0)
    def _():
        kept_ref[1] = low
        sent_ref[:block] = high.astype(BF16)


def input_grad_kernel(
    core_ref, x_ref, pack_ref, resid_ref, gain_ref, second_ref, place_ref, w0, w1, w2, w3, w4, w5, w6, w7,
    grad_ref, gain_grad, weights, sems,
):
    span = weights.shape[2]
    copies = stream_copies((w0, w1, w2, w3, w4, w5, w6, w7), slice(None), weights, sems, core_ref[0])
    start_all(copies)
    normal, inverse = row_norm(x_ref[...].astype(F32))
    wait_all(copies)
    grad_first = nt(pack_ref[:, :span], weights[0]) + nt(pack_ref[:, span : 2 * span], weights[1])
    first = jnp.sum(grad_first * normal, axis=0, keepdims=True)
    parts = three_parts(jnp.concatenate([first, second_ref[...]] + [jnp.zeros_like(first)] * 6))
    gain_grad[...] = sum(nt(part, place_ref[...]) for part in parts)
    grad = resid_ref[...] + row_norm_back(grad_first, normal, inverse, gain_ref[...])
    grad_ref[...] = nt(grad.astype(BF16), place_ref[...]).astype(BF16)


def whole(*shape):
    return pl.BlockSpec(shape, lambda *_: tuple(0 for _ in shape))


def sds(shape, dtype):
    return jax.ShapeDtypeStruct(shape, dtype)


def call(
    kernel, grid, in_specs, out_specs, out_shape, scratch=(), earlier=(), cost=5
):
    def body(*refs):
        kernel(*refs[len(earlier) :])

    return partial(
        pl.pallas_call(
            body,
            grid=grid,
            in_specs=[ANY] * len(earlier) + in_specs,
            out_specs=out_specs,
            out_shape=out_shape,
            scratch_shapes=list(scratch),
            compiler_params=pltpu.CompilerParams(
                dimension_semantics=("arbitrary",) * len(grid), vmem_limit_bytes=VMEM_LIMIT
            ),
            cost_estimate=pl.CostEstimate(
                flops=cost * 1_150_000_000, bytes_accessed=0, transcendentals=0
            ),
        ),
        *earlier,
    )


def per_device(
    inputs,
    attend_weight,
    merge_weight,
    expand_weight,
    reduce_weight,
    gain_first,
    gain_heads,
    gain_second,
    gain_hidden,
    cotangent,
    lengths,
    local_span,
    dilation,
):
    seq_size, head_size = lax.axis_size("seq"), lax.axis_size("head")
    row_count, positions, model = inputs.shape
    rows = row_count // head_size
    tokens = rows * positions
    shard_rows, width = attend_weight.shape[1:]
    heads = width * head_size // HD
    group_heads = heads // head_size
    hidden_here = expand_weight.shape[1]
    hidden_width = hidden_here * head_size
    quarter = model // 4
    groups = positions // DILATION_SMALL
    pairs = rows * heads
    owned = -(-pairs // seq_size)
    padded = owned * seq_size
    seq_index, head_index = lax.axis_index("seq"), lax.axis_index("head")
    core = seq_index & 1
    core_ref = core.reshape(1)

    attend_shard = gather_core(jnp.concatenate(list(attend_weight), axis=1))
    attend_far = gather_far(attend_shard)
    attend_got = exchange_near(attend_far, 0)
    attend_more = exchange_near(attend_far, 1)
    attend_last = exchange_near(attend_got, 1)
    attend_all = (attend_far, attend_got, attend_more, attend_last)
    attend_all = attend_all + tuple(exchange(piece, 1, 0) for piece in attend_all)
    other_shard = jnp.concatenate([expand_weight, merge_weight.T, reduce_weight.T], axis=1)
    other_shard = gate(gather_core(after(other_shard, attend_shard)), attend_far)
    both_gains = jnp.concatenate([gain_heads, gain_hidden])
    partner_gains = exchange(both_gains.reshape(-1, 128), 0, 1).reshape(-1)
    gain_heads_all = jnp.concatenate([gain_heads, partner_gains[:width]])[None]
    gain_hidden_all = jnp.concatenate([gain_hidden, partner_gains[width:]])[None]

    half_rows = shard_rows // 2
    part, near, far, beside, inside = jnp.meshgrid(
        *[jnp.arange(n) for n in (2, 2, seq_size // 4, 2, half_rows)], indexing="ij"
    )
    shard_of = seq_index ^ (4 * far + 2 * near + (beside ^ part))
    feature_of = (shard_of * shard_rows + (core ^ part) * half_rows + inside).reshape(-1)
    place = (jnp.arange(model)[:, None] == feature_of[None, :]).astype(BF16)

    def to_own_order(gain):
        return jnp.dot(
            gain[None], place.astype(F32), precision=lax.Precision.HIGHEST
        )

    gain_one, gain_two = to_own_order(gain_first), to_own_order(gain_second)
    row_start = head_index * rows

    def own_rows(tensor):
        return lax.dynamic_slice_in_dim(tensor, row_start, rows, axis=0)

    def in_own_order(tensor):
        return nn(tensor.reshape(tokens, model), place).astype(BF16)

    x_own = in_own_order(own_rows(inputs))
    places = jnp.arange(positions)
    in_length = (seq_index * positions + places)[None, :] < own_rows(lengths)[:, None]
    seed = in_own_order(
        jnp.where(in_length[..., None], own_rows(cotangent), jnp.zeros((), BF16))
    )
    span_block = places[None, :] // own_rows(local_span)[:, None]
    within = (span_block[:, :, None] == span_block[:, None, :]) & (
        places[None, :] <= places[:, None]
    )
    bias = jnp.where(within, 0.0, MASKED_SCORE).astype(F32)

    local_head = jnp.arange(heads)
    head_ids = (head_index ^ (local_head // group_heads)) * group_heads + local_head % group_heads
    offsets = (head_ids % DILATION_SMALL).astype(jnp.int32)
    pair_ids = jnp.minimum(seq_index * owned + jnp.arange(owned), pairs - 1)
    pair_rate = own_rows(dilation)[pair_ids // heads]
    pair_head = head_ids[pair_ids % heads]
    parity = jnp.where(
        pair_rate == DILATION_SMALL, 0, 1 + (pair_head % pair_rate) // DILATION_SMALL
    ).astype(jnp.int32)

    model_spec, model_shape = whole(tokens, model), (tokens, model)
    attend_scratch = pltpu.VMEM((2, model, 3 * width), BF16)

    def by_row(size):
        return pl.BlockSpec((positions, size), lambda r: (r, 0))

    def of_row(size):
        return pl.BlockSpec((heads, groups, size), lambda r: (r, 0, 0))

    model_row, qkv_row = by_row(model), by_row(3 * model)
    bias_row = pl.BlockSpec((1, positions, positions), lambda r: (r, 0, 0))
    first_in, qkv, slots, near_out, log_near = call(
        project_kernel,
        (rows,),
        [SMEM, SMEM, model_spec, bias_row, whole(1, model)] + [ANY] * 8,
        [model_row, qkv_row, of_row(3 * HD), model_row, model_row],
        [
            sds(model_shape, BF16),
            sds((tokens, 3 * model), BF16),
            sds((padded, groups, 3 * HD), BF16),
            sds(model_shape, F32),
            sds(model_shape, F32),
        ],
        [
            attend_scratch,
            pltpu.VMEM((heads // 2, 2 * positions, positions), F32),
            pltpu.VMEM((tokens, model), BF16),
            pltpu.VMEM((tokens, 3 * model), BF16),
            pltpu.SemaphoreType.DMA((8,)),
        ],
        cost=1,
    )(core_ref, offsets, x_own, bias, gain_one, *attend_all)
    other_far = gather_far(other_shard, (first_in,))
    other_got = exchange_near(other_far, 0)

    def to_owners(value):
        value = value.reshape(seq_size, owned, groups, value.shape[-1])
        return lax.all_to_all(value, "seq", 0, 0, tiled=True)

    def from_owners(value):
        value = lax.all_to_all(value, "seq", 0, 0, tiled=True)
        return value.reshape(padded, groups, value.shape[-1])

    def by_pair(size):
        return pl.BlockSpec((seq_size, 1, groups, size), lambda i: (0, i, 0, 0))

    def owned_shape(size):
        return sds((seq_size, owned, groups, size), BF16)

    slot_count = seq_size * groups
    kv_scratch = pltpu.VMEM((slot_count, 2 * HD), BF16)
    far_qkv = to_owners(slots)
    far_out = call(
        far_kernel,
        (owned,),
        [SMEM, by_pair(3 * HD)],
        by_pair(2 * HD),
        owned_shape(2 * HD),
        [kv_scratch],
        cost=4,
    )(parity, far_qkv)
    far_here = from_owners(far_out)
    expand_held, reduce_held = join(
        [other_far, other_got], (far_out,), (hidden_here + width, hidden_here)
    )
    expand_more = exchange_near(expand_held, 1)
    reduce_more = exchange_near(reduce_held, 1)

    attended, heads_in, log_all = call(
        join_kernel,
        (rows,),
        [SMEM, model_row, model_row, of_row(2 * HD), whole(1, model)],
        [model_row, model_row, model_row],
        [sds(model_shape, F32), sds(model_shape, BF16), sds(model_shape, F32)],
        cost=5,
    )(offsets, near_out, log_near, far_here, gain_heads_all)
    expand_more = gate(expand_more, heads_in)
    expand_all = (
        expand_held, expand_more, exchange(expand_held, 1, 0), exchange(expand_more, 1, 0)
    )
    hidden_scratch = pltpu.VMEM((tokens, hidden_width), F32)
    hidden_low = pltpu.VMEM((tokens, hidden_width), BF16)
    hidden_pack = (tokens, hidden_width + model // 2)
    pre_pack = (tokens, hidden_width + 2 * model)
    merge_scratch = pltpu.VMEM((2, model, width), BF16)
    weight_scratch = pltpu.VMEM((2, model, hidden_here), BF16)
    hidden_in, second_in, residual, inverse_hidden, normal_hidden, slope = call(
        forward_kernel,
        (),
        [SMEM] + [model_spec] * 3 + [whole(1, model), whole(1, hidden_width)] + [ANY] * 4,
        [whole(*hidden_pack), model_spec, model_spec, whole(tokens, 128), ANY, ANY],
        [
            sds(hidden_pack, BF16), sds(model_shape, BF16), sds(model_shape, F32),
            sds((tokens, 128), F32), sds((tokens, hidden_width), BF16),
            sds((tokens, hidden_width), BF16),
        ],
        [
            merge_scratch, weight_scratch, hidden_scratch, hidden_low, hidden_low,
            pltpu.SemaphoreType.DMA((2, 8)), pltpu.SemaphoreType.DMA((2, HIDDEN_BLOCKS)),
        ],
        cost=16,
    )(core_ref, x_own, heads_in, seed, gain_two, gain_hidden_all, *expand_all)
    reduce_more = gate(reduce_more, hidden_in)
    reduce_all = (
        reduce_held, reduce_more, exchange(reduce_held, 1, 0), exchange(reduce_more, 1, 0)
    )
    block_mine = call(
        output_kernel,
        (),
        [SMEM, whole(*hidden_pack), model_spec, whole(model, model)] + [ANY] * 4,
        model_spec,
        sds(model_shape, BF16),
        [weight_scratch, pltpu.SemaphoreType.DMA((8,))],
        cost=40,
    )(core_ref, hidden_in, residual, place, *reduce_all)

    def weight_grad(
        size, left, left_at, right, right_at, left_got_at, earlier=(), change=0, extra=None
    ):
        got = exchange(right, 1, 0)

        def spec(at):
            return pl.BlockSpec((tokens, width), lambda j: (0, at(j)))

        def rights():
            return [spec(lambda j, x=x: right_at(x, j)) for x in range(2)]

        sent_rows = 2 * quarter
        extras = []
        if extra is not None:
            sent_rows += GAIN_ROWS
            extras = [extra]
        return call(
            partial(weight_grad_kernel, change),
            (size // width,),
            [SMEM, spec(left_at)] + rights() + [spec(left_got_at)] + rights()
            + [pl.BlockSpec((GAIN_ROWS, width), lambda j: (0, j))] * len(extras),
            [
                pl.BlockSpec((2, quarter, width), lambda j: (0, 0, j)),
                pl.BlockSpec((sent_rows, width), lambda j: (0, j)),
            ],
            [sds((2, quarter, size), F32), sds((sent_rows, size), BF16)],
            [pltpu.VMEM((2, model // 2, tokens), BF16)],
            earlier=earlier,
            cost=7,
        )(core_ref, left, right, right, got, got, got, *extras)

    per_half = hidden_here // width
    hidden_blocks = hidden_width // width

    def both_rows(mine, earlier=None):
        mine = mine.reshape(rows, positions, model)
        other = exchange(mine, 0, 1)
        if earlier is not None:
            other = after(other, earlier)
        first = jnp.where(head_index == 0, mine, other)
        second = jnp.where(head_index == 0, other, mine)
        return jnp.concatenate([first, second])

    reduce_kept, reduce_sent = weight_grad(
        hidden_here, seed, lambda j: 0, hidden_in, lambda x, j: x * per_half + j,
        lambda j: hidden_blocks, earlier=(block_mine,),
    )
    (
        grad_pre, lefts, grad_resid, grad_att, stats, grad_slots, grad_heads, grad_second,
        grad_hidden,
    ) = call(
        backward_kernel,
        (),
        [SMEM, SMEM] + [model_spec] * 6
        + [whole(tokens, 128), whole(1, model), whole(1, model), whole(1, hidden_width)]
        + [ANY] * 10,
        [
            whole(*pre_pack), model_spec, model_spec, model_spec, model_spec,
            whole(padded, groups, 2 * HD), whole(1, model), whole(1, model),
            whole(1, hidden_width),
        ],
        [
            sds(pre_pack, BF16), sds(model_shape, BF16), sds(model_shape, F32),
            sds(model_shape, BF16), sds(model_shape, BF16),
            sds((padded, groups, 2 * HD), BF16), sds((1, model), F32), sds((1, model), F32),
            sds((1, hidden_width), F32),
        ],
        [
            merge_scratch, weight_scratch, weight_scratch, hidden_low, hidden_low, hidden_scratch,
            pltpu.SemaphoreType.DMA((3, 8)), pltpu.SemaphoreType.DMA((2, HIDDEN_BLOCKS)),
        ],
        earlier=(reduce_sent,),
        cost=22,
    )(
        core_ref, offsets, attended, heads_in, log_all, seed, second_in, residual,
        inverse_hidden, gain_heads_all, gain_two, gain_hidden_all, normal_hidden, slope,
        *expand_all, *reduce_all,
    )
    far_grads = to_owners(grad_slots)
    reduce_kept, reduce_sent, _ = scatter_first(reduce_kept, reduce_sent)
    near_grad = call(
        near_back_kernel,
        (rows,),
        [bias_row, qkv_row, model_row, model_row],
        qkv_row,
        sds((tokens, 3 * model), BF16),
        [pltpu.VMEM((heads, positions, positions), BF16)] * 2,
        earlier=(reduce_sent,),
        cost=60,
    )(bias, qkv, grad_att, stats)
    block_out = both_rows(block_mine, near_grad)
    expand_kept, expand_sent = weight_grad(
        hidden_here + width, lefts, lambda j: jnp.where(j < per_half, 0, 1), grad_pre,
        lambda x, j: jnp.where(j < per_half, x * per_half + j, hidden_blocks + x),
        lambda j: hidden_blocks + 2 + jnp.where(j < per_half, 0, 1),
        earlier=(near_grad,), change=per_half,
    )
    far_back = call(
        far_back_kernel,
        (owned,),
        [SMEM, by_pair(3 * HD), by_pair(2 * HD)],
        by_pair(3 * HD),
        owned_shape(3 * HD),
        [kv_scratch, pltpu.VMEM((slot_count, 2 * HD), F32)],
        earlier=(expand_sent,),
        cost=1,
    )(parity, far_qkv, far_grads)
    back_here = from_owners(far_back)
    expand_kept, expand_sent, _ = scatter_first(expand_kept, expand_sent)
    reduce_kept, reduce_sent, _ = scatter_second(reduce_kept, reduce_sent)
    grad_pack_shape = (tokens, 3 * model + model // 2)
    grad_pack = call(
        join_back_kernel,
        (rows,),
        [SMEM, qkv_row, of_row(3 * HD), model_row],
        by_row(grad_pack_shape[1]),
        sds(grad_pack_shape, BF16),
        earlier=(*reduce_sent, block_out, expand_sent),
        cost=1,
    )(offsets, near_grad, back_here, first_in)
    grad_mine, grad_shared = call(
        input_grad_kernel,
        (),
        [
            SMEM, model_spec, whole(*grad_pack_shape), model_spec, whole(1, model),
            whole(1, model), whole(model, model),
        ]
        + [ANY] * 8,
        [model_spec, whole(8, model)],
        [sds(model_shape, BF16), sds((8, model), F32)],
        [attend_scratch, pltpu.SemaphoreType.DMA((8,))],
        cost=40,
    )(core_ref, x_own, grad_pack, grad_resid, gain_one, grad_second, place, *attend_all)

    def by_head(grad):
        size = grad.shape[1] // 2
        return jnp.where(head_index == 0, grad[0], jnp.roll(grad[0], size))

    gains = jnp.concatenate(
        [
            grad_shared[0], grad_shared[1], by_head(grad_heads), by_head(grad_hidden),
        ]
    )
    gain_rows = -(-gains.shape[0] // (3 * width))
    gains = jnp.pad(gains, (0, gain_rows * 3 * width - gains.shape[0])).reshape(gain_rows, -1)
    gain_sent = to_rows(gains)
    attend_kept, attend_sent = weight_grad(
        3 * width, first_in, lambda j: 0, grad_pack, lambda x, j: 3 * x + j, lambda j: 6,
        earlier=(grad_mine,), extra=gain_sent,
    )
    attend_kept, attend_sent, attend_near = scatter_first(attend_kept, attend_sent)
    gains = from_rows(gain_sent, gain_rows) + from_rows(attend_near[2 * quarter :], gain_rows)
    gain_sent = to_rows(gains)
    expand_kept, expand_sent, _ = scatter_second(expand_kept, expand_sent)
    attend_kept, attend_sent, attend_got = scatter_second(
        attend_kept, jnp.concatenate([attend_sent, gain_sent])
    )
    gains = from_rows(gain_sent, gain_rows) + from_rows(attend_got[quarter:], gain_rows)
    stages = far_stages(seq_size)
    for stage in reversed(range(len(stages))):
        unit, radix = stages[stage]
        gain_sent = to_rows(gains)
        everyone = [from_rows(gain_sent, gain_rows)]
        rows_sent = attend_sent[0].shape[0]
        for i, piece in enumerate(attend_sent):
            got = exchange(jnp.concatenate([piece, gain_sent]), unit * (i + 1), 0)
            attend_kept = attend_kept + got[:rows_sent].astype(F32)
            everyone.append(from_rows(got[rows_sent:], gain_rows))
        while len(everyone) > 1:
            everyone = [one + two for one, two in zip(everyone[::2], everyone[1::2])]
        gains = everyone[0]
        if stage:
            held = attend_kept.reshape(stages[stage - 1][1], -1, 3 * width)
            attend_kept, attend_sent = held[0], [piece.astype(BF16) for piece in held[1:]]
    attend_last = jnp.concatenate([attend_kept[half_rows:], gains])
    attend_last = exchange(attend_last, 1, 0)
    gains = (gains + attend_last[half_rows:]).reshape(-1)
    attend_last = attend_last[:half_rows]
    attend_kept = attend_kept[:half_rows]
    grad_attend = jnp.concatenate(
        [
            jnp.where(core == 0, attend_kept, attend_last),
            jnp.where(core == 0, attend_last, attend_kept),
        ]
    )
    grad_reduce = scatter_core(scatter_far(after(reduce_kept, attend_near), reduce_sent))
    grad_expand = scatter_core(scatter_far(after(expand_kept, attend_near), expand_sent))
    grad_inputs = both_rows(grad_mine, attend_near)

    def own_half(start, size):
        return lax.dynamic_slice_in_dim(gains, start + head_index * size, size)

    return (
        block_out,
        grad_inputs,
        jnp.stack([grad_attend[:, e * width : (e + 1) * width] for e in range(3)]),
        grad_expand[:, hidden_here:].T,
        grad_expand[:, :hidden_here],
        grad_reduce.T,
        gains[:model],
        own_half(2 * model, width),
        gains[model : 2 * model],
        own_half(3 * model, hidden_here),
    )


def solution(mesh):
    placed = (
        P(None, "seq", None),
        P(None, "seq", "head"),
        P("head", "seq"),
        P("seq", "head"),
        P("head", "seq"),
        P(),
        P("head"),
        P(),
        P("head"),
        P(None, "seq", None),
        P(),
        P(),
        P(),
    )
    return jax.shard_map(
        per_device,
        mesh=mesh,
        in_specs=placed,
        out_specs=(
            P(None, "seq", None),
            P(None, "seq", None),
            P(None, "seq", "head"),
            P("head", "seq"),
            P("seq", "head"),
            P("head", "seq"),
            P(),
            P("head"),
            P(),
            P("head"),
        ),
        check_vma=False,
    )
```

```python
from functools import partial

import jax
import jax.numpy as jnp
from jax import lax
from jax.experimental import pallas as pl
from jax.experimental.pallas import tpu as pltpu
from jax.sharding import PartitionSpec as P

HD = 64
DILATION_SMALL = 8
NORM_EPSILON = 1e-05
MASKED_SCORE = -1e30
SCALE = HD ** (-0.5)
F32 = jnp.float32
BF16 = jnp.bfloat16
ANY = pl.BlockSpec(memory_space=pl.ANY)
SMEM = pl.BlockSpec(memory_space=pltpu.SMEM)
VMEM_LIMIT = 56 * 1024 * 1024


def nn(left, right):
    return lax.dot_general(left, right, (((1,), (0,)), ((), ())), preferred_element_type=F32)


def nt(left, right):
    return lax.dot_general(left, right, (((1,), (1,)), ((), ())), preferred_element_type=F32)


def tn(left, right):
    return lax.dot_general(left, right, (((0,), (0,)), ((), ())), preferred_element_type=F32)


def row_norm(values):
    center = jnp.mean(values, axis=-1, keepdims=True)
    spread = jnp.mean(values * values, axis=-1, keepdims=True) - center * center
    inverse = lax.rsqrt(spread + NORM_EPSILON)
    return (values - center) * inverse, inverse


def row_norm_back(incoming, normal, inverse, gain_row):
    scaled = incoming * gain_row
    first_mean = jnp.mean(scaled, axis=-1, keepdims=True)
    second_mean = jnp.mean(scaled * normal, axis=-1, keepdims=True)
    return inverse * (scaled - first_mean - normal * second_mean)


def three_parts(values):
    high = values.astype(BF16)
    rest = values - high.astype(F32)
    middle = rest.astype(BF16)
    low = (rest - middle.astype(F32)).astype(BF16)
    return high, middle, low


def gelu_parts(values):
    expo = jnp.exp(values * values * -0.5)
    term = 1.0 / (1.0 + (0.3275911 * 0.7071067811865476) * jnp.abs(values))
    poly = term * (
        0.254829592
        + term
        * (-0.284496736 + term * (1.421413741 + term * (-1.453152027 + term * 1.061405429)))
    )
    tail = 0.5 * poly * expo
    phi = jnp.where(values >= 0.0, 1.0 - tail, tail)
    return values * phi, phi + values * expo * 0.3989422804014327


def iota(shape, dim):
    return lax.broadcasted_iota(jnp.int32, shape, dim)


def permute(value, target):
    seq_size, head_size = lax.axis_size("seq"), lax.axis_size("head")
    pairs = []
    for s in range(seq_size):
        for h in range(head_size):
            to_seq, to_head = target(s, h)
            pairs.append((s * head_size + h, to_seq * head_size + to_head))
    return lax.ppermute(value, ("seq", "head"), pairs)


def exchange(value, seq_mask, head_mask):
    return permute(value, lambda s, h: (s ^ seq_mask, h ^ head_mask))


def exchange_near(value, turn):
    return permute(value, lambda s, h: (s, h ^ 1) if (s & 1) == turn else (s ^ 2, h))


def far_stages(seq_size):
    unit, left, stages = 4, seq_size // 4, []
    while left > 1:
        radix = 4 if left % 4 == 0 else 2
        stages.append((unit, radix))
        unit, left = unit * radix, left // radix
    return stages


def join(pieces, earlier=(), splits=None):
    rows = pieces[0][0].shape[0]
    widths = [piece.shape[1] for piece in pieces[0]]
    count = len(pieces)
    splits = splits or (sum(widths),)
    starts = [sum(splits[:i]) for i in range(len(splits))]
    if rows % 16:
        whole_array = jnp.concatenate([jnp.concatenate(line, axis=1) for line in pieces])
        out = [whole_array[:, start : start + size] for start, size in zip(starts, splits)]
        return out if len(splits) > 1 else out[0]
    flat = [piece for line in pieces for piece in line]

    def kernel(*refs):
        refs = refs[len(earlier) :]
        sources, targets, sems = refs[: len(flat)], refs[len(flat) : -1], refs[-1]
        copies = []
        for i in range(count):
            for j, width in enumerate(widths):
                left = sum(widths[:j])
                for target, start, size in zip(targets, starts, splits):
                    low, high = max(left, start), min(left + width, start + size)
                    if low < high:
                        copies.append(
                            pltpu.make_async_copy(
                                sources[i * len(widths) + j].at[:, pl.ds(low - left, high - low)],
                                target.at[pl.ds(i * rows, rows), pl.ds(low - start, high - low)],
                                sems.at[len(copies)],
                            )
                        )
        start_all(copies)
        wait_all(copies)

    out = pl.pallas_call(
        kernel,
        in_specs=[ANY] * len(earlier) + [pl.BlockSpec(memory_space=pltpu.VMEM)] * len(flat),
        out_specs=[ANY] * len(splits),
        out_shape=[
            jax.ShapeDtypeStruct((count * rows, size), flat[0].dtype) for size in splits
        ],
        scratch_shapes=[pltpu.SemaphoreType.DMA((len(flat) * len(splits),))],
        cost_estimate=pl.CostEstimate(flops=2_000_000_000, bytes_accessed=0, transcendentals=0),
    )(*earlier, *flat)
    return out if len(splits) > 1 else out[0]


def gate(value, *earlier):
    def kernel(*refs):
        pass

    return pl.pallas_call(
        kernel,
        in_specs=[ANY] * (len(earlier) + 1),
        out_specs=ANY,
        out_shape=jax.ShapeDtypeStruct(value.shape, value.dtype),
        input_output_aliases={len(earlier): 0},
        cost_estimate=pl.CostEstimate(flops=0, bytes_accessed=0, transcendentals=0),
    )(*earlier, value)


def after(value, earlier):
    zero = earlier[(0,) * earlier.ndim].astype(F32) * 0.0
    return value + zero.astype(value.dtype)


def gather_core(shard):
    core = lax.axis_index("seq") & 1
    half = shard.shape[0] // 2
    kept = lax.dynamic_slice_in_dim(shard, core * half, half)
    sent = lax.dynamic_slice_in_dim(shard, (1 - core) * half, half)
    return jnp.concatenate([kept, exchange(sent, 1, 0)])


def gather_far(held):
    stages = far_stages(lax.axis_size("seq"))
    for unit, radix in stages:
        pieces = [held] + [exchange(held, unit * i, 0) for i in range(1, radix)]
        held = jnp.concatenate(pieces) if (unit, radix) != stages[-1] else None
    return pieces


def scatter_first(kept, sent):
    got = exchange_near(sent, 1)
    block = kept.shape[1]

    def total(index):
        return kept[index] + got[index * block : (index + 1) * block].astype(F32)

    return total(0), total(1).astype(BF16), got


def scatter_second(kept, sent):
    got = exchange_near(sent, 0)
    total = kept + got[: kept.shape[0]].astype(F32)
    unit, radix = far_stages(lax.axis_size("seq"))[-1]
    total = total.reshape(radix, -1, total.shape[-1])
    return total[0], [total[i].astype(BF16) for i in range(1, radix)], got


def scatter_far(kept, sent):
    stages = far_stages(lax.axis_size("seq"))
    for stage in reversed(range(len(stages))):
        unit, radix = stages[stage]
        for i, piece in enumerate(sent):
            kept = kept + exchange(piece, unit * (i + 1), 0).astype(F32)
        if stage:
            held = kept.reshape(stages[stage - 1][1], -1, kept.shape[-1])
            kept, sent = held[0], [piece.astype(BF16) for piece in held[1:]]
    return kept


def to_rows(sums):
    high = lax.reduce_precision(sums, 8, 7)
    low = sums - high
    spare = jnp.zeros((GAIN_ROWS - 2 * sums.shape[0], sums.shape[1]), F32)
    return jnp.concatenate([high, low, spare]).astype(BF16)


def from_rows(rows, count):
    return rows[:count].astype(F32) + rows[count : 2 * count].astype(F32)


GAIN_ROWS = 16


def scatter_core(held):
    core = lax.axis_index("seq") & 1
    half = held.shape[0] // 2
    kept, got = held[:half], exchange(held[half:], 1, 0)
    first = jnp.where(core == 0, kept, got)
    second = jnp.where(core == 0, got, kept)
    return jnp.concatenate([first, second])


def stream_copies(pieces, columns, target, sems, core):
    block = target.shape[1] // 4
    blocks = [
        piece.at[pl.ds(start, block), columns]
        for piece in pieces
        for start in range(0, piece.shape[0], block)
    ]
    copies = []
    for index, source in enumerate(blocks):
        part, second, first = index // 4, index // 2 % 2, index % 2
        straight = (core ^ part) == 0
        x = jnp.where(straight, first, second)
        y = jnp.where(straight, second, first)
        row = pl.multiple_of((2 * part + y) * block, block)
        copies.append(
            pltpu.make_async_copy(source, target.at[x, pl.ds(row, block)], sems.at[index])
        )
    return copies


def start_all(copies):
    for copy in copies:
        copy.start()


def wait_all(copies):
    for copy in copies:
        copy.wait()


def pair_columns(pair, per_group, width):
    group, inside = divmod(2 * pair, per_group)
    start = group * 3 * width + inside * HD
    return [slice(start + e * width, start + e * width + 2 * HD) for e in range(3)]


def slot_select(offset, groups, positions):
    shape = (groups, positions)
    return (iota(shape, 1) == DILATION_SMALL * iota(shape, 0) + offset).astype(BF16)


def slot_spread(offs, pair, groups, positions, times=1):
    shape = (positions, 2 * groups * times)
    slot = iota(shape, 1) & (2 * groups - 1)
    offset = jnp.where(slot < groups, offs[2 * pair], offs[2 * pair + 1])
    return (iota(shape, 0) == DILATION_SMALL * (slot & (groups - 1)) + offset).astype(BF16)


def side_masks():
    lane = iota((1, 2 * HD), 1)
    return (lane < HD).astype(BF16), (lane >= HD).astype(BF16)


def beside(even, odd):
    nothing = jnp.zeros_like(even)
    return jnp.concatenate(
        [jnp.concatenate([even, nothing], axis=1), jnp.concatenate([nothing, odd], axis=1)], axis=0
    )


def project_kernel(
    core_ref, offs, x_ref, bias_ref, gain_ref, w0, w1, w2, w3, w4, w5, w6, w7,
    first_ref, qkv_ref, slot_ref, out_ref, lse_ref, weights, score_scr, first_scr, qkv_scr,
    sems,
):
    _, positions = bias_ref.shape[:2]
    model = x_ref.shape[1]
    width = weights.shape[2] // 3
    heads = model // HD
    per_group = heads // 2
    groups = positions // DILATION_SMALL
    r = pl.program_id(0)

    @pl.when(r == 0)
    def _():
        pieces = (w0, w1, w2, w3, w4, w5, w6, w7)
        copies = stream_copies(pieces, slice(None), weights, sems, core_ref[0])
        start_all(copies)
        normal, _ = row_norm(x_ref[...].astype(F32))
        first_scr[...] = (normal * gain_ref[...]).astype(BF16)
        wait_all(copies)
        for hh in range(2):
            columns = slice(hh * 3 * width, (hh + 1) * 3 * width)
            qkv_scr[:, columns] = nn(first_scr[...], weights[hh]).astype(BF16)

    low, high = side_masks()
    side = iota((positions, 2 * HD), 1) < HD
    here = pl.ds(pl.multiple_of(r * positions, positions), positions)
    first_ref[...] = first_scr[here]
    qkv_ref[...] = qkv_scr[here]
    bias = bias_ref[0]
    bias = jnp.concatenate([bias, bias], axis=0)
    for pair in range(heads // 2):
        cq, ck, cv = pair_columns(pair, per_group, width)
        query, key = qkv_ref[:, cq], qkv_ref[:, ck]
        both = jnp.concatenate([query * low, query * high], axis=0)
        score_scr[pair] = nt(both, key) * SCALE + bias
        every = jnp.concatenate([query, key, qkv_ref[:, cv]], axis=1)
        for inside in range(2):
            chosen = slot_select(offs[2 * pair + inside], groups, positions)
            slots = nn(chosen, every).astype(BF16)
            starts = [2 * HD * e + HD * inside for e in range(3)]
            slot_ref[2 * pair + inside] = jnp.concatenate(
                [slots[:, start : start + HD] for start in starts], axis=1
            )
    for pair in range(heads // 2):
        value = qkv_ref[:, pair_columns(pair, per_group, width)[2]]
        score = score_scr[pair]
        peak = jnp.max(score, axis=-1, keepdims=True)
        expo = jnp.exp(score - peak)
        total = jnp.sum(expo, axis=-1, keepdims=True)
        expo = expo.astype(BF16)
        out = nn(
            jnp.concatenate([expo[:positions], expo[positions:]], axis=1),
            jnp.concatenate([value * low, value * high], axis=0),
        )
        columns = slice(2 * pair * HD, 2 * (pair + 1) * HD)
        log, scale = peak + jnp.log(total), 1.0 / total
        out_ref[:, columns] = out * jnp.where(side, scale[:positions], scale[positions:])
        lse_ref[:, columns] = jnp.where(side, log[:positions], log[positions:])


def far_masks(parity, row_start, row_count, slots):
    row = row_start + iota((row_count, slots), 0)
    column = iota((row_count, slots), 1)
    live_row = (parity == 0) | ((row & 1) == parity - 1)
    live_column = (parity == 0) | ((column & 1) == parity - 1)
    return (column <= row) & live_column, live_row


def for_blocks(count, body):
    if count == 1:
        body(0)
    else:
        lax.fori_loop(0, count, lambda b, carry: (body(b), carry)[1], 0)


def far_kernel(parity_ref, qkv_ref, out_ref, kv_scr):
    devices, _, groups, _ = qkv_ref.shape
    slots = devices * groups
    block = min(slots, 256)
    per_block = block // groups
    parity = parity_ref[pl.program_id(0)]
    kv_scr[...] = qkv_ref[:, 0].reshape(slots, 3 * HD)[:, HD:]

    def body(index):
        piece = pl.ds(index * per_block, per_block)
        query = qkv_ref[piece, 0].reshape(block, 3 * HD)[:, :HD]
        key, value = kv_scr[:, :HD], kv_scr[:, HD:]
        allowed, live = far_masks(parity, index * block, block, slots)
        score = jnp.where(allowed, nt(query, key) * SCALE, MASKED_SCORE)
        peak = jnp.max(score, axis=-1, keepdims=True)
        expo = jnp.exp(score - peak)
        total = jnp.sum(expo, axis=-1, keepdims=True)
        out = nn(expo.astype(BF16), value) / total
        log = jnp.where(live[:, :1], peak + jnp.log(total), MASKED_SCORE)
        high, middle, low = three_parts(log)
        lane = iota((block, 2 * HD), 1)
        tile = jnp.concatenate([out, out], axis=1)
        tile = jnp.where(lane == HD, high.astype(F32), tile)
        tile = jnp.where(lane == HD + 1, middle.astype(F32), tile)
        tile = jnp.where(lane == HD + 2, low.astype(F32), tile)
        out_ref[piece, 0] = tile.astype(BF16).reshape(per_block, groups, 2 * HD)

    for_blocks(slots // block, body)


def join_kernel(offs, near_ref, log_ref, far_ref, gain_ref, att_ref, heads_ref, lse_ref):
    positions, model = near_ref.shape
    heads = model // HD
    groups = far_ref.shape[1]
    side = iota((positions, 2 * HD), 1) < HD
    place = iota((positions, 2 * HD), 0) & (DILATION_SMALL - 1)

    for pair in range(heads // 2):
        even, odd = far_ref[2 * pair], far_ref[2 * pair + 1]
        far_out = nn(
            slot_spread(offs, pair, groups, positions), beside(even[:, :HD], odd[:, :HD])
        )
        even, odd = even.astype(F32), odd.astype(F32)
        shape = (groups, HD)
        logs = [
            beside(
                jnp.broadcast_to(even[:, HD + i : HD + i + 1], shape),
                jnp.broadcast_to(odd[:, HD + i : HD + i + 1], shape),
            )
            for i in range(3)
        ]
        spread = slot_spread(offs, pair, groups, positions)
        log_far = sum(nn(spread, log.astype(BF16)) for log in logs)
        slot = jnp.where(side, offs[2 * pair], offs[2 * pair + 1])
        log_far = jnp.where(place == slot, log_far, MASKED_SCORE)
        columns = slice(2 * pair * HD, 2 * (pair + 1) * HD)
        log_near = log_ref[:, columns]
        peak = jnp.maximum(log_near, log_far)
        weight_near, weight_far = jnp.exp(log_near - peak), jnp.exp(log_far - peak)
        total = weight_near + weight_far
        lse_ref[:, columns] = pltpu.roll(peak + jnp.log(total), HD, 1)
        att_ref[:, columns] = (
            near_ref[:, columns] * weight_near + far_out * weight_far
        ) / total
    normal, _ = row_norm(att_ref[...])
    heads_ref[...] = (normal * gain_ref[...]).astype(BF16)


HIDDEN_BLOCKS = 4


def hidden_kernel(
    core_ref, offs, gain_heads, gain_second, gain_hidden, x_any, heads_any, att_any, lse_any,
    seed_any, place_any, a0, a1, a2, a3, b0, b1, b2, b3, c0, c1, c2, c3,
    block_ref, hidden_out, pre_out, left_ref, resid_ref, grad_ref, stats_ref, slot_ref,
    grad_heads, grad_second, grad_hidden,
    x_ref, heads_ref, att_ref, lse_ref, seed_ref, place_ref, merge_w, expand_w, reduce_w,
    act_scr, slope_scr, grad_scr, hidden_ref, pre_ref, tile_scr, sems, in_sems, out_sems,
):
    tokens, model = x_ref.shape
    hidden_here = expand_w.shape[2]
    half_model = model // 2
    width = merge_w.shape[2]
    heads = model // HD
    groups = slot_ref.shape[1]
    positions = groups * DILATION_SMALL
    hidden_width = 2 * hidden_here
    block = hidden_width // HIDDEN_BLOCKS
    core = core_ref[0]
    chunks = ((a0, a1, a2, a3), (b0, b1, b2, b3), (c0, c1, c2, c3))
    third = a0.shape[1]

    def chunk_copies(target, first_column, size, at):
        copies = []
        for chunk, pieces in enumerate(chunks):
            low = max(first_column, chunk * third)
            high = min(first_column + size, (chunk + 1) * third)
            if low < high:
                copies += stream_copies(
                    pieces,
                    pl.ds(low - chunk * third, high - low),
                    target.at[:, :, pl.ds(low - first_column, high - low)],
                    sems.at[at + len(copies) // 8],
                    core,
                )
        return copies

    expand_copies = chunk_copies(expand_w, 0, hidden_here, 0)
    merge_copies = chunk_copies(merge_w, hidden_here, width, 2)
    reduce_copies = chunk_copies(reduce_w, hidden_here + width, hidden_here, 3)
    inputs = [
        pltpu.make_async_copy(source, target, in_sems.at[i])
        for i, (source, target) in enumerate(
            (
                (heads_any, heads_ref), (x_any, x_ref), (seed_any, seed_ref),
                (place_any, place_ref), (att_any, att_ref), (lse_any, lse_ref),
            )
        )
    ]
    start_all(inputs[:2])
    start_all(merge_copies)
    start_all(expand_copies)
    start_all(inputs[2:3])
    start_all(reduce_copies)
    start_all(inputs[3:])

    def columns_of(index):
        return slice(index * block, (index + 1) * block)

    def weight_block(weights, index):
        per_group = hidden_here // block
        inside = index % per_group
        return weights[index // per_group, :, inside * block : (inside + 1) * block]

    def send(source, target, index, start, size):
        columns = slice(start, start + size)
        copy = pltpu.make_async_copy(
            source.at[:, columns], target.at[:, columns], out_sems.at[index]
        )
        copy.start()
        return copy

    wait_all(inputs[:2])
    wait_all(merge_copies)
    heads_in = heads_ref[...]
    merged = [nt(heads_in[:, hh * width : (hh + 1) * width], merge_w[hh]) for hh in range(2)]
    residual = x_ref[...].astype(F32) + (merged[0] + merged[1])
    resid_ref[...] = residual
    normal_two, inverse_two = row_norm(residual)
    second_in = (normal_two * gain_second[...]).astype(BF16)
    start = hidden_width + model
    pre_ref[:, hidden_width:start] = heads_in
    pre_ref[:, start : start + half_model] = second_in[:, half_model:]
    left_ref[:, :half_model] = second_in[:, :half_model]
    wait_all(expand_copies)
    total_one = jnp.zeros((tokens, 1), F32)
    total_two = jnp.zeros((tokens, 1), F32)
    for index in range(HIDDEN_BLOCKS):
        columns = columns_of(index)
        act, slope = gelu_parts(nn(second_in, weight_block(expand_w, index)))
        act_scr[:, columns] = act
        slope_scr[:, columns] = slope
        total_one += jnp.sum(act, axis=-1, keepdims=True)
        total_two += jnp.sum(act * act, axis=-1, keepdims=True)
    center = total_one / hidden_width
    inverse = lax.rsqrt(total_two / hidden_width - center * center + NORM_EPSILON)
    wait_all(inputs[2:3])
    hidden_ref[:, hidden_width:] = seed_ref[:, half_model:]
    wait_all(reduce_copies)
    total_one = jnp.zeros((tokens, 1), F32)
    total_two = jnp.zeros((tokens, 1), F32)
    sends = []
    for index in range(HIDDEN_BLOCKS):
        columns = columns_of(index)
        normal = (act_scr[:, columns] - center) * inverse
        act_scr[:, columns] = normal
        gain = gain_hidden[:, columns]
        scaled = normal * gain
        hidden_ref[:, columns] = scaled.astype(BF16)
        sends.append(send(hidden_ref, hidden_out, index, index * block, block))
        grad = nn(seed_ref[...], weight_block(reduce_w, index))
        grad_hidden[:, columns] = jnp.sum(grad * normal, axis=0, keepdims=True)
        grad_scr[:, columns] = grad * gain
        total_one += jnp.sum(grad * gain, axis=-1, keepdims=True)
        total_two += jnp.sum(grad * scaled, axis=-1, keepdims=True)
    sends.append(send(hidden_ref, hidden_out, HIDDEN_BLOCKS, hidden_width, half_model))
    mean_one = total_one / hidden_width
    mean_two = total_two / hidden_width
    grad_second_in = jnp.zeros((tokens, model), F32)
    for index in range(HIDDEN_BLOCKS):
        columns = columns_of(index)
        grad = inverse * (grad_scr[:, columns] - mean_one - act_scr[:, columns] * mean_two)
        grad_pre = (grad * slope_scr[:, columns]).astype(BF16)
        pre_ref[:, columns] = grad_pre
        sends.append(send(pre_ref, pre_out, HIDDEN_BLOCKS + 1 + index, index * block, block))
        grad_second_in += nt(grad_pre, weight_block(expand_w, index))
    normal_two, inverse_two = row_norm(resid_ref[...])
    grad_second[...] = jnp.sum(grad_second_in * normal_two, axis=0, keepdims=True)
    resid = seed_ref[...].astype(F32) + row_norm_back(
        grad_second_in, normal_two, inverse_two, gain_second[...]
    )
    block_out = nt(hidden_ref[:, :hidden_here], reduce_w[0]) + nt(
        hidden_ref[:, hidden_here:hidden_width], reduce_w[1]
    )
    block_out = (resid_ref[...] + block_out).astype(BF16)
    resid_ref[...] = resid
    resid_low = resid.astype(BF16)
    left_ref[:, half_model:] = resid_low[:, :half_model]
    pre_ref[:, start + half_model :] = resid_low[:, half_model:]
    sends.append(send(pre_ref, pre_out, 2 * HIDDEN_BLOCKS + 1, hidden_width, 2 * model))
    grad_heads_in = jnp.concatenate([nn(resid_low, merge_w[hh]) for hh in range(2)], axis=1)
    wait_all(inputs[3:])
    block_ref[...] = nt(block_out, place_ref[...]).astype(BF16)
    normal_heads, inverse_heads = row_norm(att_ref[...])
    grad_heads[...] = jnp.sum(grad_heads_in * normal_heads, axis=0, keepdims=True)
    grad_att = row_norm_back(
        grad_heads_in, normal_heads, inverse_heads, gain_heads[...]
    ).astype(BF16)
    grad_ref[...] = grad_att
    grad_scr[:, :model] = grad_att.astype(F32) * att_ref[...]
    across = (iota((2 * HD, 2 * HD), 0) // HD != iota((2 * HD, 2 * HD), 1) // HD).astype(BF16)
    lane = iota((positions, 2 * HD), 1)
    side, inside_lane = lane < HD, lane & (HD - 1)

    def for_row(r, carry):
        here = pl.ds(pl.multiple_of(r * positions, positions), positions)
        for pair in range(heads // 2):
            columns = slice(2 * pair * HD, 2 * (pair + 1) * HD)
            top, middle, _ = three_parts(grad_scr[here, columns])
            dots = nn(top, across) + nn(middle, across)
            stats = jnp.zeros((positions, 2 * HD), F32)
            for index, part in enumerate(three_parts(lse_ref[here, columns]) + three_parts(dots)):
                stats = jnp.where(inside_lane == index, part.astype(F32), stats)
            stats_ref[here, columns] = stats.astype(BF16)
            grad = grad_ref[here, columns].astype(F32)
            tile_scr[2 * pair] = jnp.where(side, grad, stats)
            tile_scr[2 * pair + 1] = jnp.where(side, stats, grad)
        for head in range(heads):
            tile = tile_scr[head, pl.ds(offs[head], groups, stride=DILATION_SMALL), :]
            if head % 2:
                tile = jnp.concatenate([tile[:, HD:], tile[:, :HD]], axis=1)
            slot_ref[r * heads + head] = tile.astype(BF16)
        return carry

    lax.fori_loop(0, tokens // positions, for_row, 0)
    wait_all(sends)


def far_back_kernel(parity_ref, qkv_ref, grad_ref, out_ref, kv_scr, total_scr):
    devices, _, groups, _ = qkv_ref.shape
    slots = devices * groups
    block = min(slots, 256)
    per_block = block // groups
    parity = parity_ref[pl.program_id(0)]
    kv_scr[...] = qkv_ref[:, 0].reshape(slots, 3 * HD)[:, HD:]
    total_scr[...] = jnp.zeros_like(total_scr)

    def body(index):
        piece = pl.ds(index * per_block, per_block)
        query = qkv_ref[piece, 0].reshape(block, 3 * HD)[:, :HD]
        tile = grad_ref[piece, 0].reshape(block, 2 * HD)
        key, value = kv_scr[:, :HD], kv_scr[:, HD:]
        grad = tile[:, :HD]
        stats = tile[:, HD:].astype(F32)
        log = stats[:, 0:1] + stats[:, 1:2] + stats[:, 2:3]
        dots = stats[:, 3:4] + stats[:, 4:5] + stats[:, 5:6]
        allowed, live = far_masks(parity, index * block, block, slots)
        score = jnp.where(allowed & live, nt(query, key) * SCALE - log, MASKED_SCORE)
        weight = jnp.exp(score)
        grad_score = (weight * (nt(grad, value) - dots)).astype(BF16)
        grad_query = nn(grad_score, key) * SCALE
        total_scr[:, :HD] += tn(grad_score, query) * SCALE
        total_scr[:, HD:] += tn(weight.astype(BF16), grad)
        out_ref[piece, 0, :, :HD] = grad_query.astype(BF16).reshape(per_block, groups, HD)

    for_blocks(slots // block, body)
    out_ref[:, 0, :, HD:] = total_scr[...].astype(BF16).reshape(devices, groups, 2 * HD)


def near_back_kernel(bias_ref, qkv_ref, grad_ref, stats_ref, out_ref, weight_scr, score_scr):
    positions, model = grad_ref.shape
    heads = model // HD
    per_group = heads // 2
    width = per_group * HD
    low, high = side_masks()
    inside = iota((1, 2 * HD), 1) & (HD - 1)
    less_log = jnp.where(inside < 3, -1.0 / SCALE, 0.0).astype(BF16)
    less_dots = jnp.where((inside >= 3) & (inside < 6), -1.0, 0.0).astype(BF16)

    bias = bias_ref[0]
    for pair in range(heads // 2):
        cq, ck, cv = pair_columns(pair, per_group, width)
        own = slice(2 * pair * HD, 2 * (pair + 1) * HD)
        query, key, value = qkv_ref[:, cq], qkv_ref[:, ck], qkv_ref[:, cv]
        grad, stats = grad_ref[:, own], stats_ref[:, own]
        for side, (mine, other) in enumerate(((low, high), (high, low))):
            more = stats * other
            score = nt(query * mine + more, key * mine + less_log * other)
            weight = jnp.exp(score * SCALE + bias)
            through = nt(grad * mine + more, value * mine + less_dots * other)
            weight_scr[2 * pair + side] = weight.astype(BF16)
            score_scr[2 * pair + side] = (weight * through).astype(BF16)
    for pair in range(heads // 2):
        cq, ck, cv = pair_columns(pair, per_group, width)
        own = slice(2 * pair * HD, 2 * (pair + 1) * HD)
        query, key, grad = qkv_ref[:, cq], qkv_ref[:, ck], grad_ref[:, own]
        even, odd = score_scr[2 * pair], score_scr[2 * pair + 1]
        out_ref[:, cq] = (SCALE * nn(
            jnp.concatenate([even, odd], axis=1),
            jnp.concatenate([key * low, key * high], axis=0),
        )).astype(BF16)
        out_ref[:, ck] = (SCALE * tn(
            jnp.concatenate([even, odd], axis=0),
            jnp.concatenate([query * low, query * high], axis=0),
        )).astype(BF16)
        out_ref[:, cv] = (tn(
            jnp.concatenate([weight_scr[2 * pair], weight_scr[2 * pair + 1]], axis=0),
            jnp.concatenate([grad * low, grad * high], axis=0),
        )).astype(BF16)


def join_back_kernel(offs, near_ref, far_ref, first_ref, out_ref):
    positions, model = first_ref.shape
    heads = model // HD
    per_group = heads // 2
    width = per_group * HD
    groups = far_ref.shape[1]
    out_ref[:, 3 * model :] = first_ref[:, model // 2 :]

    for pair in range(heads // 2):
        even, odd = far_ref[2 * pair], far_ref[2 * pair + 1]
        spread = slot_spread(offs, pair, groups, positions)
        for e, columns in enumerate(pair_columns(pair, per_group, width)):
            part = slice(e * HD, (e + 1) * HD)
            far = nn(spread, beside(even[:, part], odd[:, part]))
            out_ref[:, columns] = (near_ref[:, columns].astype(F32) + far).astype(BF16)


def weight_grad_kernel(
    change, core_ref, left, right_0, right_1, left_got, right_0_got, right_1_got,
    *refs,
):
    kept_ref, sent_ref, left_scr = refs[-3:]
    block = kept_ref.shape[1]
    if len(refs) > 3:
        sent_ref[2 * block :] = refs[0][...]
    step = pl.program_id(0)

    @pl.when((step == 0) | (step == change))
    def _():
        left_scr[0] = left[...].T
        left_scr[1] = left_got[...].T

    product = [
        nn(left_scr[0], right[...]) + nn(left_scr[1], got[...])
        for right, got in ((right_0, right_0_got), (right_1, right_1_got))
    ]
    kept_ref[0] = product[0][:block]
    sent_ref[block : 2 * block] = product[1][block:].astype(BF16)
    low, high = product[0][block:], product[1][:block]

    @pl.when(core_ref[0] == 0)
    def _():
        kept_ref[1] = high
        sent_ref[:block] = low.astype(BF16)

    @pl.when(core_ref[0] != 0)
    def _():
        kept_ref[1] = low
        sent_ref[:block] = high.astype(BF16)


def input_grad_kernel(
    core_ref, x_ref, pack_ref, resid_ref, gain_ref, second_ref, place_ref, w0, w1, w2, w3, w4, w5, w6, w7,
    grad_ref, gain_grad, weights, sems,
):
    span = weights.shape[2]
    copies = stream_copies((w0, w1, w2, w3, w4, w5, w6, w7), slice(None), weights, sems, core_ref[0])
    start_all(copies)
    normal, inverse = row_norm(x_ref[...].astype(F32))
    wait_all(copies)
    grad_first = nt(pack_ref[:, :span], weights[0]) + nt(pack_ref[:, span : 2 * span], weights[1])
    first = jnp.sum(grad_first * normal, axis=0, keepdims=True)
    parts = three_parts(jnp.concatenate([first, second_ref[...]] + [jnp.zeros_like(first)] * 6))
    gain_grad[...] = sum(nt(part, place_ref[...]) for part in parts)
    grad = resid_ref[...] + row_norm_back(grad_first, normal, inverse, gain_ref[...])
    grad_ref[...] = nt(grad.astype(BF16), place_ref[...]).astype(BF16)


def whole(*shape):
    return pl.BlockSpec(shape, lambda *_: tuple(0 for _ in shape))


def sds(shape, dtype):
    return jax.ShapeDtypeStruct(shape, dtype)


def call(
    kernel, grid, in_specs, out_specs, out_shape, scratch=(), earlier=(), cost=5
):
    def body(*refs):
        kernel(*refs[len(earlier) :])

    return partial(
        pl.pallas_call(
            body,
            grid=grid,
            in_specs=[ANY] * len(earlier) + in_specs,
            out_specs=out_specs,
            out_shape=out_shape,
            scratch_shapes=list(scratch),
            compiler_params=pltpu.CompilerParams(
                dimension_semantics=("arbitrary",) * len(grid), vmem_limit_bytes=VMEM_LIMIT
            ),
            cost_estimate=pl.CostEstimate(
                flops=cost * 1_150_000_000, bytes_accessed=0, transcendentals=0
            ),
        ),
        *earlier,
    )


def per_device(
    inputs,
    attend_weight,
    merge_weight,
    expand_weight,
    reduce_weight,
    gain_first,
    gain_heads,
    gain_second,
    gain_hidden,
    cotangent,
    lengths,
    local_span,
    dilation,
):
    seq_size, head_size = lax.axis_size("seq"), lax.axis_size("head")
    row_count, positions, model = inputs.shape
    rows = row_count // head_size
    tokens = rows * positions
    shard_rows, width = attend_weight.shape[1:]
    heads = width * head_size // HD
    group_heads = heads // head_size
    hidden_here = expand_weight.shape[1]
    hidden_width = hidden_here * head_size
    quarter = model // 4
    groups = positions // DILATION_SMALL
    pairs = rows * heads
    owned = -(-pairs // seq_size)
    padded = owned * seq_size
    seq_index, head_index = lax.axis_index("seq"), lax.axis_index("head")
    core = seq_index & 1
    core_ref = core.reshape(1)

    attend_shard = gather_core(jnp.concatenate(list(attend_weight), axis=1))
    attend_far = jnp.concatenate(gather_far(attend_shard))
    other_shard = jnp.concatenate([expand_weight, merge_weight.T, reduce_weight.T], axis=1)
    other_shard = gather_core(after(other_shard, attend_shard))
    third = other_shard.shape[1] // 3
    other_shards = [
        gate(other_shard[:, i * third : (i + 1) * third], attend_far) for i in range(3)
    ]
    attend_got = exchange_near(attend_far, 0)
    attend_more = exchange_near(attend_far, 1)
    other_pieces = [gather_far(other_shards[0])]
    attend_got = gate(attend_got, *other_pieces[0][1:])
    attend_last = exchange_near(attend_got, 1)
    other_pieces.append(gather_far(gate(other_shards[1], attend_got)))
    other_far = [jnp.concatenate(pieces) for pieces in other_pieces]
    other_got = [exchange_near(other_far[0], 0)]
    attend_last = gate(attend_last, *other_pieces[1][1:], other_got[0])
    attend_all = (attend_far, attend_got, attend_more, attend_last)
    attend_all = attend_all + tuple(exchange(piece, 1, 0) for piece in attend_all)
    both_gains = jnp.concatenate([gain_heads, gain_hidden])
    partner_gains = exchange(both_gains.reshape(-1, 128), 0, 1).reshape(-1)
    gain_heads_all = jnp.concatenate([gain_heads, partner_gains[:width]])[None]
    gain_hidden_all = jnp.concatenate([gain_hidden, partner_gains[width:]])[None]

    half_rows = shard_rows // 2
    part, near, far, beside, inside = jnp.meshgrid(
        *[jnp.arange(n) for n in (2, 2, seq_size // 4, 2, half_rows)], indexing="ij"
    )
    shard_of = seq_index ^ (4 * far + 2 * near + (beside ^ part))
    feature_of = (shard_of * shard_rows + (core ^ part) * half_rows + inside).reshape(-1)
    feature_of = gate(feature_of, attend_far)
    place = (jnp.arange(model)[:, None] == feature_of[None, :]).astype(BF16)

    def to_own_order(gain):
        return jnp.dot(
            gain[None], place.astype(F32), precision=lax.Precision.HIGHEST
        )

    gain_one, gain_two = to_own_order(gain_first), to_own_order(gain_second)
    row_start = head_index * rows
    lengths, local_span, dilation = gate(
        jnp.stack([lengths, local_span, dilation]), attend_far
    )

    def own_rows(tensor):
        return lax.dynamic_slice_in_dim(tensor, row_start, rows, axis=0)

    def in_own_order(tensor):
        return nn(tensor.reshape(tokens, model), place).astype(BF16)

    x_own = in_own_order(own_rows(inputs))
    places = jnp.arange(positions)
    in_length = (seq_index * positions + places)[None, :] < own_rows(lengths)[:, None]
    seed = in_own_order(
        jnp.where(in_length[..., None], own_rows(cotangent), jnp.zeros((), BF16))
    )
    span_block = places[None, :] // own_rows(local_span)[:, None]
    within = (span_block[:, :, None] == span_block[:, None, :]) & (
        places[None, :] <= places[:, None]
    )
    bias = jnp.where(within, 0.0, MASKED_SCORE).astype(F32)

    local_head = jnp.arange(heads)
    head_ids = (head_index ^ (local_head // group_heads)) * group_heads + local_head % group_heads
    offsets = gate((head_ids % DILATION_SMALL).astype(jnp.int32), attend_far)
    pair_ids = jnp.minimum(seq_index * owned + jnp.arange(owned), pairs - 1)
    pair_rate = own_rows(dilation)[pair_ids // heads]
    pair_head = head_ids[pair_ids % heads]
    parity = jnp.where(
        pair_rate == DILATION_SMALL, 0, 1 + (pair_head % pair_rate) // DILATION_SMALL
    ).astype(jnp.int32)

    model_spec, model_shape = whole(tokens, model), (tokens, model)
    attend_scratch = pltpu.VMEM((2, model, 3 * width), BF16)

    def by_row(size):
        return pl.BlockSpec((positions, size), lambda r: (r, 0))

    def of_row(size):
        return pl.BlockSpec((heads, groups, size), lambda r: (r, 0, 0))

    model_row, qkv_row = by_row(model), by_row(3 * model)
    bias_row = pl.BlockSpec((1, positions, positions), lambda r: (r, 0, 0))
    first_in, qkv, slots, near_out, log_near = call(
        project_kernel,
        (rows,),
        [SMEM, SMEM, model_spec, bias_row, whole(1, model)] + [ANY] * 8,
        [model_row, qkv_row, of_row(3 * HD), model_row, model_row],
        [
            sds(model_shape, BF16),
            sds((tokens, 3 * model), BF16),
            sds((padded, groups, 3 * HD), BF16),
            sds(model_shape, F32),
            sds(model_shape, F32),
        ],
        [
            attend_scratch,
            pltpu.VMEM((heads // 2, 2 * positions, positions), F32),
            pltpu.VMEM((tokens, model), BF16),
            pltpu.VMEM((tokens, 3 * model), BF16),
            pltpu.SemaphoreType.DMA((8,)),
        ],
        cost=1,
    )(core_ref, offsets, x_own, bias, gain_one, *attend_all)
    other_held = [gate(jnp.concatenate([other_far[0], other_got[0]]), first_in)]
    other_more = [exchange_near(other_held[0], 1)]
    other_got.append(exchange_near(gate(other_far[1], first_in), 0))
    other_pieces.append(gather_far(gate(other_shards[2], first_in)))
    other_far.append(gate(jnp.concatenate(other_pieces[2]), other_more[0]))
    other_got.append(exchange_near(other_far[2], 0))
    other_held.append(jnp.concatenate([other_far[1], other_got[1]]))
    other_more.append(exchange_near(other_held[1], 1))
    other_core = [(exchange(other_held[0], 1, 0), exchange(other_more[0], 1, 0))]

    def to_owners(value):
        value = value.reshape(seq_size, owned, groups, value.shape[-1])
        return lax.all_to_all(value, "seq", 0, 0, tiled=True)

    def from_owners(value):
        value = lax.all_to_all(value, "seq", 0, 0, tiled=True)
        return value.reshape(padded, groups, value.shape[-1])

    def by_pair(size):
        return pl.BlockSpec((seq_size, 1, groups, size), lambda i: (0, i, 0, 0))

    def owned_shape(size):
        return sds((seq_size, owned, groups, size), BF16)

    slot_count = seq_size * groups
    kv_scratch = pltpu.VMEM((slot_count, 2 * HD), BF16)
    far_qkv = to_owners(slots)
    far_out = call(
        far_kernel,
        (owned,),
        [SMEM, by_pair(3 * HD)],
        by_pair(2 * HD),
        owned_shape(2 * HD),
        [kv_scratch],
        cost=4,
        earlier=(seed, place, gain_two),
    )(parity, far_qkv)
    far_here = from_owners(far_out)
    other_held.append(
        gate(jnp.concatenate([other_far[2], other_got[2]]), far_out, other_more[1])
    )
    other_more.append(exchange_near(other_held[2], 1))
    other_core.append((exchange(other_held[1], 1, 0), exchange(other_more[1], 1, 0)))
    held_core = exchange(other_held[2], 1, 0)

    attended, heads_in, log_all = call(
        join_kernel,
        (rows,),
        [SMEM, model_row, model_row, of_row(2 * HD), whole(1, model)],
        [model_row, model_row, model_row],
        [sds(model_shape, F32), sds(model_shape, BF16), sds(model_shape, F32)],
        cost=5,
        earlier=other_core[0],
    )(offsets, near_out, log_near, far_here, gain_heads_all)
    other_more[2] = gate(other_more[2], heads_in)
    other_core.append((held_core, exchange(other_more[2], 1, 0)))
    weights_all = [
        piece for i in range(3) for piece in (other_held[i], other_more[i], *other_core[i])
    ]
    hidden_pack = (tokens, hidden_width + model // 2)
    pre_pack = (tokens, hidden_width + 2 * model)
    low_scratch = pltpu.VMEM(model_shape, BF16)
    full_scratch = pltpu.VMEM(model_shape, F32)
    hidden_scratch = pltpu.VMEM((tokens, hidden_width), F32)
    weight_scratch = pltpu.VMEM((2, model, hidden_here), BF16)
    (
        block_mine, hidden_in, grad_pre, lefts, grad_resid, grad_att, stats, grad_slots,
        grad_heads, grad_second, grad_hidden,
    ) = call(
        hidden_kernel,
        (),
        [SMEM, SMEM, whole(1, model), whole(1, model), whole(1, hidden_width)] + [ANY] * 18,
        [
            model_spec, ANY, ANY, model_spec, model_spec, model_spec, model_spec,
            whole(padded, groups, 2 * HD), whole(1, model), whole(1, model),
            whole(1, hidden_width),
        ],
        [
            sds(model_shape, BF16), sds(hidden_pack, BF16), sds(pre_pack, BF16),
            sds(model_shape, BF16), sds(model_shape, F32), sds(model_shape, BF16),
            sds(model_shape, BF16), sds((padded, groups, 2 * HD), BF16), sds((1, model), F32),
            sds((1, model), F32), sds((1, hidden_width), F32),
        ],
        [
            low_scratch, low_scratch, full_scratch, full_scratch, low_scratch,
            pltpu.VMEM((model, model), BF16), pltpu.VMEM((2, model, width), BF16),
            weight_scratch, weight_scratch, hidden_scratch, hidden_scratch, hidden_scratch,
            pltpu.VMEM(hidden_pack, BF16), pltpu.VMEM(pre_pack, BF16),
            pltpu.VMEM((heads, positions, 2 * HD), F32), pltpu.SemaphoreType.DMA((5, 8)),
            pltpu.SemaphoreType.DMA((6,)), pltpu.SemaphoreType.DMA((2 * HIDDEN_BLOCKS + 2,)),
        ],
        cost=30,
    )(
        core_ref, offsets, gain_heads_all, gain_two, gain_hidden_all, x_own, heads_in, attended,
        log_all, seed, place, *weights_all,
    )

    def weight_grad(
        size, left, left_at, right, right_at, left_got_at, earlier=(), change=0, extra=None
    ):
        got = exchange(right, 1, 0)

        def spec(at):
            return pl.BlockSpec((tokens, width), lambda j: (0, at(j)))

        def rights():
            return [spec(lambda j, x=x: right_at(x, j)) for x in range(2)]

        sent_rows = 2 * quarter
        extras = []
        if extra is not None:
            sent_rows += GAIN_ROWS
            extras = [extra]
        return call(
            partial(weight_grad_kernel, change),
            (size // width,),
            [SMEM, spec(left_at)] + rights() + [spec(left_got_at)] + rights()
            + [pl.BlockSpec((GAIN_ROWS, width), lambda j: (0, j))] * len(extras),
            [
                pl.BlockSpec((2, quarter, width), lambda j: (0, 0, j)),
                pl.BlockSpec((sent_rows, width), lambda j: (0, j)),
            ],
            [sds((2, quarter, size), F32), sds((sent_rows, size), BF16)],
            [pltpu.VMEM((2, model // 2, tokens), BF16)],
            earlier=earlier,
            cost=7,
        )(core_ref, left, right, right, got, got, got, *extras)

    per_half = hidden_here // width
    hidden_blocks = hidden_width // width

    def both_rows(mine, earlier=None):
        mine = mine.reshape(rows, positions, model)
        other = exchange(mine, 0, 1)
        if earlier is not None:
            other = gate(other, earlier)
        first = jnp.where(head_index == 0, mine, other)
        second = jnp.where(head_index == 0, other, mine)
        return jnp.concatenate([first, second])

    far_grads = to_owners(grad_slots)
    near_grad = call(
        near_back_kernel,
        (rows,),
        [bias_row, qkv_row, model_row, model_row],
        qkv_row,
        sds((tokens, 3 * model), BF16),
        [pltpu.VMEM((heads, positions, positions), BF16)] * 2,
        cost=60,
    )(bias, qkv, grad_att, stats)
    reduce_kept, reduce_sent = weight_grad(
        hidden_here, seed, lambda j: 0, hidden_in, lambda x, j: x * per_half + j,
        lambda j: hidden_blocks, earlier=(near_grad,),
    )
    far_back = call(
        far_back_kernel,
        (owned,),
        [SMEM, by_pair(3 * HD), by_pair(2 * HD)],
        by_pair(3 * HD),
        owned_shape(3 * HD),
        [kv_scratch, pltpu.VMEM((slot_count, 2 * HD), F32)],
        earlier=(reduce_sent,),
        cost=1,
    )(parity, far_qkv, far_grads)
    expand_kept, expand_sent = weight_grad(
        hidden_here + width, lefts, lambda j: jnp.where(j < per_half, 0, 1), grad_pre,
        lambda x, j: jnp.where(j < per_half, x * per_half + j, hidden_blocks + x),
        lambda j: hidden_blocks + 2 + jnp.where(j < per_half, 0, 1),
        earlier=(far_back,), change=per_half,
    )
    back_here = from_owners(far_back)
    block_out = both_rows(block_mine, expand_sent)
    reduce_kept, reduce_sent, _ = scatter_first(reduce_kept, reduce_sent)
    grad_pack_shape = (tokens, 3 * model + model // 2)
    grad_pack = call(
        join_back_kernel,
        (rows,),
        [SMEM, qkv_row, of_row(3 * HD), model_row],
        by_row(grad_pack_shape[1]),
        sds(grad_pack_shape, BF16),
        earlier=(reduce_sent, block_out),
        cost=1,
    )(offsets, near_grad, back_here, first_in)
    grad_mine, grad_shared = call(
        input_grad_kernel,
        (),
        [
            SMEM, model_spec, whole(*grad_pack_shape), model_spec, whole(1, model),
            whole(1, model), whole(model, model),
        ]
        + [ANY] * 8,
        [model_spec, whole(8, model)],
        [sds(model_shape, BF16), sds((8, model), F32)],
        [attend_scratch, pltpu.SemaphoreType.DMA((8,))],
        cost=40,
    )(core_ref, x_own, grad_pack, grad_resid, gain_one, grad_second, place, *attend_all)

    expand_kept, expand_sent, _ = scatter_first(
        gate(expand_kept, grad_mine), expand_sent
    )
    def by_head(grad):
        size = grad.shape[1] // 2
        return jnp.where(head_index == 0, grad[0], jnp.roll(grad[0], size))

    grad_shared = gate(grad_shared, expand_sent)
    gains = jnp.concatenate(
        [
            grad_shared[0], grad_shared[1], by_head(grad_heads), by_head(grad_hidden),
        ]
    )
    gain_rows = -(-gains.shape[0] // (3 * width))
    gains = jnp.pad(gains, (0, gain_rows * 3 * width - gains.shape[0])).reshape(gain_rows, -1)
    gain_sent = to_rows(gains)
    reduce_kept, reduce_sent, _ = scatter_second(reduce_kept, reduce_sent)
    attend_kept, attend_sent = weight_grad(
        3 * width, first_in, lambda j: 0, grad_pack, lambda x, j: 3 * x + j, lambda j: 6,
        earlier=(grad_mine, *reduce_sent), extra=gain_sent,
    )
    attend_kept, attend_sent, attend_near = scatter_first(attend_kept, attend_sent)
    gains = from_rows(gain_sent, gain_rows) + from_rows(attend_near[2 * quarter :], gain_rows)
    gain_sent = to_rows(gains)
    reduce_total = scatter_far(reduce_kept, reduce_sent)
    expand_kept, expand_sent, _ = scatter_second(expand_kept, expand_sent)
    attend_sent = after(after(attend_sent, reduce_total), expand_sent[0])
    attend_kept, attend_sent, attend_got = scatter_second(
        attend_kept, jnp.concatenate([attend_sent, gain_sent])
    )
    gains = from_rows(gain_sent, gain_rows) + from_rows(attend_got[quarter:], gain_rows)
    stages = far_stages(seq_size)
    for stage in reversed(range(len(stages))):
        unit, radix = stages[stage]
        gain_sent = to_rows(gains)
        everyone = [from_rows(gain_sent, gain_rows)]
        rows_sent = attend_sent[0].shape[0]
        for i, piece in enumerate(attend_sent):
            got = exchange(jnp.concatenate([piece, gain_sent]), unit * (i + 1), 0)
            attend_kept = attend_kept + got[:rows_sent].astype(F32)
            everyone.append(from_rows(got[rows_sent:], gain_rows))
        while len(everyone) > 1:
            everyone = [one + two for one, two in zip(everyone[::2], everyone[1::2])]
        gains = everyone[0]
        if stage:
            held = attend_kept.reshape(stages[stage - 1][1], -1, 3 * width)
            attend_kept, attend_sent = held[0], [piece.astype(BF16) for piece in held[1:]]
    attend_last = jnp.concatenate([attend_kept[half_rows:], gains])
    attend_last = exchange(attend_last, 1, 0)
    gains = (gains + attend_last[half_rows:]).reshape(-1)
    attend_last = attend_last[:half_rows]
    attend_kept = attend_kept[:half_rows]
    grad_attend = jnp.concatenate(
        [
            jnp.where(core == 0, attend_kept, attend_last),
            jnp.where(core == 0, attend_last, attend_kept),
        ]
    )
    grad_reduce = scatter_core(gate(reduce_total, attend_got))
    grad_expand = scatter_core(scatter_far(gate(expand_kept, attend_got), expand_sent))
    grad_inputs = both_rows(grad_mine, attend_near)

    def own_half(start, size):
        return lax.dynamic_slice_in_dim(gains, start + head_index * size, size)

    return (
        block_out,
        grad_inputs,
        jnp.stack([grad_attend[:, e * width : (e + 1) * width] for e in range(3)]),
        grad_expand[:, hidden_here:].T,
        grad_expand[:, :hidden_here],
        grad_reduce.T,
        gains[:model],
        own_half(2 * model, width),
        gains[model : 2 * model],
        own_half(3 * model, hidden_here),
    )


def solution(mesh):
    placed = (
        P(None, "seq", None),
        P(None, "seq", "head"),
        P("head", "seq"),
        P("seq", "head"),
        P("head", "seq"),
        P(),
        P("head"),
        P(),
        P("head"),
        P(None, "seq", None),
        P(),
        P(),
        P(),
    )
    return jax.shard_map(
        per_device,
        mesh=mesh,
        in_specs=placed,
        out_specs=(
            P(None, "seq", None),
            P(None, "seq", None),
            P(None, "seq", "head"),
            P("head", "seq"),
            P("seq", "head"),
            P("head", "seq"),
            P(),
            P("head"),
            P(),
            P("head"),
        ),
        check_vma=False,
    )
```

```python
from functools import partial

import jax
import jax.numpy as jnp
from jax import lax
from jax.experimental import pallas as pl
from jax.experimental.pallas import tpu as pltpu
from jax.sharding import PartitionSpec as P

HD = 64
DILATION_SMALL = 8
NORM_EPSILON = 1e-05
MASKED_SCORE = -1e30
SCALE = HD ** (-0.5)
F32 = jnp.float32
BF16 = jnp.bfloat16
ANY = pl.BlockSpec(memory_space=pl.ANY)
SMEM = pl.BlockSpec(memory_space=pltpu.SMEM)
VMEM_LIMIT = 56 * 1024 * 1024


def nn(left, right):
    return lax.dot_general(left, right, (((1,), (0,)), ((), ())), preferred_element_type=F32)


def nt(left, right):
    return lax.dot_general(left, right, (((1,), (1,)), ((), ())), preferred_element_type=F32)


def tn(left, right):
    return lax.dot_general(left, right, (((0,), (0,)), ((), ())), preferred_element_type=F32)


def row_norm(values):
    center = jnp.mean(values, axis=-1, keepdims=True)
    spread = jnp.mean(values * values, axis=-1, keepdims=True) - center * center
    inverse = lax.rsqrt(spread + NORM_EPSILON)
    return (values - center) * inverse, inverse


def row_norm_back(incoming, normal, inverse, gain_row):
    scaled = incoming * gain_row
    first_mean = jnp.mean(scaled, axis=-1, keepdims=True)
    second_mean = jnp.mean(scaled * normal, axis=-1, keepdims=True)
    return inverse * (scaled - first_mean - normal * second_mean)


def three_parts(values):
    high = values.astype(BF16)
    rest = values - high.astype(F32)
    middle = rest.astype(BF16)
    low = (rest - middle.astype(F32)).astype(BF16)
    return high, middle, low


def gelu_parts(values):
    expo = jnp.exp(values * values * -0.5)
    term = 1.0 / (1.0 + (0.3275911 * 0.7071067811865476) * jnp.abs(values))
    poly = term * (
        0.254829592
        + term
        * (-0.284496736 + term * (1.421413741 + term * (-1.453152027 + term * 1.061405429)))
    )
    tail = 0.5 * poly * expo
    phi = jnp.where(values >= 0.0, 1.0 - tail, tail)
    return values * phi, phi + values * expo * 0.3989422804014327


def iota(shape, dim):
    return lax.broadcasted_iota(jnp.int32, shape, dim)


def permute(value, target):
    seq_size, head_size = lax.axis_size("seq"), lax.axis_size("head")
    pairs = []
    for s in range(seq_size):
        for h in range(head_size):
            to_seq, to_head = target(s, h)
            pairs.append((s * head_size + h, to_seq * head_size + to_head))
    return lax.ppermute(value, ("seq", "head"), pairs)


def exchange(value, seq_mask, head_mask):
    return permute(value, lambda s, h: (s ^ seq_mask, h ^ head_mask))


def exchange_near(value, turn):
    return permute(value, lambda s, h: (s, h ^ 1) if (s & 1) == turn else (s ^ 2, h))


def far_stages(seq_size):
    unit, left, stages = 4, seq_size // 4, []
    while left > 1:
        radix = 4 if left % 4 == 0 else 2
        stages.append((unit, radix))
        unit, left = unit * radix, left // radix
    return stages


def gate(value, *earlier):
    def kernel(*refs):
        pass

    return pl.pallas_call(
        kernel,
        in_specs=[ANY] * (len(earlier) + 1),
        out_specs=ANY,
        out_shape=jax.ShapeDtypeStruct(value.shape, value.dtype),
        input_output_aliases={len(earlier): 0},
        cost_estimate=pl.CostEstimate(flops=0, bytes_accessed=0, transcendentals=0),
    )(*earlier, value)


def after(value, earlier):
    zero = earlier[(0,) * earlier.ndim].astype(F32) * 0.0
    return value + zero.astype(value.dtype)


def gather_core(shard):
    core = lax.axis_index("seq") & 1
    half = shard.shape[0] // 2
    kept = lax.dynamic_slice_in_dim(shard, core * half, half)
    sent = lax.dynamic_slice_in_dim(shard, (1 - core) * half, half)
    return jnp.concatenate([kept, exchange(sent, 1, 0)])


def gather_far(held):
    stages = far_stages(lax.axis_size("seq"))
    for unit, radix in stages:
        pieces = [held] + [exchange(held, unit * i, 0) for i in range(1, radix)]
        held = jnp.concatenate(pieces) if (unit, radix) != stages[-1] else None
    return pieces


def scatter_first(kept, sent):
    got = exchange_near(sent, 1)
    block = kept.shape[1]

    def total(index):
        return kept[index].astype(F32) + got[index * block : (index + 1) * block].astype(F32)

    return total(0), total(1).astype(BF16), got


def scatter_second(kept, sent):
    got = exchange_near(sent, 0)
    total = kept + got[: kept.shape[0]].astype(F32)
    unit, radix = far_stages(lax.axis_size("seq"))[-1]
    total = total.reshape(radix, -1, total.shape[-1])
    return total[0], [total[i].astype(BF16) for i in range(1, radix)], got


def scatter_far(kept, sent):
    stages = far_stages(lax.axis_size("seq"))
    for stage in reversed(range(len(stages))):
        unit, radix = stages[stage]
        for i, piece in enumerate(sent):
            kept = kept + exchange(piece, unit * (i + 1), 0).astype(F32)
        if stage:
            held = kept.reshape(stages[stage - 1][1], -1, kept.shape[-1])
            kept, sent = held[0], [piece.astype(BF16) for piece in held[1:]]
    return kept


def to_rows(sums):
    high = lax.reduce_precision(sums, 8, 7)
    low = sums - high
    spare = jnp.zeros((GAIN_ROWS - 2 * sums.shape[0], sums.shape[1]), F32)
    return jnp.concatenate([high, low, spare]).astype(BF16)


def from_rows(rows, count):
    return rows[:count].astype(F32) + rows[count : 2 * count].astype(F32)


GAIN_ROWS = 16


def stream_copies(pieces, columns, target, sems, core):
    block = target.shape[1] // 4
    blocks = [
        piece.at[pl.ds(start, block), columns]
        for piece in pieces
        for start in range(0, piece.shape[0], block)
    ]
    copies = []
    for index, source in enumerate(blocks):
        part, second, first = index // 4, index // 2 % 2, index % 2
        straight = (core ^ part) == 0
        x = jnp.where(straight, first, second)
        y = jnp.where(straight, second, first)
        row = pl.multiple_of((2 * part + y) * block, block)
        copies.append(
            pltpu.make_async_copy(source, target.at[x, pl.ds(row, block)], sems.at[index])
        )
    return copies


def start_all(copies):
    for copy in copies:
        copy.start()


def wait_all(copies):
    for copy in copies:
        copy.wait()


def pair_columns(pair, per_group, width):
    group, inside = divmod(2 * pair, per_group)
    start = group * 3 * width + inside * HD
    return [slice(start + e * width, start + e * width + 2 * HD) for e in range(3)]


def slot_select(offset, groups, positions):
    shape = (groups, positions)
    return (iota(shape, 1) == DILATION_SMALL * iota(shape, 0) + offset).astype(BF16)


def slot_spread(offs, pair, groups, positions, times=1):
    shape = (positions, 2 * groups * times)
    slot = iota(shape, 1) & (2 * groups - 1)
    offset = jnp.where(slot < groups, offs[2 * pair], offs[2 * pair + 1])
    return (iota(shape, 0) == DILATION_SMALL * (slot & (groups - 1)) + offset).astype(BF16)


def side_masks():
    lane = iota((1, 2 * HD), 1)
    return (lane < HD).astype(BF16), (lane >= HD).astype(BF16)


def beside(even, odd):
    nothing = jnp.zeros_like(even)
    return jnp.concatenate(
        [jnp.concatenate([even, nothing], axis=1), jnp.concatenate([nothing, odd], axis=1)], axis=0
    )


def project_kernel(
    core_ref, offs, x_ref, bias_ref, gain_ref, w0, w1, w2, w3, w4, w5, w6, w7,
    first_ref, qkv_ref, slot_ref, out_ref, lse_ref, weights, score_scr, first_scr, qkv_scr,
    sems,
):
    _, positions = bias_ref.shape[:2]
    model = x_ref.shape[1]
    width = weights.shape[2] // 3
    heads = model // HD
    per_group = heads // 2
    groups = positions // DILATION_SMALL
    r = pl.program_id(0)

    @pl.when(r == 0)
    def _():
        pieces = (w0, w1, w2, w3, w4, w5, w6, w7)
        copies = stream_copies(pieces, slice(None), weights, sems, core_ref[0])
        start_all(copies)
        normal, _ = row_norm(x_ref[...].astype(F32))
        first_scr[...] = (normal * gain_ref[...]).astype(BF16)
        wait_all(copies)
        for hh in range(2):
            columns = slice(hh * 3 * width, (hh + 1) * 3 * width)
            qkv_scr[:, columns] = nn(first_scr[...], weights[hh]).astype(BF16)

    low, high = side_masks()
    side = iota((positions, 2 * HD), 1) < HD
    here = pl.ds(pl.multiple_of(r * positions, positions), positions)
    first_ref[...] = first_scr[here]
    qkv_ref[...] = qkv_scr[here]
    bias = bias_ref[0]
    bias = jnp.concatenate([bias, bias], axis=0)
    for pair in range(heads // 2):
        cq, ck, cv = pair_columns(pair, per_group, width)
        query, key = qkv_ref[:, cq], qkv_ref[:, ck]
        both = jnp.concatenate([query * low, query * high], axis=0)
        score_scr[pair] = nt(both, key) * SCALE + bias
        every = jnp.concatenate([query, key, qkv_ref[:, cv]], axis=1)
        for inside in range(2):
            chosen = slot_select(offs[2 * pair + inside], groups, positions)
            slots = nn(chosen, every).astype(BF16)
            starts = [2 * HD * e + HD * inside for e in range(3)]
            slot_ref[2 * pair + inside] = jnp.concatenate(
                [slots[:, start : start + HD] for start in starts], axis=1
            )
    for pair in range(heads // 2):
        value = qkv_ref[:, pair_columns(pair, per_group, width)[2]]
        score = score_scr[pair]
        peak = jnp.max(score, axis=-1, keepdims=True)
        expo = jnp.exp(score - peak)
        total = jnp.sum(expo, axis=-1, keepdims=True)
        expo = expo.astype(BF16)
        out = nn(
            jnp.concatenate([expo[:positions], expo[positions:]], axis=1),
            jnp.concatenate([value * low, value * high], axis=0),
        )
        columns = slice(2 * pair * HD, 2 * (pair + 1) * HD)
        log, scale = peak + jnp.log(total), 1.0 / total
        out_ref[:, columns] = out * jnp.where(side, scale[:positions], scale[positions:])
        lse_ref[:, columns] = jnp.where(side, log[:positions], log[positions:])


def far_masks(parity, row_start, row_count, slots):
    row = row_start + iota((row_count, slots), 0)
    column = iota((row_count, slots), 1)
    live_row = (parity == 0) | ((row & 1) == parity - 1)
    live_column = (parity == 0) | ((column & 1) == parity - 1)
    return (column <= row) & live_column, live_row


def for_blocks(count, body):
    if count == 1:
        body(0)
    else:
        lax.fori_loop(0, count, lambda b, carry: (body(b), carry)[1], 0)


def far_kernel(parity_ref, qkv_ref, out_ref, kv_scr):
    devices, _, groups, _ = qkv_ref.shape
    slots = devices * groups
    block = min(slots, 256)
    per_block = block // groups
    parity = parity_ref[pl.program_id(0)]
    kv_scr[...] = qkv_ref[:, 0].reshape(slots, 3 * HD)[:, HD:]

    def body(index):
        piece = pl.ds(index * per_block, per_block)
        query = qkv_ref[piece, 0].reshape(block, 3 * HD)[:, :HD]
        key, value = kv_scr[:, :HD], kv_scr[:, HD:]
        allowed, live = far_masks(parity, index * block, block, slots)
        score = jnp.where(allowed, nt(query, key) * SCALE, MASKED_SCORE)
        peak = jnp.max(score, axis=-1, keepdims=True)
        expo = jnp.exp(score - peak)
        total = jnp.sum(expo, axis=-1, keepdims=True)
        out = nn(expo.astype(BF16), value) / total
        log = jnp.where(live[:, :1], peak + jnp.log(total), MASKED_SCORE)
        high, middle, low = three_parts(log)
        lane = iota((block, 2 * HD), 1)
        tile = jnp.concatenate([out, out], axis=1)
        tile = jnp.where(lane == HD, high.astype(F32), tile)
        tile = jnp.where(lane == HD + 1, middle.astype(F32), tile)
        tile = jnp.where(lane == HD + 2, low.astype(F32), tile)
        out_ref[piece, 0] = tile.astype(BF16).reshape(per_block, groups, 2 * HD)

    for_blocks(slots // block, body)


HIDDEN_BLOCKS = 4


def hidden_kernel(
    core_ref, offs, gain_heads, gain_second, gain_hidden, far_ref, near_any, log_any, x_any,
    seed_any, place_any, a0, a1, a2, a3, b0, b1, b2, b3, c0, c1, c2, c3,
    block_ref, hidden_out, pre_out, left_ref, resid_ref, grad_ref, stats_ref, slot_ref,
    grad_heads, grad_second, grad_hidden,
    x_ref, att_ref, lse_ref, seed_ref, place_ref, merge_w, expand_w, reduce_w,
    act_scr, slope_scr, grad_scr, hidden_ref, pre_ref, tile_scr, sems, in_sems, out_sems,
):
    tokens, model = x_ref.shape
    hidden_here = expand_w.shape[2]
    half_model = model // 2
    width = merge_w.shape[2]
    heads = model // HD
    groups = slot_ref.shape[1]
    positions = groups * DILATION_SMALL
    hidden_width = 2 * hidden_here
    block = hidden_width // HIDDEN_BLOCKS
    core = core_ref[0]
    chunks = ((a0, a1, a2, a3), (b0, b1, b2, b3), (c0, c1, c2, c3))
    third = a0.shape[1]

    def chunk_copies(target, first_column, size, at):
        copies = []
        for chunk, pieces in enumerate(chunks):
            low = max(first_column, chunk * third)
            high = min(first_column + size, (chunk + 1) * third)
            if low < high:
                copies += stream_copies(
                    pieces,
                    pl.ds(low - chunk * third, high - low),
                    target.at[:, :, pl.ds(low - first_column, high - low)],
                    sems.at[at + len(copies) // 8],
                    core,
                )
        return copies

    expand_copies = chunk_copies(expand_w, 0, hidden_here, 0)
    merge_copies = chunk_copies(merge_w, hidden_here, width, 2)
    reduce_copies = chunk_copies(reduce_w, hidden_here + width, hidden_here, 3)
    inputs = [
        pltpu.make_async_copy(source, target, in_sems.at[i])
        for i, (source, target) in enumerate(
            (
                (near_any, att_ref), (log_any, lse_ref), (x_any, x_ref), (seed_any, seed_ref),
                (place_any, place_ref),
            )
        )
    ]
    start_all(inputs[:3])
    start_all(merge_copies)
    start_all(expand_copies)
    start_all(inputs[3:4])
    start_all(reduce_copies)
    start_all(inputs[4:])

    def columns_of(index):
        return slice(index * block, (index + 1) * block)

    def weight_block(weights, index):
        per_group = hidden_here // block
        inside = index % per_group
        return weights[index // per_group, :, inside * block : (inside + 1) * block]

    def send(source, target, index, start, size):
        columns = slice(start, start + size)
        copy = pltpu.make_async_copy(
            source.at[:, columns], target.at[:, columns], out_sems.at[index]
        )
        copy.start()
        return copy

    wait_all(inputs[:3])

    lane = iota((positions, 2 * HD), 1)
    side, inside_lane = lane < HD, lane & (HD - 1)
    place = iota((positions, 2 * HD), 0) & (DILATION_SMALL - 1)

    def join_row(r, carry):
        here = pl.ds(pl.multiple_of(r * positions, positions), positions)
        for pair in range(heads // 2):
            even, odd = far_ref[r * heads + 2 * pair], far_ref[r * heads + 2 * pair + 1]
            spread = slot_spread(offs, pair, groups, positions)
            far_out = nn(spread, beside(even[:, :HD], odd[:, :HD]))
            even, odd = even.astype(F32), odd.astype(F32)
            logs = [
                beside(
                    jnp.broadcast_to(even[:, HD + i : HD + i + 1], (groups, HD)),
                    jnp.broadcast_to(odd[:, HD + i : HD + i + 1], (groups, HD)),
                )
                for i in range(3)
            ]
            log_far = sum(nn(spread, log.astype(BF16)) for log in logs)
            slot = jnp.where(side, offs[2 * pair], offs[2 * pair + 1])
            log_far = jnp.where(place == slot, log_far, MASKED_SCORE)
            columns = slice(2 * pair * HD, 2 * (pair + 1) * HD)
            log_near = lse_ref[here, columns]
            peak = jnp.maximum(log_near, log_far)
            weight_near, weight_far = jnp.exp(log_near - peak), jnp.exp(log_far - peak)
            total = weight_near + weight_far
            lse_ref[here, columns] = pltpu.roll(peak + jnp.log(total), HD, 1)
            att_ref[here, columns] = (
                att_ref[here, columns] * weight_near + far_out * weight_far
            ) / total
        return carry

    lax.fori_loop(0, tokens // positions, join_row, 0)
    normal_heads, _ = row_norm(att_ref[...])
    heads_in = (normal_heads * gain_heads[...]).astype(BF16)
    wait_all(merge_copies)
    merged = [nt(heads_in[:, hh * width : (hh + 1) * width], merge_w[hh]) for hh in range(2)]
    residual = x_ref[...].astype(F32) + (merged[0] + merged[1])
    resid_ref[...] = residual
    normal_two, inverse_two = row_norm(residual)
    second_in = (normal_two * gain_second[...]).astype(BF16)
    start = hidden_width + model
    pre_ref[:, hidden_width:start] = heads_in
    pre_ref[:, start : start + half_model] = second_in[:, half_model:]
    left_ref[:, :half_model] = second_in[:, :half_model]
    wait_all(expand_copies)
    total_one = jnp.zeros((tokens, 1), F32)
    total_two = jnp.zeros((tokens, 1), F32)
    for index in range(HIDDEN_BLOCKS):
        columns = columns_of(index)
        act, slope = gelu_parts(nn(second_in, weight_block(expand_w, index)))
        act_scr[:, columns] = act
        slope_scr[:, columns] = slope
        total_one += jnp.sum(act, axis=-1, keepdims=True)
        total_two += jnp.sum(act * act, axis=-1, keepdims=True)
    center = total_one / hidden_width
    inverse = lax.rsqrt(total_two / hidden_width - center * center + NORM_EPSILON)
    wait_all(inputs[3:4])
    hidden_ref[:, hidden_width:] = seed_ref[:, half_model:]
    wait_all(reduce_copies)
    total_one = jnp.zeros((tokens, 1), F32)
    total_two = jnp.zeros((tokens, 1), F32)
    sends = []
    for index in range(HIDDEN_BLOCKS):
        columns = columns_of(index)
        normal = (act_scr[:, columns] - center) * inverse
        act_scr[:, columns] = normal
        gain = gain_hidden[:, columns]
        scaled = normal * gain
        hidden_ref[:, columns] = scaled.astype(BF16)
        sends.append(send(hidden_ref, hidden_out, index, index * block, block))
        grad = nn(seed_ref[...], weight_block(reduce_w, index))
        grad_hidden[:, columns] = jnp.sum(grad * normal, axis=0, keepdims=True)
        grad_scr[:, columns] = grad * gain
        total_one += jnp.sum(grad * gain, axis=-1, keepdims=True)
        total_two += jnp.sum(grad * scaled, axis=-1, keepdims=True)
    sends.append(send(hidden_ref, hidden_out, HIDDEN_BLOCKS, hidden_width, half_model))
    mean_one = total_one / hidden_width
    mean_two = total_two / hidden_width
    grad_second_in = jnp.zeros((tokens, model), F32)
    for index in range(HIDDEN_BLOCKS):
        columns = columns_of(index)
        grad = inverse * (grad_scr[:, columns] - mean_one - act_scr[:, columns] * mean_two)
        grad_pre = (grad * slope_scr[:, columns]).astype(BF16)
        pre_ref[:, columns] = grad_pre
        sends.append(send(pre_ref, pre_out, HIDDEN_BLOCKS + 1 + index, index * block, block))
        grad_second_in += nt(grad_pre, weight_block(expand_w, index))
    normal_two, inverse_two = row_norm(resid_ref[...])
    grad_second[...] = jnp.sum(grad_second_in * normal_two, axis=0, keepdims=True)
    resid = seed_ref[...].astype(F32) + row_norm_back(
        grad_second_in, normal_two, inverse_two, gain_second[...]
    )
    block_out = nt(hidden_ref[:, :hidden_here], reduce_w[0]) + nt(
        hidden_ref[:, hidden_here:hidden_width], reduce_w[1]
    )
    block_out = (resid_ref[...] + block_out).astype(BF16)
    resid_ref[...] = resid
    resid_low = resid.astype(BF16)
    left_ref[:, half_model:] = resid_low[:, :half_model]
    pre_ref[:, start + half_model :] = resid_low[:, half_model:]
    sends.append(send(pre_ref, pre_out, 2 * HIDDEN_BLOCKS + 1, hidden_width, 2 * model))
    grad_heads_in = jnp.concatenate([nn(resid_low, merge_w[hh]) for hh in range(2)], axis=1)
    wait_all(inputs[4:])
    block_ref[...] = nt(block_out, place_ref[...]).astype(BF16)
    normal_heads, inverse_heads = row_norm(att_ref[...])
    grad_heads[...] = jnp.sum(grad_heads_in * normal_heads, axis=0, keepdims=True)
    grad_att = row_norm_back(
        grad_heads_in, normal_heads, inverse_heads, gain_heads[...]
    ).astype(BF16)
    grad_ref[...] = grad_att
    grad_scr[:, :model] = grad_att.astype(F32) * att_ref[...]
    across = (iota((2 * HD, 2 * HD), 0) // HD != iota((2 * HD, 2 * HD), 1) // HD).astype(BF16)
    def for_row(r, carry):
        here = pl.ds(pl.multiple_of(r * positions, positions), positions)
        for pair in range(heads // 2):
            columns = slice(2 * pair * HD, 2 * (pair + 1) * HD)
            top, middle, _ = three_parts(grad_scr[here, columns])
            dots = nn(top, across) + nn(middle, across)
            stats = jnp.zeros((positions, 2 * HD), F32)
            for index, part in enumerate(three_parts(lse_ref[here, columns]) + three_parts(dots)):
                stats = jnp.where(inside_lane == index, part.astype(F32), stats)
            stats_ref[here, columns] = stats.astype(BF16)
            grad = grad_ref[here, columns].astype(F32)
            tile_scr[2 * pair] = jnp.where(side, grad, stats)
            tile_scr[2 * pair + 1] = jnp.where(side, stats, grad)
        for head in range(heads):
            tile = tile_scr[head, pl.ds(offs[head], groups, stride=DILATION_SMALL), :]
            if head % 2:
                tile = jnp.concatenate([tile[:, HD:], tile[:, :HD]], axis=1)
            slot_ref[r * heads + head] = tile.astype(BF16)
        return carry

    lax.fori_loop(0, tokens // positions, for_row, 0)
    wait_all(sends)


def far_back_kernel(parity_ref, qkv_ref, grad_ref, out_ref, kv_scr, total_scr):
    devices, _, groups, _ = qkv_ref.shape
    slots = devices * groups
    block = min(slots, 256)
    per_block = block // groups
    parity = parity_ref[pl.program_id(0)]
    kv_scr[...] = qkv_ref[:, 0].reshape(slots, 3 * HD)[:, HD:]
    total_scr[...] = jnp.zeros_like(total_scr)

    def body(index):
        piece = pl.ds(index * per_block, per_block)
        query = qkv_ref[piece, 0].reshape(block, 3 * HD)[:, :HD]
        tile = grad_ref[piece, 0].reshape(block, 2 * HD)
        key, value = kv_scr[:, :HD], kv_scr[:, HD:]
        grad = tile[:, :HD]
        stats = tile[:, HD:].astype(F32)
        log = stats[:, 0:1] + stats[:, 1:2] + stats[:, 2:3]
        dots = stats[:, 3:4] + stats[:, 4:5] + stats[:, 5:6]
        allowed, live = far_masks(parity, index * block, block, slots)
        score = jnp.where(allowed & live, nt(query, key) * SCALE - log, MASKED_SCORE)
        weight = jnp.exp(score)
        grad_score = (weight * (nt(grad, value) - dots)).astype(BF16)
        grad_query = nn(grad_score, key) * SCALE
        total_scr[:, :HD] += tn(grad_score, query) * SCALE
        total_scr[:, HD:] += tn(weight.astype(BF16), grad)
        out_ref[piece, 0, :, :HD] = grad_query.astype(BF16).reshape(per_block, groups, HD)

    for_blocks(slots // block, body)
    out_ref[:, 0, :, HD:] = total_scr[...].astype(BF16).reshape(devices, groups, 2 * HD)


def near_back_kernel(bias_ref, qkv_ref, grad_ref, stats_ref, out_ref, weight_scr, score_scr):
    positions, model = grad_ref.shape
    heads = model // HD
    per_group = heads // 2
    width = per_group * HD
    low, high = side_masks()
    inside = iota((1, 2 * HD), 1) & (HD - 1)
    less_log = jnp.where(inside < 3, -1.0 / SCALE, 0.0).astype(BF16)
    less_dots = jnp.where((inside >= 3) & (inside < 6), -1.0, 0.0).astype(BF16)

    bias = bias_ref[0]
    for pair in range(heads // 2):
        cq, ck, cv = pair_columns(pair, per_group, width)
        own = slice(2 * pair * HD, 2 * (pair + 1) * HD)
        query, key, value = qkv_ref[:, cq], qkv_ref[:, ck], qkv_ref[:, cv]
        grad, stats = grad_ref[:, own], stats_ref[:, own]
        for side, (mine, other) in enumerate(((low, high), (high, low))):
            more = stats * other
            score = nt(query * mine + more, key * mine + less_log * other)
            weight = jnp.exp(score * SCALE + bias)
            through = nt(grad * mine + more, value * mine + less_dots * other)
            weight_scr[2 * pair + side] = weight.astype(BF16)
            score_scr[2 * pair + side] = (weight * through).astype(BF16)
    for pair in range(heads // 2):
        cq, ck, cv = pair_columns(pair, per_group, width)
        own = slice(2 * pair * HD, 2 * (pair + 1) * HD)
        query, key, grad = qkv_ref[:, cq], qkv_ref[:, ck], grad_ref[:, own]
        even, odd = score_scr[2 * pair], score_scr[2 * pair + 1]
        out_ref[:, cq] = (SCALE * nn(
            jnp.concatenate([even, odd], axis=1),
            jnp.concatenate([key * low, key * high], axis=0),
        )).astype(BF16)
        out_ref[:, ck] = (SCALE * tn(
            jnp.concatenate([even, odd], axis=0),
            jnp.concatenate([query * low, query * high], axis=0),
        )).astype(BF16)
        out_ref[:, cv] = (tn(
            jnp.concatenate([weight_scr[2 * pair], weight_scr[2 * pair + 1]], axis=0),
            jnp.concatenate([grad * low, grad * high], axis=0),
        )).astype(BF16)


def join_back_kernel(offs, near_ref, far_ref, first_ref, out_ref):
    positions, model = first_ref.shape
    heads = model // HD
    per_group = heads // 2
    width = per_group * HD
    groups = far_ref.shape[1]
    out_ref[:, 3 * model :] = first_ref[:, model // 2 :]

    for pair in range(heads // 2):
        even, odd = far_ref[2 * pair], far_ref[2 * pair + 1]
        spread = slot_spread(offs, pair, groups, positions)
        for e, columns in enumerate(pair_columns(pair, per_group, width)):
            part = slice(e * HD, (e + 1) * HD)
            far = nn(spread, beside(even[:, part], odd[:, part]))
            out_ref[:, columns] = (near_ref[:, columns].astype(F32) + far).astype(BF16)


def weight_grad_kernel(
    change, core_ref, left, right_0, right_1, left_got, right_0_got, right_1_got,
    *refs,
):
    kept_ref, sent_ref, left_scr = refs[-3:]
    block = kept_ref.shape[1]
    if len(refs) > 3:
        sent_ref[2 * block :] = refs[0][...]
    step = pl.program_id(0)

    @pl.when((step == 0) | (step == change))
    def _():
        left_scr[0] = left[...].T
        left_scr[1] = left_got[...].T

    product = [
        nn(left_scr[0], right[...]) + nn(left_scr[1], got[...])
        for right, got in ((right_0, right_0_got), (right_1, right_1_got))
    ]
    kept_ref[0] = product[0][:block].astype(BF16)
    sent_ref[block : 2 * block] = product[1][block:].astype(BF16)
    low, high = product[0][block:], product[1][:block]

    @pl.when(core_ref[0] == 0)
    def _():
        kept_ref[1] = high.astype(BF16)
        sent_ref[:block] = low.astype(BF16)

    @pl.when(core_ref[0] != 0)
    def _():
        kept_ref[1] = low.astype(BF16)
        sent_ref[:block] = high.astype(BF16)


def input_grad_kernel(
    core_ref, x_ref, pack_ref, resid_ref, gain_ref, second_ref, place_ref, w0, w1, w2, w3, w4, w5, w6, w7,
    grad_ref, gain_grad, weights, sems,
):
    span = weights.shape[2]
    copies = stream_copies((w0, w1, w2, w3, w4, w5, w6, w7), slice(None), weights, sems, core_ref[0])
    start_all(copies)
    normal, inverse = row_norm(x_ref[...].astype(F32))
    wait_all(copies)
    grad_first = nt(pack_ref[:, :span], weights[0]) + nt(pack_ref[:, span : 2 * span], weights[1])
    first = jnp.sum(grad_first * normal, axis=0, keepdims=True)
    parts = three_parts(jnp.concatenate([first, second_ref[...]] + [jnp.zeros_like(first)] * 6))
    gain_grad[...] = sum(nt(part, place_ref[...]) for part in parts)
    grad = resid_ref[...] + row_norm_back(grad_first, normal, inverse, gain_ref[...])
    grad_ref[...] = nt(grad.astype(BF16), place_ref[...]).astype(BF16)


def finish_kernel(
    core_ref, kept_ref, got_ref, attend_ref, merge_ref, expand_ref, reduce_ref, gain_ref
):
    rows = attend_ref.shape[1] // 2
    width, hidden = merge_ref.shape[1], expand_ref.shape[1]
    gain_ref[...] = kept_ref[rows:, : 3 * width] + got_ref[rows:, : 3 * width]

    def place_halves(first, second):
        for half, source in enumerate((first, second)):
            here = slice(half * rows, (half + 1) * rows)
            for e in range(3):
                attend_ref[e, here] = source[:rows, e * width : (e + 1) * width]
            start = 3 * width
            expand_ref[here] = source[:rows, start : start + hidden]
            merge_ref[here] = source[:rows, start + hidden : start + hidden + width]
            reduce_ref[here] = source[:rows, start + hidden + width :]

    @pl.when(core_ref[0] == 0)
    def _():
        place_halves(kept_ref, got_ref)

    @pl.when(core_ref[0] != 0)
    def _():
        place_halves(got_ref, kept_ref)


def whole(*shape):
    return pl.BlockSpec(shape, lambda *_: tuple(0 for _ in shape))


def sds(shape, dtype):
    return jax.ShapeDtypeStruct(shape, dtype)


def call(
    kernel, grid, in_specs, out_specs, out_shape, scratch=(), earlier=(), cost=5
):
    def body(*refs):
        kernel(*refs[len(earlier) :])

    return partial(
        pl.pallas_call(
            body,
            grid=grid,
            in_specs=[ANY] * len(earlier) + in_specs,
            out_specs=out_specs,
            out_shape=out_shape,
            scratch_shapes=list(scratch),
            compiler_params=pltpu.CompilerParams(
                dimension_semantics=("arbitrary",) * len(grid), vmem_limit_bytes=VMEM_LIMIT
            ),
            cost_estimate=pl.CostEstimate(
                flops=cost * 1_150_000_000, bytes_accessed=0, transcendentals=0
            ),
        ),
        *earlier,
    )


def per_device(
    inputs,
    attend_weight,
    merge_weight,
    expand_weight,
    reduce_weight,
    gain_first,
    gain_heads,
    gain_second,
    gain_hidden,
    cotangent,
    lengths,
    local_span,
    dilation,
):
    seq_size, head_size = lax.axis_size("seq"), lax.axis_size("head")
    row_count, positions, model = inputs.shape
    rows = row_count // head_size
    tokens = rows * positions
    shard_rows, width = attend_weight.shape[1:]
    heads = width * head_size // HD
    group_heads = heads // head_size
    hidden_here = expand_weight.shape[1]
    hidden_width = hidden_here * head_size
    quarter = model // 4
    groups = positions // DILATION_SMALL
    pairs = rows * heads
    owned = -(-pairs // seq_size)
    padded = owned * seq_size
    seq_index, head_index = lax.axis_index("seq"), lax.axis_index("head")
    core = seq_index & 1
    core_ref = core.reshape(1)

    attend_shard = gather_core(jnp.concatenate(list(attend_weight), axis=1))
    attend_far = jnp.concatenate(gather_far(attend_shard))
    other_shard = jnp.concatenate([expand_weight, merge_weight.T, reduce_weight.T], axis=1)
    other_shard = gather_core(after(other_shard, attend_shard))
    third = other_shard.shape[1] // 3
    other_shards = [
        gate(other_shard[:, i * third : (i + 1) * third], attend_far) for i in range(3)
    ]
    attend_got = exchange_near(attend_far, 0)
    attend_more = exchange_near(attend_far, 1)
    other_pieces = [gather_far(other_shards[0])]
    attend_last = exchange_near(attend_got, 1)
    other_pieces.append(gather_far(gate(other_shards[1], attend_got)))
    other_far = [jnp.concatenate(pieces) for pieces in other_pieces]
    other_got = [exchange_near(other_far[0], 0)]
    attend_last = gate(attend_last, other_got[0])
    other_pieces.append(gather_far(gate(other_shards[2], attend_last)))
    attend_all = (attend_far, attend_got, attend_more, attend_last)
    attend_all = attend_all + tuple(exchange(piece, 1, 0) for piece in attend_all)
    both_gains = jnp.concatenate([gain_heads, gain_hidden])
    partner_gains = exchange(both_gains.reshape(-1, 128), 0, 1).reshape(-1)
    gain_heads_all = jnp.concatenate([gain_heads, partner_gains[:width]])[None]
    gain_hidden_all = jnp.concatenate([gain_hidden, partner_gains[width:]])[None]

    half_rows = shard_rows // 2
    part, near, far, beside, inside = jnp.meshgrid(
        *[jnp.arange(n) for n in (2, 2, seq_size // 4, 2, half_rows)], indexing="ij"
    )
    shard_of = seq_index ^ (4 * far + 2 * near + (beside ^ part))
    feature_of = (shard_of * shard_rows + (core ^ part) * half_rows + inside).reshape(-1)
    feature_of = gate(feature_of, attend_far)
    place = (jnp.arange(model)[:, None] == feature_of[None, :]).astype(BF16)

    def to_own_order(gain):
        return jnp.dot(
            gain[None], place.astype(F32), precision=lax.Precision.HIGHEST
        )

    gain_one, gain_two = to_own_order(gain_first), to_own_order(gain_second)
    row_start = head_index * rows
    lengths, local_span, dilation = gate(
        jnp.stack([lengths, local_span, dilation]), attend_far
    )

    def own_rows(tensor):
        return lax.dynamic_slice_in_dim(tensor, row_start, rows, axis=0)

    def in_own_order(tensor):
        return nn(tensor.reshape(tokens, model), place).astype(BF16)

    x_own = in_own_order(own_rows(inputs))
    places = jnp.arange(positions)
    in_length = (seq_index * positions + places)[None, :] < own_rows(lengths)[:, None]
    seed = in_own_order(
        jnp.where(in_length[..., None], own_rows(cotangent), jnp.zeros((), BF16))
    )
    span_block = places[None, :] // own_rows(local_span)[:, None]
    within = (span_block[:, :, None] == span_block[:, None, :]) & (
        places[None, :] <= places[:, None]
    )
    bias = jnp.where(within, 0.0, MASKED_SCORE).astype(F32)

    local_head = jnp.arange(heads)
    head_ids = (head_index ^ (local_head // group_heads)) * group_heads + local_head % group_heads
    offsets = gate((head_ids % DILATION_SMALL).astype(jnp.int32), attend_far)
    pair_ids = jnp.minimum(seq_index * owned + jnp.arange(owned), pairs - 1)
    pair_rate = own_rows(dilation)[pair_ids // heads]
    pair_head = head_ids[pair_ids % heads]
    parity = jnp.where(
        pair_rate == DILATION_SMALL, 0, 1 + (pair_head % pair_rate) // DILATION_SMALL
    ).astype(jnp.int32)

    model_spec, model_shape = whole(tokens, model), (tokens, model)
    attend_scratch = pltpu.VMEM((2, model, 3 * width), BF16)

    def by_row(size):
        return pl.BlockSpec((positions, size), lambda r: (r, 0))

    def of_row(size):
        return pl.BlockSpec((heads, groups, size), lambda r: (r, 0, 0))

    model_row, qkv_row = by_row(model), by_row(3 * model)
    bias_row = pl.BlockSpec((1, positions, positions), lambda r: (r, 0, 0))
    first_in, qkv, slots, near_out, log_near = call(
        project_kernel,
        (rows,),
        [SMEM, SMEM, model_spec, bias_row, whole(1, model)] + [ANY] * 8,
        [model_row, qkv_row, of_row(3 * HD), model_row, model_row],
        [
            sds(model_shape, BF16),
            sds((tokens, 3 * model), BF16),
            sds((padded, groups, 3 * HD), BF16),
            sds(model_shape, F32),
            sds(model_shape, F32),
        ],
        [
            attend_scratch,
            pltpu.VMEM((heads // 2, 2 * positions, positions), F32),
            pltpu.VMEM((tokens, model), BF16),
            pltpu.VMEM((tokens, 3 * model), BF16),
            pltpu.SemaphoreType.DMA((8,)),
        ],
        cost=20,
    )(core_ref, offsets, x_own, bias, gain_one, *attend_all)
    other_held = [jnp.concatenate([other_far[0], other_got[0]])]
    other_more = [exchange_near(other_held[0], 1)]
    other_got.append(exchange_near(other_far[1], 0))
    other_far.append(gate(jnp.concatenate(other_pieces[2]), other_more[0]))
    other_got.append(exchange_near(other_far[2], 0))
    other_held.append(jnp.concatenate([other_far[1], other_got[1]]))
    other_more.append(exchange_near(other_held[1], 1))
    other_core = [(exchange(other_held[0], 1, 0), exchange(other_more[0], 1, 0))]

    def to_owners(value):
        value = value.reshape(seq_size, owned, groups, value.shape[-1])
        return lax.all_to_all(value, "seq", 0, 0, tiled=True)

    def from_owners(value):
        value = lax.all_to_all(value, "seq", 0, 0, tiled=True)
        return value.reshape(padded, groups, value.shape[-1])

    def by_pair(size):
        return pl.BlockSpec((seq_size, 1, groups, size), lambda i: (0, i, 0, 0))

    def owned_shape(size):
        return sds((seq_size, owned, groups, size), BF16)

    slot_count = seq_size * groups
    kv_scratch = pltpu.VMEM((slot_count, 2 * HD), BF16)
    far_qkv = to_owners(slots)
    far_out = call(
        far_kernel,
        (owned,),
        [SMEM, by_pair(3 * HD)],
        by_pair(2 * HD),
        owned_shape(2 * HD),
        [kv_scratch],
        cost=4,
        earlier=(seed, place, gain_two),
    )(parity, far_qkv)
    far_here = from_owners(far_out)
    other_held.append(
        gate(jnp.concatenate([other_far[2], other_got[2]]), far_out)
    )
    other_more.append(exchange_near(other_held[2], 1))
    other_core.append((exchange(other_held[1], 1, 0), exchange(other_more[1], 1, 0)))
    held_core = exchange(other_held[2], 1, 0)

    other_core.append((held_core, exchange(other_more[2], 1, 0)))
    weights_all = [
        piece for i in range(3) for piece in (other_held[i], other_more[i], *other_core[i])
    ]
    hidden_pack = (tokens, hidden_width + model // 2)
    pre_pack = (tokens, hidden_width + 2 * model)
    low_scratch = pltpu.VMEM(model_shape, BF16)
    full_scratch = pltpu.VMEM(model_shape, F32)
    hidden_scratch = pltpu.VMEM((tokens, hidden_width), F32)
    weight_scratch = pltpu.VMEM((2, model, hidden_here), BF16)
    (
        block_mine, hidden_in, grad_pre, lefts, grad_resid, grad_att, stats, grad_slots,
        grad_heads, grad_second, grad_hidden,
    ) = call(
        hidden_kernel,
        (),
        [SMEM, SMEM, whole(1, model), whole(1, model), whole(1, hidden_width),
         whole(padded, groups, 2 * HD)] + [ANY] * 17,
        [
            model_spec, ANY, ANY, model_spec, model_spec, model_spec, model_spec,
            whole(padded, groups, 2 * HD), whole(1, model), whole(1, model),
            whole(1, hidden_width),
        ],
        [
            sds(model_shape, BF16), sds(hidden_pack, BF16), sds(pre_pack, BF16),
            sds(model_shape, BF16), sds(model_shape, F32), sds(model_shape, BF16),
            sds(model_shape, BF16), sds((padded, groups, 2 * HD), BF16), sds((1, model), F32),
            sds((1, model), F32), sds((1, hidden_width), F32),
        ],
        [
            low_scratch, full_scratch, full_scratch, low_scratch,
            pltpu.VMEM((model, model), BF16), pltpu.VMEM((2, model, width), BF16),
            weight_scratch, weight_scratch, hidden_scratch, hidden_scratch, hidden_scratch,
            pltpu.VMEM(hidden_pack, BF16), pltpu.VMEM(pre_pack, BF16),
            pltpu.VMEM((heads, positions, 2 * HD), F32), pltpu.SemaphoreType.DMA((5, 8)),
            pltpu.SemaphoreType.DMA((5,)), pltpu.SemaphoreType.DMA((2 * HIDDEN_BLOCKS + 2,)),
        ],
        cost=8,
    )(
        core_ref, offsets, gain_heads_all, gain_two, gain_hidden_all, far_here, near_out,
        log_near, x_own, seed, place, *weights_all,
    )

    def weight_grad(
        size, left, left_at, right, right_at, left_got_at, earlier=(), change=0, extra=None
    ):
        got = exchange(right, 1, 0)

        def spec(at):
            return pl.BlockSpec((tokens, width), lambda j: (0, at(j)))

        def rights():
            return [spec(lambda j, x=x: right_at(x, j)) for x in range(2)]

        sent_rows = 2 * quarter
        extras = []
        if extra is not None:
            sent_rows += GAIN_ROWS
            extras = [extra]
        return call(
            partial(weight_grad_kernel, change),
            (size // width,),
            [SMEM, spec(left_at)] + rights() + [spec(left_got_at)] + rights()
            + [pl.BlockSpec((GAIN_ROWS, width), lambda j: (0, j))] * len(extras),
            [
                pl.BlockSpec((2, quarter, width), lambda j: (0, 0, j)),
                pl.BlockSpec((sent_rows, width), lambda j: (0, j)),
            ],
            [sds((2, quarter, size), BF16), sds((sent_rows, size), BF16)],
            [pltpu.VMEM((2, model // 2, tokens), BF16)],
            earlier=earlier,
            cost=7,
        )(core_ref, left, right, right, got, got, got, *extras)

    per_half = hidden_here // width
    hidden_blocks = hidden_width // width

    def both_rows(mine, earlier=None):
        mine = mine.reshape(rows, positions, model)
        other = exchange(mine, 0, 1)
        if earlier is not None:
            other = gate(other, earlier)
        both = jnp.concatenate([other, other])
        return lax.dynamic_update_slice_in_dim(both, mine, row_start, axis=0)

    far_grads = to_owners(grad_slots)
    near_grad = call(
        near_back_kernel,
        (rows,),
        [bias_row, qkv_row, model_row, model_row],
        qkv_row,
        sds((tokens, 3 * model), BF16),
        [pltpu.VMEM((heads, positions, positions), BF16)] * 2,
        cost=60,
    )(bias, qkv, grad_att, stats)
    reduce_kept, reduce_sent = weight_grad(
        hidden_here, seed, lambda j: 0, hidden_in, lambda x, j: x * per_half + j,
        lambda j: hidden_blocks, earlier=(near_grad,),
    )
    far_back = call(
        far_back_kernel,
        (owned,),
        [SMEM, by_pair(3 * HD), by_pair(2 * HD)],
        by_pair(3 * HD),
        owned_shape(3 * HD),
        [kv_scratch, pltpu.VMEM((slot_count, 2 * HD), F32)],
        earlier=(reduce_sent,),
        cost=0,
    )(parity, far_qkv, far_grads)
    expand_kept, expand_sent = weight_grad(
        hidden_here + width, lefts, lambda j: jnp.where(j < per_half, 0, 1), grad_pre,
        lambda x, j: jnp.where(j < per_half, x * per_half + j, hidden_blocks + x),
        lambda j: hidden_blocks + 2 + jnp.where(j < per_half, 0, 1),
        earlier=(far_back,), change=per_half,
    )
    back_here = from_owners(far_back)
    block_out = both_rows(block_mine, expand_sent)
    reduce_kept, reduce_sent, _ = scatter_first(reduce_kept, reduce_sent)
    grad_pack_shape = (tokens, 3 * model + model // 2)
    grad_pack = call(
        join_back_kernel,
        (rows,),
        [SMEM, qkv_row, of_row(3 * HD), model_row],
        by_row(grad_pack_shape[1]),
        sds(grad_pack_shape, BF16),
        earlier=(reduce_sent, block_out),
        cost=1,
    )(offsets, near_grad, back_here, first_in)
    grad_mine, grad_shared = call(
        input_grad_kernel,
        (),
        [
            SMEM, model_spec, whole(*grad_pack_shape), model_spec, whole(1, model),
            whole(1, model), whole(model, model),
        ]
        + [ANY] * 8,
        [model_spec, whole(8, model)],
        [sds(model_shape, BF16), sds((8, model), F32)],
        [attend_scratch, pltpu.SemaphoreType.DMA((8,))],
        cost=3,
    )(core_ref, x_own, grad_pack, grad_resid, gain_one, grad_second, place, *attend_all)

    expand_kept, expand_sent, _ = scatter_first(
        gate(expand_kept, grad_mine), expand_sent
    )
    def by_head(grad):
        size = grad.shape[1] // 2
        return jnp.where(head_index == 0, grad[0], jnp.roll(grad[0], size))

    grad_shared = gate(grad_shared, expand_sent)
    gains = jnp.concatenate(
        [
            grad_shared[0], grad_shared[1], by_head(grad_heads), by_head(grad_hidden),
        ]
    )
    gain_rows = -(-gains.shape[0] // (3 * width))
    gains = jnp.pad(gains, (0, gain_rows * 3 * width - gains.shape[0])).reshape(gain_rows, -1)
    gain_sent = to_rows(gains)
    reduce_kept, reduce_sent, _ = scatter_second(reduce_kept, reduce_sent)
    attend_kept, attend_sent = weight_grad(
        3 * width, first_in, lambda j: 0, grad_pack, lambda x, j: 3 * x + j, lambda j: 6,
        earlier=(grad_mine, *reduce_sent), extra=gain_sent,
    )
    attend_kept, attend_sent, attend_near = scatter_first(attend_kept, attend_sent)
    gains = from_rows(gain_sent, gain_rows) + from_rows(attend_near[2 * quarter :], gain_rows)
    gain_sent = to_rows(gains)
    reduce_total = scatter_far(reduce_kept, reduce_sent)
    expand_kept, expand_sent, _ = scatter_second(expand_kept, expand_sent)
    attend_sent = after(after(attend_sent, reduce_total), expand_sent[0])
    attend_kept, attend_sent, attend_got = scatter_second(
        attend_kept, jnp.concatenate([attend_sent, gain_sent])
    )
    gains = from_rows(gain_sent, gain_rows) + from_rows(attend_got[quarter:], gain_rows)
    stages = far_stages(seq_size)
    for stage in reversed(range(len(stages))):
        unit, radix = stages[stage]
        gain_sent = to_rows(gains)
        everyone = [from_rows(gain_sent, gain_rows)]
        rows_sent = attend_sent[0].shape[0]
        for i, piece in enumerate(attend_sent):
            got = exchange(jnp.concatenate([piece, gain_sent]), unit * (i + 1), 0)
            attend_kept = attend_kept + got[:rows_sent].astype(F32)
            everyone.append(from_rows(got[rows_sent:], gain_rows))
        while len(everyone) > 1:
            everyone = [one + two for one, two in zip(everyone[::2], everyone[1::2])]
        gains = everyone[0]
        if stage:
            held = attend_kept.reshape(stages[stage - 1][1], -1, 3 * width)
            attend_kept, attend_sent = held[0], [piece.astype(BF16) for piece in held[1:]]
    grad_inputs = both_rows(gate(grad_mine, attend_got))
    expand_total = scatter_far(gate(expand_kept, attend_got), expand_sent)
    totals = jnp.concatenate([attend_kept, expand_total, reduce_total], axis=1)
    gains = jnp.pad(gains, ((0, 8 - gain_rows), (0, totals.shape[1] - gains.shape[1])))
    last_kept = jnp.concatenate([totals[:half_rows], gains])
    last_got = exchange(jnp.concatenate([totals[half_rows:], gains]), 1, 0)
    last_shape = last_kept.shape
    grad_attend, grad_merge, grad_expand, grad_reduce, gains = call(
        finish_kernel,
        (),
        [SMEM, whole(*last_shape), whole(*last_shape)],
        [
            whole(3, shard_rows, width), whole(shard_rows, width), whole(shard_rows, hidden_here),
            whole(shard_rows, hidden_here), whole(8, 3 * width),
        ],
        [
            sds((3, shard_rows, width), F32), sds((shard_rows, width), F32),
            sds((shard_rows, hidden_here), F32), sds((shard_rows, hidden_here), F32),
            sds((8, 3 * width), F32),
        ],
        cost=1,
    )(core_ref, last_kept, last_got)
    gains = gains[:gain_rows].reshape(-1)

    def own_half(start, size):
        return jnp.where(
            head_index == 0, gains[start : start + size], gains[start + size : start + 2 * size]
        )

    return (
        block_out,
        grad_inputs,
        grad_attend,
        grad_merge.T,
        grad_expand,
        grad_reduce.T,
        gains[:model],
        own_half(2 * model, width),
        gains[model : 2 * model],
        own_half(3 * model, hidden_here),
    )


def solution(mesh):
    placed = (
        P(None, "seq", None),
        P(None, "seq", "head"),
        P("head", "seq"),
        P("seq", "head"),
        P("head", "seq"),
        P(),
        P("head"),
        P(),
        P("head"),
        P(None, "seq", None),
        P(),
        P(),
        P(),
    )
    return jax.shard_map(
        per_device,
        mesh=mesh,
        in_specs=placed,
        out_specs=(
            P(None, "seq", None),
            P(None, "seq", None),
            P(None, "seq", "head"),
            P("head", "seq"),
            P("seq", "head"),
            P("head", "seq"),
            P(),
            P("head"),
            P(),
            P("head"),
        ),
        check_vma=False,
    )
```

```python
from functools import partial

import jax
import jax.numpy as jnp
from jax import lax
from jax.experimental import pallas as pl
from jax.experimental.pallas import tpu as pltpu
from jax.sharding import PartitionSpec as P

HD = 64
DILATION_SMALL = 8
NORM_EPSILON = 1e-05
MASKED_SCORE = -1e30
SCALE = HD ** (-0.5)
F32 = jnp.float32
BF16 = jnp.bfloat16
ANY = pl.BlockSpec(memory_space=pl.ANY)
SMEM = pl.BlockSpec(memory_space=pltpu.SMEM)
VMEM_LIMIT = 56 * 1024 * 1024


def nn(left, right):
    return lax.dot_general(left, right, (((1,), (0,)), ((), ())), preferred_element_type=F32)


def nt(left, right):
    return lax.dot_general(left, right, (((1,), (1,)), ((), ())), preferred_element_type=F32)


def tn(left, right):
    return lax.dot_general(left, right, (((0,), (0,)), ((), ())), preferred_element_type=F32)


def row_norm(values):
    center = jnp.mean(values, axis=-1, keepdims=True)
    spread = jnp.mean(values * values, axis=-1, keepdims=True) - center * center
    inverse = lax.rsqrt(spread + NORM_EPSILON)
    return (values - center) * inverse, inverse


def row_norm_back(incoming, normal, inverse, gain_row):
    scaled = incoming * gain_row
    first_mean = jnp.mean(scaled, axis=-1, keepdims=True)
    second_mean = jnp.mean(scaled * normal, axis=-1, keepdims=True)
    return inverse * (scaled - first_mean - normal * second_mean)


def three_parts(values):
    high = values.astype(BF16)
    rest = values - high.astype(F32)
    middle = rest.astype(BF16)
    low = (rest - middle.astype(F32)).astype(BF16)
    return high, middle, low


def gelu_parts(values):
    expo = jnp.exp(values * values * -0.5)
    term = 1.0 / (1.0 + (0.3275911 * 0.7071067811865476) * jnp.abs(values))
    poly = term * (
        0.254829592
        + term
        * (-0.284496736 + term * (1.421413741 + term * (-1.453152027 + term * 1.061405429)))
    )
    tail = 0.5 * poly * expo
    phi = jnp.where(values >= 0.0, 1.0 - tail, tail)
    return values * phi, phi + values * expo * 0.3989422804014327


def iota(shape, dim):
    return lax.broadcasted_iota(jnp.int32, shape, dim)


def permute(value, target):
    seq_size, head_size = lax.axis_size("seq"), lax.axis_size("head")
    pairs = []
    for s in range(seq_size):
        for h in range(head_size):
            to_seq, to_head = target(s, h)
            pairs.append((s * head_size + h, to_seq * head_size + to_head))
    return lax.ppermute(value, ("seq", "head"), pairs)


def exchange(value, seq_mask, head_mask):
    return permute(value, lambda s, h: (s ^ seq_mask, h ^ head_mask))


def exchange_near(value, turn):
    return permute(value, lambda s, h: (s, h ^ 1) if (s & 1) == turn else (s ^ 2, h))


def far_stages(seq_size):
    unit, left, stages = 4, seq_size // 4, []
    while left > 1:
        radix = 4 if left % 4 == 0 else 2
        stages.append((unit, radix))
        unit, left = unit * radix, left // radix
    return stages


def gate(value, *earlier):
    def kernel(*refs):
        pass

    return pl.pallas_call(
        kernel,
        in_specs=[ANY] * (len(earlier) + 1),
        out_specs=ANY,
        out_shape=jax.ShapeDtypeStruct(value.shape, value.dtype),
        input_output_aliases={len(earlier): 0},
        cost_estimate=pl.CostEstimate(flops=0, bytes_accessed=0, transcendentals=0),
    )(*earlier, value)


def after(value, earlier):
    zero = earlier[(0,) * earlier.ndim].astype(F32) * 0.0
    return value + zero.astype(value.dtype)


def gather_core(shard):
    core = lax.axis_index("seq") & 1
    half = shard.shape[0] // 2
    kept = lax.dynamic_slice_in_dim(shard, core * half, half)
    sent = lax.dynamic_slice_in_dim(shard, (1 - core) * half, half)
    return jnp.concatenate([kept, exchange(sent, 1, 0)])


def gather_far(held):
    stages = far_stages(lax.axis_size("seq"))
    for unit, radix in stages:
        pieces = [held] + [exchange(held, unit * i, 0) for i in range(1, radix)]
        held = jnp.concatenate(pieces) if (unit, radix) != stages[-1] else None
    return pieces


def scatter_first(kept, sent):
    got = exchange_near(sent, 1)
    block = kept.shape[1]

    def total(index):
        return kept[index].astype(F32) + got[index * block : (index + 1) * block].astype(F32)

    return total(0), total(1).astype(BF16), got


def scatter_second(kept, sent):
    got = exchange_near(sent, 0)
    total = kept + got[: kept.shape[0]].astype(F32)
    unit, radix = far_stages(lax.axis_size("seq"))[-1]
    total = total.reshape(radix, -1, total.shape[-1])
    return total[0], [total[i].astype(BF16) for i in range(1, radix)], got


def scatter_far(kept, sent):
    stages = far_stages(lax.axis_size("seq"))
    for stage in reversed(range(len(stages))):
        unit, radix = stages[stage]
        for i, piece in enumerate(sent):
            kept = kept + exchange(piece, unit * (i + 1), 0).astype(F32)
        if stage:
            held = kept.reshape(stages[stage - 1][1], -1, kept.shape[-1])
            kept, sent = held[0], [piece.astype(BF16) for piece in held[1:]]
    return kept


def to_rows(sums):
    high = lax.reduce_precision(sums, 8, 7)
    low = sums - high
    spare = jnp.zeros((GAIN_ROWS - 2 * sums.shape[0], sums.shape[1]), F32)
    return jnp.concatenate([high, low, spare]).astype(BF16)


def from_rows(rows, count):
    return rows[:count].astype(F32) + rows[count : 2 * count].astype(F32)


GAIN_ROWS = 16


def stream_copies(pieces, columns, target, sems, core):
    block = target.shape[1] // 4
    blocks = [
        piece.at[pl.ds(start, block), columns]
        for piece in pieces
        for start in range(0, piece.shape[0], block)
    ]
    copies = []
    for index, source in enumerate(blocks):
        part, second, first = index // 4, index // 2 % 2, index % 2
        straight = (core ^ part) == 0
        x = jnp.where(straight, first, second)
        y = jnp.where(straight, second, first)
        row = pl.multiple_of((2 * part + y) * block, block)
        copies.append(
            pltpu.make_async_copy(source, target.at[x, pl.ds(row, block)], sems.at[index])
        )
    return copies


def start_all(copies):
    for copy in copies:
        copy.start()


def wait_all(copies):
    for copy in copies:
        copy.wait()


def pair_columns(pair, per_group, width):
    group, inside = divmod(2 * pair, per_group)
    start = group * 3 * width + inside * HD
    return [slice(start + e * width, start + e * width + 2 * HD) for e in range(3)]


def slot_select(offset, groups, positions):
    shape = (groups, positions)
    return (iota(shape, 1) == DILATION_SMALL * iota(shape, 0) + offset).astype(BF16)


def slot_spread(offs, pair, groups, positions, times=1):
    shape = (positions, 2 * groups * times)
    slot = iota(shape, 1) & (2 * groups - 1)
    offset = jnp.where(slot < groups, offs[2 * pair], offs[2 * pair + 1])
    return (iota(shape, 0) == DILATION_SMALL * (slot & (groups - 1)) + offset).astype(BF16)


def side_masks():
    lane = iota((1, 2 * HD), 1)
    return (lane < HD).astype(BF16), (lane >= HD).astype(BF16)


def beside(even, odd):
    nothing = jnp.zeros_like(even)
    return jnp.concatenate(
        [jnp.concatenate([even, nothing], axis=1), jnp.concatenate([nothing, odd], axis=1)], axis=0
    )


def prepare_kernel(
    head_ref, scalars, feature_ref, gains_ref, x_ref, seed_ref, place_out, x_out, seed_out, gains_out
):
    rows, positions, model = x_ref.shape
    feature = feature_ref[...]
    place = (iota((model, model), 0) == feature).astype(BF16)
    place_out[...] = place
    at = scalars[rows] + iota((positions, model), 0)
    for r in range(rows):
        here = slice(r * positions, (r + 1) * positions)
        x_out[here] = nn(x_ref[r], place).astype(BF16)
        seed = jnp.where(at < scalars[r], seed_ref[r].astype(F32), 0.0).astype(BF16)
        seed_out[here] = nn(seed, place).astype(BF16)
    gains_out[...] = sum(nn(part, place) for part in three_parts(gains_ref[...]))


def project_kernel(
    core_ref, offs, x_ref, bias_ref, gain_ref, w0, w1, w2, w3, w4, w5, w6, w7,
    first_ref, qkv_ref, slot_ref, out_ref, lse_ref, weights, score_scr, first_scr, qkv_scr,
    sems,
):
    _, positions = bias_ref.shape[:2]
    model = x_ref.shape[1]
    width = weights.shape[2] // 3
    heads = model // HD
    per_group = heads // 2
    groups = positions // DILATION_SMALL
    r = pl.program_id(0)

    @pl.when(r == 0)
    def _():
        pieces = (w0, w1, w2, w3, w4, w5, w6, w7)
        copies = stream_copies(pieces, slice(None), weights, sems, core_ref[0])
        start_all(copies)
        normal, _ = row_norm(x_ref[...].astype(F32))
        first_scr[...] = (normal * gain_ref[...]).astype(BF16)
        wait_all(copies)
        for hh in range(2):
            columns = slice(hh * 3 * width, (hh + 1) * 3 * width)
            qkv_scr[:, columns] = nn(first_scr[...], weights[hh]).astype(BF16)

    low, high = side_masks()
    side = iota((positions, 2 * HD), 1) < HD
    here = pl.ds(pl.multiple_of(r * positions, positions), positions)
    first_ref[...] = first_scr[here]
    qkv_ref[...] = qkv_scr[here]
    bias = bias_ref[0]
    bias = jnp.concatenate([bias, bias], axis=0)
    for pair in range(heads // 2):
        cq, ck, cv = pair_columns(pair, per_group, width)
        query, key = qkv_ref[:, cq], qkv_ref[:, ck]
        both = jnp.concatenate([query * low, query * high], axis=0)
        score_scr[pair] = nt(both, key) * SCALE + bias
        every = jnp.concatenate([query, key, qkv_ref[:, cv]], axis=1)
        for inside in range(2):
            chosen = slot_select(offs[2 * pair + inside], groups, positions)
            slots = nn(chosen, every).astype(BF16)
            starts = [2 * HD * e + HD * inside for e in range(3)]
            slot_ref[2 * pair + inside] = jnp.concatenate(
                [slots[:, start : start + HD] for start in starts], axis=1
            )
    for pair in range(heads // 2):
        value = qkv_ref[:, pair_columns(pair, per_group, width)[2]]
        score = score_scr[pair]
        peak = jnp.max(score, axis=-1, keepdims=True)
        expo = jnp.exp(score - peak)
        total = jnp.sum(expo, axis=-1, keepdims=True)
        expo = expo.astype(BF16)
        out = nn(
            jnp.concatenate([expo[:positions], expo[positions:]], axis=1),
            jnp.concatenate([value * low, value * high], axis=0),
        )
        columns = slice(2 * pair * HD, 2 * (pair + 1) * HD)
        log, scale = peak + jnp.log(total), 1.0 / total
        out_ref[:, columns] = out * jnp.where(side, scale[:positions], scale[positions:])
        lse_ref[:, columns] = jnp.where(side, log[:positions], log[positions:])


def far_masks(parity, row_start, row_count, slots):
    row = row_start + iota((row_count, slots), 0)
    column = iota((row_count, slots), 1)
    live_row = (parity == 0) | ((row & 1) == parity - 1)
    live_column = (parity == 0) | ((column & 1) == parity - 1)
    return (column <= row) & live_column, live_row


def for_blocks(count, body):
    if count == 1:
        body(0)
    else:
        lax.fori_loop(0, count, lambda b, carry: (body(b), carry)[1], 0)


def far_kernel(parity_ref, qkv_ref, out_ref, kv_scr):
    devices, _, groups, _ = qkv_ref.shape
    slots = devices * groups
    block = min(slots, 256)
    per_block = block // groups
    parity = parity_ref[pl.program_id(0)]
    kv_scr[...] = qkv_ref[:, 0].reshape(slots, 3 * HD)[:, HD:]

    def body(index):
        piece = pl.ds(index * per_block, per_block)
        query = qkv_ref[piece, 0].reshape(block, 3 * HD)[:, :HD]
        key, value = kv_scr[:, :HD], kv_scr[:, HD:]
        allowed, live = far_masks(parity, index * block, block, slots)
        score = jnp.where(allowed, nt(query, key) * SCALE, MASKED_SCORE)
        peak = jnp.max(score, axis=-1, keepdims=True)
        expo = jnp.exp(score - peak)
        total = jnp.sum(expo, axis=-1, keepdims=True)
        out = nn(expo.astype(BF16), value) / total
        log = jnp.where(live[:, :1], peak + jnp.log(total), MASKED_SCORE)
        high, middle, low = three_parts(log)
        lane = iota((block, 2 * HD), 1)
        tile = jnp.concatenate([out, out], axis=1)
        tile = jnp.where(lane == HD, high.astype(F32), tile)
        tile = jnp.where(lane == HD + 1, middle.astype(F32), tile)
        tile = jnp.where(lane == HD + 2, low.astype(F32), tile)
        out_ref[piece, 0] = tile.astype(BF16).reshape(per_block, groups, 2 * HD)

    for_blocks(slots // block, body)


HIDDEN_BLOCKS = 4


def hidden_kernel(
    core_ref, offs, gain_heads, gain_second, gain_hidden, far_ref, near_any, log_any, x_any,
    seed_any, place_any, a0, a1, a2, a3, b0, b1, b2, b3, c0, c1, c2, c3,
    block_ref, hidden_out, pre_out, left_ref, resid_ref, grad_ref, stats_ref, slot_ref,
    grad_heads, grad_second, grad_hidden,
    x_ref, att_ref, lse_ref, seed_ref, place_ref, merge_w, expand_w, reduce_w,
    act_scr, slope_scr, grad_scr, hidden_ref, pre_ref, tile_scr, sems, in_sems, out_sems,
):
    tokens, model = x_ref.shape
    hidden_here = expand_w.shape[2]
    half_model = model // 2
    width = merge_w.shape[2]
    heads = model // HD
    groups = slot_ref.shape[1]
    positions = groups * DILATION_SMALL
    hidden_width = 2 * hidden_here
    block = hidden_width // HIDDEN_BLOCKS
    core = core_ref[0]
    chunks = ((a0, a1, a2, a3), (b0, b1, b2, b3), (c0, c1, c2, c3))
    third = a0.shape[1]

    def chunk_copies(target, first_column, size, at):
        copies = []
        for chunk, pieces in enumerate(chunks):
            low = max(first_column, chunk * third)
            high = min(first_column + size, (chunk + 1) * third)
            if low < high:
                copies += stream_copies(
                    pieces,
                    pl.ds(low - chunk * third, high - low),
                    target.at[:, :, pl.ds(low - first_column, high - low)],
                    sems.at[at + len(copies) // 8],
                    core,
                )
        return copies

    expand_copies = chunk_copies(expand_w, 0, hidden_here, 0)
    merge_copies = chunk_copies(merge_w, hidden_here, width, 2)
    reduce_copies = chunk_copies(reduce_w, hidden_here + width, hidden_here, 3)
    inputs = [
        pltpu.make_async_copy(source, target, in_sems.at[i])
        for i, (source, target) in enumerate(
            (
                (near_any, att_ref), (log_any, lse_ref), (x_any, x_ref), (seed_any, seed_ref),
                (place_any, place_ref),
            )
        )
    ]
    start_all(inputs[:3])
    start_all(merge_copies)
    start_all(expand_copies)
    start_all(inputs[3:4])
    start_all(reduce_copies)
    start_all(inputs[4:])

    def columns_of(index):
        return slice(index * block, (index + 1) * block)

    def weight_block(weights, index):
        per_group = hidden_here // block
        inside = index % per_group
        return weights[index // per_group, :, inside * block : (inside + 1) * block]

    def send(source, target, index, start, size):
        columns = slice(start, start + size)
        copy = pltpu.make_async_copy(
            source.at[:, columns], target.at[:, columns], out_sems.at[index]
        )
        copy.start()
        return copy

    wait_all(inputs[:3])

    lane = iota((positions, 2 * HD), 1)
    side, inside_lane = lane < HD, lane & (HD - 1)
    place = iota((positions, 2 * HD), 0) & (DILATION_SMALL - 1)

    def join_row(r, carry):
        here = pl.ds(pl.multiple_of(r * positions, positions), positions)
        for pair in range(heads // 2):
            even, odd = far_ref[r * heads + 2 * pair], far_ref[r * heads + 2 * pair + 1]
            spread = slot_spread(offs, pair, groups, positions)
            far_out = nn(spread, beside(even[:, :HD], odd[:, :HD]))
            even, odd = even.astype(F32), odd.astype(F32)
            logs = [
                beside(
                    jnp.broadcast_to(even[:, HD + i : HD + i + 1], (groups, HD)),
                    jnp.broadcast_to(odd[:, HD + i : HD + i + 1], (groups, HD)),
                )
                for i in range(3)
            ]
            log_far = sum(nn(spread, log.astype(BF16)) for log in logs)
            slot = jnp.where(side, offs[2 * pair], offs[2 * pair + 1])
            log_far = jnp.where(place == slot, log_far, MASKED_SCORE)
            columns = slice(2 * pair * HD, 2 * (pair + 1) * HD)
            log_near = lse_ref[here, columns]
            peak = jnp.maximum(log_near, log_far)
            weight_near, weight_far = jnp.exp(log_near - peak), jnp.exp(log_far - peak)
            total = weight_near + weight_far
            lse_ref[here, columns] = pltpu.roll(peak + jnp.log(total), HD, 1)
            att_ref[here, columns] = (
                att_ref[here, columns] * weight_near + far_out * weight_far
            ) / total
        return carry

    lax.fori_loop(0, tokens // positions, join_row, 0)
    normal_heads, _ = row_norm(att_ref[...])
    heads_in = (normal_heads * gain_heads[...]).astype(BF16)
    wait_all(merge_copies)
    merged = [nt(heads_in[:, hh * width : (hh + 1) * width], merge_w[hh]) for hh in range(2)]
    residual = x_ref[...].astype(F32) + (merged[0] + merged[1])
    resid_ref[...] = residual
    normal_two, inverse_two = row_norm(residual)
    second_in = (normal_two * gain_second[...]).astype(BF16)
    start = hidden_width + model
    pre_ref[:, hidden_width:start] = heads_in
    pre_ref[:, start : start + half_model] = second_in[:, half_model:]
    left_ref[:, :half_model] = second_in[:, :half_model]
    wait_all(expand_copies)
    total_one = jnp.zeros((tokens, 1), F32)
    total_two = jnp.zeros((tokens, 1), F32)
    for index in range(HIDDEN_BLOCKS):
        columns = columns_of(index)
        act, slope = gelu_parts(nn(second_in, weight_block(expand_w, index)))
        act_scr[:, columns] = act
        slope_scr[:, columns] = slope
        total_one += jnp.sum(act, axis=-1, keepdims=True)
        total_two += jnp.sum(act * act, axis=-1, keepdims=True)
    center = total_one / hidden_width
    inverse = lax.rsqrt(total_two / hidden_width - center * center + NORM_EPSILON)
    wait_all(inputs[3:4])
    hidden_ref[:, hidden_width:] = seed_ref[:, half_model:]
    wait_all(reduce_copies)
    total_one = jnp.zeros((tokens, 1), F32)
    total_two = jnp.zeros((tokens, 1), F32)
    sends = []
    for index in range(HIDDEN_BLOCKS):
        columns = columns_of(index)
        normal = (act_scr[:, columns] - center) * inverse
        act_scr[:, columns] = normal
        gain = gain_hidden[:, columns]
        scaled = normal * gain
        hidden_ref[:, columns] = scaled.astype(BF16)
        sends.append(send(hidden_ref, hidden_out, index, index * block, block))
        grad = nn(seed_ref[...], weight_block(reduce_w, index))
        grad_hidden[:, columns] = jnp.sum(grad * normal, axis=0, keepdims=True)
        grad_scr[:, columns] = grad * gain
        total_one += jnp.sum(grad * gain, axis=-1, keepdims=True)
        total_two += jnp.sum(grad * scaled, axis=-1, keepdims=True)
    sends.append(send(hidden_ref, hidden_out, HIDDEN_BLOCKS, hidden_width, half_model))
    mean_one = total_one / hidden_width
    mean_two = total_two / hidden_width
    grad_second_in = jnp.zeros((tokens, model), F32)
    for index in range(HIDDEN_BLOCKS):
        columns = columns_of(index)
        grad = inverse * (grad_scr[:, columns] - mean_one - act_scr[:, columns] * mean_two)
        grad_pre = (grad * slope_scr[:, columns]).astype(BF16)
        pre_ref[:, columns] = grad_pre
        sends.append(send(pre_ref, pre_out, HIDDEN_BLOCKS + 1 + index, index * block, block))
        grad_second_in += nt(grad_pre, weight_block(expand_w, index))
    normal_two, inverse_two = row_norm(resid_ref[...])
    grad_second[...] = jnp.sum(grad_second_in * normal_two, axis=0, keepdims=True)
    resid = seed_ref[...].astype(F32) + row_norm_back(
        grad_second_in, normal_two, inverse_two, gain_second[...]
    )
    block_out = nt(hidden_ref[:, :hidden_here], reduce_w[0]) + nt(
        hidden_ref[:, hidden_here:hidden_width], reduce_w[1]
    )
    block_out = (resid_ref[...] + block_out).astype(BF16)
    resid_ref[...] = resid
    resid_low = resid.astype(BF16)
    left_ref[:, half_model:] = resid_low[:, :half_model]
    pre_ref[:, start + half_model :] = resid_low[:, half_model:]
    sends.append(send(pre_ref, pre_out, 2 * HIDDEN_BLOCKS + 1, hidden_width, 2 * model))
    grad_heads_in = jnp.concatenate([nn(resid_low, merge_w[hh]) for hh in range(2)], axis=1)
    wait_all(inputs[4:])
    block_ref[...] = nt(block_out, place_ref[...]).astype(BF16)
    normal_heads, inverse_heads = row_norm(att_ref[...])
    grad_heads[...] = jnp.sum(grad_heads_in * normal_heads, axis=0, keepdims=True)
    grad_att = row_norm_back(
        grad_heads_in, normal_heads, inverse_heads, gain_heads[...]
    ).astype(BF16)
    grad_ref[...] = grad_att
    grad_scr[:, :model] = grad_att.astype(F32) * att_ref[...]
    across = (iota((2 * HD, 2 * HD), 0) // HD != iota((2 * HD, 2 * HD), 1) // HD).astype(BF16)
    def for_row(r, carry):
        here = pl.ds(pl.multiple_of(r * positions, positions), positions)
        for pair in range(heads // 2):
            columns = slice(2 * pair * HD, 2 * (pair + 1) * HD)
            top, middle, _ = three_parts(grad_scr[here, columns])
            dots = nn(top, across) + nn(middle, across)
            stats = jnp.zeros((positions, 2 * HD), F32)
            for index, part in enumerate(three_parts(lse_ref[here, columns]) + three_parts(dots)):
                stats = jnp.where(inside_lane == index, part.astype(F32), stats)
            stats_ref[here, columns] = stats.astype(BF16)
            grad = grad_ref[here, columns].astype(F32)
            tile_scr[2 * pair] = jnp.where(side, grad, stats)
            tile_scr[2 * pair + 1] = jnp.where(side, stats, grad)
        for head in range(heads):
            tile = tile_scr[head, pl.ds(offs[head], groups, stride=DILATION_SMALL), :]
            if head % 2:
                tile = jnp.concatenate([tile[:, HD:], tile[:, :HD]], axis=1)
            slot_ref[r * heads + head] = tile.astype(BF16)
        return carry

    lax.fori_loop(0, tokens // positions, for_row, 0)
    wait_all(sends)


def far_back_kernel(parity_ref, qkv_ref, grad_ref, out_ref, kv_scr, total_scr):
    devices, _, groups, _ = qkv_ref.shape
    slots = devices * groups
    block = min(slots, 256)
    per_block = block // groups
    parity = parity_ref[pl.program_id(0)]
    kv_scr[...] = qkv_ref[:, 0].reshape(slots, 3 * HD)[:, HD:]
    total_scr[...] = jnp.zeros_like(total_scr)

    def body(index):
        piece = pl.ds(index * per_block, per_block)
        query = qkv_ref[piece, 0].reshape(block, 3 * HD)[:, :HD]
        tile = grad_ref[piece, 0].reshape(block, 2 * HD)
        key, value = kv_scr[:, :HD], kv_scr[:, HD:]
        grad = tile[:, :HD]
        stats = tile[:, HD:].astype(F32)
        log = stats[:, 0:1] + stats[:, 1:2] + stats[:, 2:3]
        dots = stats[:, 3:4] + stats[:, 4:5] + stats[:, 5:6]
        allowed, live = far_masks(parity, index * block, block, slots)
        score = jnp.where(allowed & live, nt(query, key) * SCALE - log, MASKED_SCORE)
        weight = jnp.exp(score)
        grad_score = (weight * (nt(grad, value) - dots)).astype(BF16)
        grad_query = nn(grad_score, key) * SCALE
        total_scr[:, :HD] += tn(grad_score, query) * SCALE
        total_scr[:, HD:] += tn(weight.astype(BF16), grad)
        out_ref[piece, 0, :, :HD] = grad_query.astype(BF16).reshape(per_block, groups, HD)

    for_blocks(slots // block, body)
    out_ref[:, 0, :, HD:] = total_scr[...].astype(BF16).reshape(devices, groups, 2 * HD)


def near_back_kernel(bias_ref, qkv_ref, grad_ref, stats_ref, out_ref, weight_scr, score_scr):
    positions, model = grad_ref.shape
    heads = model // HD
    per_group = heads // 2
    width = per_group * HD
    low, high = side_masks()
    inside = iota((1, 2 * HD), 1) & (HD - 1)
    less_log = jnp.where(inside < 3, -1.0 / SCALE, 0.0).astype(BF16)
    less_dots = jnp.where((inside >= 3) & (inside < 6), -1.0, 0.0).astype(BF16)

    bias = bias_ref[0]
    for pair in range(heads // 2):
        cq, ck, cv = pair_columns(pair, per_group, width)
        own = slice(2 * pair * HD, 2 * (pair + 1) * HD)
        query, key, value = qkv_ref[:, cq], qkv_ref[:, ck], qkv_ref[:, cv]
        grad, stats = grad_ref[:, own], stats_ref[:, own]
        for side, (mine, other) in enumerate(((low, high), (high, low))):
            more = stats * other
            score = nt(query * mine + more, key * mine + less_log * other)
            weight = jnp.exp(score * SCALE + bias)
            through = nt(grad * mine + more, value * mine + less_dots * other)
            weight_scr[2 * pair + side] = weight.astype(BF16)
            score_scr[2 * pair + side] = (weight * through).astype(BF16)
    for pair in range(heads // 2):
        cq, ck, cv = pair_columns(pair, per_group, width)
        own = slice(2 * pair * HD, 2 * (pair + 1) * HD)
        query, key, grad = qkv_ref[:, cq], qkv_ref[:, ck], grad_ref[:, own]
        even, odd = score_scr[2 * pair], score_scr[2 * pair + 1]
        out_ref[:, cq] = (SCALE * nn(
            jnp.concatenate([even, odd], axis=1),
            jnp.concatenate([key * low, key * high], axis=0),
        )).astype(BF16)
        out_ref[:, ck] = (SCALE * tn(
            jnp.concatenate([even, odd], axis=0),
            jnp.concatenate([query * low, query * high], axis=0),
        )).astype(BF16)
        out_ref[:, cv] = (tn(
            jnp.concatenate([weight_scr[2 * pair], weight_scr[2 * pair + 1]], axis=0),
            jnp.concatenate([grad * low, grad * high], axis=0),
        )).astype(BF16)


def join_back_kernel(offs, near_ref, far_ref, first_ref, out_ref):
    positions, model = first_ref.shape
    heads = model // HD
    per_group = heads // 2
    width = per_group * HD
    groups = far_ref.shape[1]
    out_ref[:, 3 * model :] = first_ref[:, model // 2 :]

    for pair in range(heads // 2):
        even, odd = far_ref[2 * pair], far_ref[2 * pair + 1]
        spread = slot_spread(offs, pair, groups, positions)
        for e, columns in enumerate(pair_columns(pair, per_group, width)):
            part = slice(e * HD, (e + 1) * HD)
            far = nn(spread, beside(even[:, part], odd[:, part]))
            out_ref[:, columns] = (near_ref[:, columns].astype(F32) + far).astype(BF16)


def weight_grad_kernel(
    change, core_ref, left, right_0, right_1, left_got, right_0_got, right_1_got,
    *refs,
):
    kept_ref, sent_ref, left_scr = refs[-3:]
    block = kept_ref.shape[1]
    if len(refs) > 3:
        sent_ref[2 * block :] = refs[0][...]
    step = pl.program_id(0)

    @pl.when((step == 0) | (step == change))
    def _():
        left_scr[0] = left[...].T
        left_scr[1] = left_got[...].T

    product = [
        nn(left_scr[0], right[...]) + nn(left_scr[1], got[...])
        for right, got in ((right_0, right_0_got), (right_1, right_1_got))
    ]
    kept_ref[0] = product[0][:block].astype(BF16)
    sent_ref[block : 2 * block] = product[1][block:].astype(BF16)
    low, high = product[0][block:], product[1][:block]

    @pl.when(core_ref[0] == 0)
    def _():
        kept_ref[1] = high.astype(BF16)
        sent_ref[:block] = low.astype(BF16)

    @pl.when(core_ref[0] != 0)
    def _():
        kept_ref[1] = low.astype(BF16)
        sent_ref[:block] = high.astype(BF16)


def input_grad_kernel(
    core_ref, x_ref, pack_ref, resid_ref, gain_ref, second_ref, place_ref, w0, w1, w2, w3, w4, w5, w6, w7,
    grad_ref, gain_grad, weights, sems,
):
    span = weights.shape[2]
    copies = stream_copies((w0, w1, w2, w3, w4, w5, w6, w7), slice(None), weights, sems, core_ref[0])
    start_all(copies)
    normal, inverse = row_norm(x_ref[...].astype(F32))
    wait_all(copies)
    grad_first = nt(pack_ref[:, :span], weights[0]) + nt(pack_ref[:, span : 2 * span], weights[1])
    first = jnp.sum(grad_first * normal, axis=0, keepdims=True)
    parts = three_parts(jnp.concatenate([first, second_ref[...]] + [jnp.zeros_like(first)] * 6))
    gain_grad[...] = sum(nt(part, place_ref[...]) for part in parts)
    grad = resid_ref[...] + row_norm_back(grad_first, normal, inverse, gain_ref[...])
    grad_ref[...] = nt(grad.astype(BF16), place_ref[...]).astype(BF16)


def finish_kernel(
    core_ref, kept_ref, got_ref, attend_ref, merge_ref, expand_ref, reduce_ref, gain_ref
):
    rows = attend_ref.shape[1] // 2
    width, hidden = merge_ref.shape[1], expand_ref.shape[1]
    gain_ref[...] = kept_ref[rows:, : 3 * width] + got_ref[rows:, : 3 * width]

    def place_halves(first, second):
        for half, source in enumerate((first, second)):
            here = slice(half * rows, (half + 1) * rows)
            for e in range(3):
                attend_ref[e, here] = source[:rows, e * width : (e + 1) * width]
            start = 3 * width
            expand_ref[here] = source[:rows, start : start + hidden]
            merge_ref[here] = source[:rows, start + hidden : start + hidden + width]
            reduce_ref[here] = source[:rows, start + hidden + width :]

    @pl.when(core_ref[0] == 0)
    def _():
        place_halves(kept_ref, got_ref)

    @pl.when(core_ref[0] != 0)
    def _():
        place_halves(got_ref, kept_ref)


def whole(*shape):
    return pl.BlockSpec(shape, lambda *_: tuple(0 for _ in shape))


def sds(shape, dtype):
    return jax.ShapeDtypeStruct(shape, dtype)


def call(
    kernel, grid, in_specs, out_specs, out_shape, scratch=(), earlier=(), cost=5
):
    def body(*refs):
        kernel(*refs[len(earlier) :])

    return partial(
        pl.pallas_call(
            body,
            grid=grid,
            in_specs=[ANY] * len(earlier) + in_specs,
            out_specs=out_specs,
            out_shape=out_shape,
            scratch_shapes=list(scratch),
            compiler_params=pltpu.CompilerParams(
                dimension_semantics=("arbitrary",) * len(grid), vmem_limit_bytes=VMEM_LIMIT
            ),
            cost_estimate=pl.CostEstimate(
                flops=cost * 1_150_000_000, bytes_accessed=0, transcendentals=0
            ),
        ),
        *earlier,
    )


def per_device(
    inputs,
    attend_weight,
    merge_weight,
    expand_weight,
    reduce_weight,
    gain_first,
    gain_heads,
    gain_second,
    gain_hidden,
    cotangent,
    lengths,
    local_span,
    dilation,
):
    seq_size, head_size = lax.axis_size("seq"), lax.axis_size("head")
    row_count, positions, model = inputs.shape
    rows = row_count // head_size
    tokens = rows * positions
    shard_rows, width = attend_weight.shape[1:]
    heads = width * head_size // HD
    group_heads = heads // head_size
    hidden_here = expand_weight.shape[1]
    hidden_width = hidden_here * head_size
    quarter = model // 4
    groups = positions // DILATION_SMALL
    pairs = rows * heads
    owned = -(-pairs // seq_size)
    padded = owned * seq_size
    seq_index, head_index = lax.axis_index("seq"), lax.axis_index("head")
    core = seq_index & 1
    core_ref = core.reshape(1)

    attend_shard = gather_core(jnp.concatenate(list(attend_weight), axis=1))
    attend_far = jnp.concatenate(gather_far(attend_shard))
    other_shard = jnp.concatenate([expand_weight, merge_weight.T, reduce_weight.T], axis=1)
    other_shard = gather_core(after(other_shard, attend_shard))
    third = other_shard.shape[1] // 3
    other_shards = [
        gate(other_shard[:, i * third : (i + 1) * third], attend_far) for i in range(3)
    ]
    attend_got = exchange_near(attend_far, 0)
    attend_more = exchange_near(attend_far, 1)
    other_pieces = [gather_far(other_shards[0])]
    attend_last = exchange_near(attend_got, 1)
    other_pieces.append(gather_far(gate(other_shards[1], attend_got)))
    other_far = [jnp.concatenate(pieces) for pieces in other_pieces]
    other_got = [exchange_near(other_far[0], 0)]
    attend_last = gate(attend_last, other_got[0])
    other_pieces.append(gather_far(gate(other_shards[2], attend_last)))
    attend_all = (attend_far, attend_got, attend_more, attend_last)
    attend_all = attend_all + tuple(exchange(piece, 1, 0) for piece in attend_all)
    both_gains = jnp.concatenate([gain_heads, gain_hidden])
    partner_gains = exchange(both_gains.reshape(-1, 128), 0, 1).reshape(-1)
    gain_heads_all = jnp.concatenate([gain_heads, partner_gains[:width]])[None]
    gain_hidden_all = jnp.concatenate([gain_hidden, partner_gains[width:]])[None]

    half_rows = shard_rows // 2
    part, near, far, beside, inside = jnp.meshgrid(
        *[jnp.arange(n) for n in (2, 2, seq_size // 4, 2, half_rows)], indexing="ij"
    )
    shard_of = seq_index ^ (4 * far + 2 * near + (beside ^ part))
    feature_of = (shard_of * shard_rows + (core ^ part) * half_rows + inside).reshape(-1)
    feature_of = gate(feature_of, attend_far)

    row_start = head_index * rows
    lengths, local_span, dilation = gate(
        jnp.stack([lengths, local_span, dilation]), attend_far
    )

    def own_rows(tensor):
        return lax.dynamic_slice_in_dim(tensor, row_start, rows, axis=0)

    scalars = jnp.concatenate([own_rows(lengths), (seq_index * positions).reshape(1)])
    both_rows_gains = jnp.pad(jnp.stack([gain_first, gain_second]), ((0, 6), (0, 0)))
    own_block = pl.BlockSpec((rows, positions, model), lambda i, head: (head[0], 0, 0))

    def fixed(*shape):
        return pl.BlockSpec(shape, lambda i, head: tuple(0 for _ in shape))

    place, x_own, seed, own_gains = pl.pallas_call(
        prepare_kernel,
        grid_spec=pltpu.PrefetchScalarGridSpec(
            num_scalar_prefetch=1,
            grid=(1,),
            in_specs=[SMEM, fixed(1, model), fixed(8, model), own_block, own_block],
            out_specs=[
                fixed(model, model), fixed(tokens, model), fixed(tokens, model), fixed(8, model)
            ],
        ),
        out_shape=[
            sds((model, model), BF16), sds((tokens, model), BF16), sds((tokens, model), BF16),
            sds((8, model), F32),
        ],
        compiler_params=pltpu.CompilerParams(vmem_limit_bytes=VMEM_LIMIT),
        cost_estimate=pl.CostEstimate(flops=0, bytes_accessed=0, transcendentals=0),
    )(
        head_index.reshape(1), scalars, feature_of[None], both_rows_gains, inputs, cotangent
    )
    gain_one, gain_two = own_gains[:1], own_gains[1:2]
    places = jnp.arange(positions)
    span_block = places[None, :] // own_rows(local_span)[:, None]
    within = (span_block[:, :, None] == span_block[:, None, :]) & (
        places[None, :] <= places[:, None]
    )
    bias = jnp.where(within, 0.0, MASKED_SCORE).astype(F32)

    local_head = jnp.arange(heads)
    head_ids = (head_index ^ (local_head // group_heads)) * group_heads + local_head % group_heads
    offsets = gate((head_ids % DILATION_SMALL).astype(jnp.int32), attend_far)
    pair_ids = jnp.minimum(seq_index * owned + jnp.arange(owned), pairs - 1)
    pair_rate = own_rows(dilation)[pair_ids // heads]
    pair_head = head_ids[pair_ids % heads]
    parity = jnp.where(
        pair_rate == DILATION_SMALL, 0, 1 + (pair_head % pair_rate) // DILATION_SMALL
    ).astype(jnp.int32)

    model_spec, model_shape = whole(tokens, model), (tokens, model)
    attend_scratch = pltpu.VMEM((2, model, 3 * width), BF16)

    def by_row(size):
        return pl.BlockSpec((positions, size), lambda r: (r, 0))

    def of_row(size):
        return pl.BlockSpec((heads, groups, size), lambda r: (r, 0, 0))

    model_row, qkv_row = by_row(model), by_row(3 * model)
    bias_row = pl.BlockSpec((1, positions, positions), lambda r: (r, 0, 0))
    first_in, qkv, slots, near_out, log_near = call(
        project_kernel,
        (rows,),
        [SMEM, SMEM, model_spec, bias_row, whole(1, model)] + [ANY] * 8,
        [model_row, qkv_row, of_row(3 * HD), model_row, model_row],
        [
            sds(model_shape, BF16),
            sds((tokens, 3 * model), BF16),
            sds((padded, groups, 3 * HD), BF16),
            sds(model_shape, F32),
            sds(model_shape, F32),
        ],
        [
            attend_scratch,
            pltpu.VMEM((heads // 2, 2 * positions, positions), F32),
            pltpu.VMEM((tokens, model), BF16),
            pltpu.VMEM((tokens, 3 * model), BF16),
            pltpu.SemaphoreType.DMA((8,)),
        ],
        cost=20,
    )(core_ref, offsets, x_own, bias, gain_one, *attend_all)
    other_held = [jnp.concatenate([other_far[0], other_got[0]])]
    other_more = [exchange_near(other_held[0], 1)]
    other_got.append(exchange_near(other_far[1], 0))
    other_far.append(gate(jnp.concatenate(other_pieces[2]), other_more[0]))
    other_got.append(exchange_near(other_far[2], 0))
    other_held.append(jnp.concatenate([other_far[1], other_got[1]]))
    other_more.append(exchange_near(other_held[1], 1))
    other_core = [(exchange(other_held[0], 1, 0), exchange(other_more[0], 1, 0))]

    def to_owners(value):
        value = value.reshape(seq_size, owned, groups, value.shape[-1])
        return lax.all_to_all(value, "seq", 0, 0, tiled=True)

    def from_owners(value):
        value = lax.all_to_all(value, "seq", 0, 0, tiled=True)
        return value.reshape(padded, groups, value.shape[-1])

    def by_pair(size):
        return pl.BlockSpec((seq_size, 1, groups, size), lambda i: (0, i, 0, 0))

    def owned_shape(size):
        return sds((seq_size, owned, groups, size), BF16)

    slot_count = seq_size * groups
    kv_scratch = pltpu.VMEM((slot_count, 2 * HD), BF16)
    far_qkv = to_owners(slots)
    far_out = call(
        far_kernel,
        (owned,),
        [SMEM, by_pair(3 * HD)],
        by_pair(2 * HD),
        owned_shape(2 * HD),
        [kv_scratch],
        cost=4,
        earlier=(seed, place, gain_two),
    )(parity, far_qkv)
    far_here = from_owners(far_out)
    other_held.append(
        gate(jnp.concatenate([other_far[2], other_got[2]]), far_out)
    )
    other_more.append(exchange_near(other_held[2], 1))
    other_core.append((exchange(other_held[1], 1, 0), exchange(other_more[1], 1, 0)))
    held_core = exchange(other_held[2], 1, 0)

    other_core.append((held_core, exchange(other_more[2], 1, 0)))
    weights_all = [
        piece for i in range(3) for piece in (other_held[i], other_more[i], *other_core[i])
    ]
    hidden_pack = (tokens, hidden_width + model // 2)
    pre_pack = (tokens, hidden_width + 2 * model)
    low_scratch = pltpu.VMEM(model_shape, BF16)
    full_scratch = pltpu.VMEM(model_shape, F32)
    hidden_scratch = pltpu.VMEM((tokens, hidden_width), F32)
    weight_scratch = pltpu.VMEM((2, model, hidden_here), BF16)
    (
        block_mine, hidden_in, grad_pre, lefts, grad_resid, grad_att, stats, grad_slots,
        grad_heads, grad_second, grad_hidden,
    ) = call(
        hidden_kernel,
        (),
        [SMEM, SMEM, whole(1, model), whole(1, model), whole(1, hidden_width),
         whole(padded, groups, 2 * HD)] + [ANY] * 17,
        [
            model_spec, ANY, ANY, model_spec, model_spec, model_spec, model_spec,
            whole(padded, groups, 2 * HD), whole(1, model), whole(1, model),
            whole(1, hidden_width),
        ],
        [
            sds(model_shape, BF16), sds(hidden_pack, BF16), sds(pre_pack, BF16),
            sds(model_shape, BF16), sds(model_shape, F32), sds(model_shape, BF16),
            sds(model_shape, BF16), sds((padded, groups, 2 * HD), BF16), sds((1, model), F32),
            sds((1, model), F32), sds((1, hidden_width), F32),
        ],
        [
            low_scratch, full_scratch, full_scratch, low_scratch,
            pltpu.VMEM((model, model), BF16), pltpu.VMEM((2, model, width), BF16),
            weight_scratch, weight_scratch, hidden_scratch, hidden_scratch, hidden_scratch,
            pltpu.VMEM(hidden_pack, BF16), pltpu.VMEM(pre_pack, BF16),
            pltpu.VMEM((heads, positions, 2 * HD), F32), pltpu.SemaphoreType.DMA((5, 8)),
            pltpu.SemaphoreType.DMA((5,)), pltpu.SemaphoreType.DMA((2 * HIDDEN_BLOCKS + 2,)),
        ],
        cost=8,
    )(
        core_ref, offsets, gain_heads_all, gain_two, gain_hidden_all, far_here, near_out,
        log_near, x_own, seed, place, *weights_all,
    )

    def weight_grad(
        size, left, left_at, right, right_at, left_got_at, earlier=(), change=0, extra=None
    ):
        got = exchange(right, 1, 0)

        def spec(at):
            return pl.BlockSpec((tokens, width), lambda j: (0, at(j)))

        def rights():
            return [spec(lambda j, x=x: right_at(x, j)) for x in range(2)]

        sent_rows = 2 * quarter
        extras = []
        if extra is not None:
            sent_rows += GAIN_ROWS
            extras = [extra]
        return call(
            partial(weight_grad_kernel, change),
            (size // width,),
            [SMEM, spec(left_at)] + rights() + [spec(left_got_at)] + rights()
            + [pl.BlockSpec((GAIN_ROWS, width), lambda j: (0, j))] * len(extras),
            [
                pl.BlockSpec((2, quarter, width), lambda j: (0, 0, j)),
                pl.BlockSpec((sent_rows, width), lambda j: (0, j)),
            ],
            [sds((2, quarter, size), BF16), sds((sent_rows, size), BF16)],
            [pltpu.VMEM((2, model // 2, tokens), BF16)],
            earlier=earlier,
            cost=7,
        )(core_ref, left, right, right, got, got, got, *extras)

    per_half = hidden_here // width
    hidden_blocks = hidden_width // width

    def both_rows(mine, earlier=None):
        mine = mine.reshape(rows, positions, model)
        other = exchange(mine, 0, 1)
        if earlier is not None:
            other = gate(other, earlier)
        both = jnp.concatenate([other, other])
        return lax.dynamic_update_slice_in_dim(both, mine, row_start, axis=0)

    far_grads = to_owners(grad_slots)
    near_grad = call(
        near_back_kernel,
        (rows,),
        [bias_row, qkv_row, model_row, model_row],
        qkv_row,
        sds((tokens, 3 * model), BF16),
        [pltpu.VMEM((heads, positions, positions), BF16)] * 2,
        cost=60,
    )(bias, qkv, grad_att, stats)
    reduce_kept, reduce_sent = weight_grad(
        hidden_here, seed, lambda j: 0, hidden_in, lambda x, j: x * per_half + j,
        lambda j: hidden_blocks, earlier=(near_grad,),
    )
    far_back = call(
        far_back_kernel,
        (owned,),
        [SMEM, by_pair(3 * HD), by_pair(2 * HD)],
        by_pair(3 * HD),
        owned_shape(3 * HD),
        [kv_scratch, pltpu.VMEM((slot_count, 2 * HD), F32)],
        earlier=(reduce_sent,),
        cost=0,
    )(parity, far_qkv, far_grads)
    expand_kept, expand_sent = weight_grad(
        hidden_here + width, lefts, lambda j: jnp.where(j < per_half, 0, 1), grad_pre,
        lambda x, j: jnp.where(j < per_half, x * per_half + j, hidden_blocks + x),
        lambda j: hidden_blocks + 2 + jnp.where(j < per_half, 0, 1),
        earlier=(far_back,), change=per_half,
    )
    back_here = from_owners(far_back)
    block_out = both_rows(block_mine, expand_sent)
    reduce_kept, reduce_sent, _ = scatter_first(reduce_kept, reduce_sent)
    grad_pack_shape = (tokens, 3 * model + model // 2)
    grad_pack = call(
        join_back_kernel,
        (rows,),
        [SMEM, qkv_row, of_row(3 * HD), model_row],
        by_row(grad_pack_shape[1]),
        sds(grad_pack_shape, BF16),
        earlier=(reduce_sent, block_out),
        cost=1,
    )(offsets, near_grad, back_here, first_in)
    grad_mine, grad_shared = call(
        input_grad_kernel,
        (),
        [
            SMEM, model_spec, whole(*grad_pack_shape), model_spec, whole(1, model),
            whole(1, model), whole(model, model),
        ]
        + [ANY] * 8,
        [model_spec, whole(8, model)],
        [sds(model_shape, BF16), sds((8, model), F32)],
        [attend_scratch, pltpu.SemaphoreType.DMA((8,))],
        cost=3,
    )(core_ref, x_own, grad_pack, grad_resid, gain_one, grad_second, place, *attend_all)

    expand_kept, expand_sent, _ = scatter_first(
        gate(expand_kept, grad_mine), expand_sent
    )
    def by_head(grad):
        size = grad.shape[1] // 2
        return jnp.where(head_index == 0, grad[0], jnp.roll(grad[0], size))

    grad_shared = gate(grad_shared, expand_sent)
    gains = jnp.concatenate(
        [
            grad_shared[0], grad_shared[1], by_head(grad_heads), by_head(grad_hidden),
        ]
    )
    gain_rows = -(-gains.shape[0] // (3 * width))
    gains = jnp.pad(gains, (0, gain_rows * 3 * width - gains.shape[0])).reshape(gain_rows, -1)
    gain_sent = to_rows(gains)
    reduce_kept, reduce_sent, _ = scatter_second(reduce_kept, reduce_sent)
    attend_kept, attend_sent = weight_grad(
        3 * width, first_in, lambda j: 0, grad_pack, lambda x, j: 3 * x + j, lambda j: 6,
        earlier=(grad_mine, *reduce_sent), extra=gain_sent,
    )
    attend_kept, attend_sent, attend_near = scatter_first(attend_kept, attend_sent)
    gains = from_rows(gain_sent, gain_rows) + from_rows(attend_near[2 * quarter :], gain_rows)
    gain_sent = to_rows(gains)
    reduce_total = scatter_far(reduce_kept, reduce_sent)
    expand_kept, expand_sent, _ = scatter_second(expand_kept, expand_sent)
    attend_sent = after(after(attend_sent, reduce_total), expand_sent[0])
    attend_kept, attend_sent, attend_got = scatter_second(
        attend_kept, jnp.concatenate([attend_sent, gain_sent])
    )
    gains = from_rows(gain_sent, gain_rows) + from_rows(attend_got[quarter:], gain_rows)
    stages = far_stages(seq_size)
    for stage in reversed(range(len(stages))):
        unit, radix = stages[stage]
        gain_sent = to_rows(gains)
        everyone = [from_rows(gain_sent, gain_rows)]
        rows_sent = attend_sent[0].shape[0]
        for i, piece in enumerate(attend_sent):
            got = exchange(jnp.concatenate([piece, gain_sent]), unit * (i + 1), 0)
            attend_kept = attend_kept + got[:rows_sent].astype(F32)
            everyone.append(from_rows(got[rows_sent:], gain_rows))
        while len(everyone) > 1:
            everyone = [one + two for one, two in zip(everyone[::2], everyone[1::2])]
        gains = everyone[0]
        if stage:
            held = attend_kept.reshape(stages[stage - 1][1], -1, 3 * width)
            attend_kept, attend_sent = held[0], [piece.astype(BF16) for piece in held[1:]]
    grad_inputs = both_rows(gate(grad_mine, attend_got))
    expand_total = scatter_far(gate(expand_kept, attend_got), expand_sent)
    totals = jnp.concatenate([attend_kept, expand_total, reduce_total], axis=1)
    gains = jnp.pad(gains, ((0, 8 - gain_rows), (0, totals.shape[1] - gains.shape[1])))
    last_kept = jnp.concatenate([totals[:half_rows], gains])
    last_got = exchange(jnp.concatenate([totals[half_rows:], gains]), 1, 0)
    last_shape = last_kept.shape
    grad_attend, grad_merge, grad_expand, grad_reduce, gains = call(
        finish_kernel,
        (),
        [SMEM, whole(*last_shape), whole(*last_shape)],
        [
            whole(3, shard_rows, width), whole(shard_rows, width), whole(shard_rows, hidden_here),
            whole(shard_rows, hidden_here), whole(8, 3 * width),
        ],
        [
            sds((3, shard_rows, width), F32), sds((shard_rows, width), F32),
            sds((shard_rows, hidden_here), F32), sds((shard_rows, hidden_here), F32),
            sds((8, 3 * width), F32),
        ],
        cost=1,
    )(core_ref, last_kept, last_got)
    gains = gains[:gain_rows].reshape(-1)

    def own_half(start, size):
        return jnp.where(
            head_index == 0, gains[start : start + size], gains[start + size : start + 2 * size]
        )

    return (
        block_out,
        grad_inputs,
        grad_attend,
        grad_merge.T,
        grad_expand,
        grad_reduce.T,
        gains[:model],
        own_half(2 * model, width),
        gains[model : 2 * model],
        own_half(3 * model, hidden_here),
    )


def solution(mesh):
    placed = (
        P(None, "seq", None),
        P(None, "seq", "head"),
        P("head", "seq"),
        P("seq", "head"),
        P("head", "seq"),
        P(),
        P("head"),
        P(),
        P("head"),
        P(None, "seq", None),
        P(),
        P(),
        P(),
    )
    return jax.shard_map(
        per_device,
        mesh=mesh,
        in_specs=placed,
        out_specs=(
            P(None, "seq", None),
            P(None, "seq", None),
            P(None, "seq", "head"),
            P("head", "seq"),
            P("seq", "head"),
            P("head", "seq"),
            P(),
            P("head"),
            P(),
            P("head"),
        ),
        check_vma=False,
    )
```

```python
from functools import partial

import jax
import jax.numpy as jnp
from jax import lax
from jax.experimental import pallas as pl
from jax.experimental.pallas import tpu as pltpu
from jax.sharding import PartitionSpec as P

HD = 64
DILATION_SMALL = 8
NORM_EPSILON = 1e-05
MASKED_SCORE = -1e30
SCALE = HD ** (-0.5)
F32 = jnp.float32
BF16 = jnp.bfloat16
ANY = pl.BlockSpec(memory_space=pl.ANY)
SMEM = pl.BlockSpec(memory_space=pltpu.SMEM)
VMEM_LIMIT = 56 * 1024 * 1024


def nn(left, right):
    return lax.dot_general(left, right, (((1,), (0,)), ((), ())), preferred_element_type=F32)


def nt(left, right):
    return lax.dot_general(left, right, (((1,), (1,)), ((), ())), preferred_element_type=F32)


def tn(left, right):
    return lax.dot_general(left, right, (((0,), (0,)), ((), ())), preferred_element_type=F32)


def row_norm(values):
    center = jnp.mean(values, axis=-1, keepdims=True)
    spread = jnp.mean(values * values, axis=-1, keepdims=True) - center * center
    inverse = lax.rsqrt(spread + NORM_EPSILON)
    return (values - center) * inverse, inverse


def row_norm_back(incoming, normal, inverse, gain_row):
    scaled = incoming * gain_row
    first_mean = jnp.mean(scaled, axis=-1, keepdims=True)
    second_mean = jnp.mean(scaled * normal, axis=-1, keepdims=True)
    return inverse * (scaled - first_mean - normal * second_mean)


def three_parts(values):
    high = values.astype(BF16)
    rest = values - high.astype(F32)
    middle = rest.astype(BF16)
    low = (rest - middle.astype(F32)).astype(BF16)
    return high, middle, low


def gelu_parts(values):
    expo = jnp.exp(values * values * -0.5)
    term = 1.0 / (1.0 + (0.3275911 * 0.7071067811865476) * jnp.abs(values))
    poly = term * (
        0.254829592
        + term
        * (-0.284496736 + term * (1.421413741 + term * (-1.453152027 + term * 1.061405429)))
    )
    tail = 0.5 * poly * expo
    phi = jnp.where(values >= 0.0, 1.0 - tail, tail)
    return values * phi, phi + values * expo * 0.3989422804014327


def iota(shape, dim):
    return lax.broadcasted_iota(jnp.int32, shape, dim)


def permute(value, target):
    seq_size, head_size = lax.axis_size("seq"), lax.axis_size("head")
    pairs = []
    for s in range(seq_size):
        for h in range(head_size):
            to_seq, to_head = target(s, h)
            pairs.append((s * head_size + h, to_seq * head_size + to_head))
    return lax.ppermute(value, ("seq", "head"), pairs)


def exchange(value, seq_mask, head_mask):
    return permute(value, lambda s, h: (s ^ seq_mask, h ^ head_mask))


def exchange_near(value, turn):
    return permute(value, lambda s, h: (s, h ^ 1) if (s & 1) == turn else (s ^ 2, h))


def far_stages(seq_size):
    unit, left, stages = 4, seq_size // 4, []
    while left > 1:
        radix = 4 if left % 4 == 0 else 2
        stages.append((unit, radix))
        unit, left = unit * radix, left // radix
    return stages


def gate(value, *earlier):
    def kernel(*refs):
        pass

    return pl.pallas_call(
        kernel,
        in_specs=[ANY] * (len(earlier) + 1),
        out_specs=ANY,
        out_shape=jax.ShapeDtypeStruct(value.shape, value.dtype),
        input_output_aliases={len(earlier): 0},
        cost_estimate=pl.CostEstimate(flops=0, bytes_accessed=0, transcendentals=0),
    )(*earlier, value)


def after(value, earlier):
    zero = earlier[(0,) * earlier.ndim].astype(F32) * 0.0
    return value + zero.astype(value.dtype)


def gather_core(shard):
    core = lax.axis_index("seq") & 1
    half = shard.shape[0] // 2
    kept = lax.dynamic_slice_in_dim(shard, core * half, half)
    sent = lax.dynamic_slice_in_dim(shard, (1 - core) * half, half)
    return jnp.concatenate([kept, exchange(sent, 1, 0)])


def gather_far(held):
    stages = far_stages(lax.axis_size("seq"))
    for unit, radix in stages:
        pieces = [held] + [exchange(held, unit * i, 0) for i in range(1, radix)]
        held = jnp.concatenate(pieces) if (unit, radix) != stages[-1] else None
    return pieces


def scatter_first(kept, sent):
    got = exchange_near(sent, 1)
    block = kept.shape[1]

    def total(index):
        return kept[index].astype(F32) + got[index * block : (index + 1) * block].astype(F32)

    return total(0), total(1).astype(BF16), got


def scatter_second(kept, sent):
    got = exchange_near(sent, 0)
    total = kept + got[: kept.shape[0]].astype(F32)
    unit, radix = far_stages(lax.axis_size("seq"))[-1]
    total = total.reshape(radix, -1, total.shape[-1])
    return total[0], [total[i].astype(BF16) for i in range(1, radix)], got


def scatter_far(kept, sent):
    stages = far_stages(lax.axis_size("seq"))
    for stage in reversed(range(len(stages))):
        unit, radix = stages[stage]
        for i, piece in enumerate(sent):
            kept = kept + exchange(piece, unit * (i + 1), 0).astype(F32)
        if stage:
            held = kept.reshape(stages[stage - 1][1], -1, kept.shape[-1])
            kept, sent = held[0], [piece.astype(BF16) for piece in held[1:]]
    return kept


def to_rows(sums):
    high = lax.reduce_precision(sums, 8, 7)
    low = sums - high
    spare = jnp.zeros((GAIN_ROWS - 2 * sums.shape[0], sums.shape[1]), F32)
    return jnp.concatenate([high, low, spare]).astype(BF16)


def from_rows(rows, count):
    return rows[:count].astype(F32) + rows[count : 2 * count].astype(F32)


GAIN_ROWS = 16


def stream_copies(pieces, columns, target, sems, core):
    block = target.shape[1] // 4
    blocks = [
        piece.at[pl.ds(start, block), columns]
        for piece in pieces
        for start in range(0, piece.shape[0], block)
    ]
    copies = []
    for index, source in enumerate(blocks):
        part, second, first = index // 4, index // 2 % 2, index % 2
        straight = (core ^ part) == 0
        x = jnp.where(straight, first, second)
        y = jnp.where(straight, second, first)
        row = pl.multiple_of((2 * part + y) * block, block)
        copies.append(
            pltpu.make_async_copy(source, target.at[x, pl.ds(row, block)], sems.at[index])
        )
    return copies


def start_all(copies):
    for copy in copies:
        copy.start()


def wait_all(copies):
    for copy in copies:
        copy.wait()


def pair_columns(pair, per_group, width):
    group, inside = divmod(2 * pair, per_group)
    start = group * 3 * width + inside * HD
    return [slice(start + e * width, start + e * width + 2 * HD) for e in range(3)]


def slot_select(offset, groups, positions):
    shape = (groups, positions)
    return (iota(shape, 1) == DILATION_SMALL * iota(shape, 0) + offset).astype(BF16)


def slot_spread(offs, pair, groups, positions, times=1):
    shape = (positions, 2 * groups * times)
    slot = iota(shape, 1) & (2 * groups - 1)
    offset = jnp.where(slot < groups, offs[2 * pair], offs[2 * pair + 1])
    return (iota(shape, 0) == DILATION_SMALL * (slot & (groups - 1)) + offset).astype(BF16)


def side_masks():
    lane = iota((1, 2 * HD), 1)
    return (lane < HD).astype(BF16), (lane >= HD).astype(BF16)


def beside(even, odd):
    nothing = jnp.zeros_like(even)
    return jnp.concatenate(
        [jnp.concatenate([even, nothing], axis=1), jnp.concatenate([nothing, odd], axis=1)], axis=0
    )


def prepare_kernel(
    head_ref, scalars, feature_ref, gains_ref, x_ref, seed_ref, place_out, x_out, seed_out, gains_out
):
    rows, positions, model = x_ref.shape
    feature = feature_ref[...]
    place = (iota((model, model), 0) == feature).astype(BF16)
    place_out[...] = place
    at = scalars[rows] + iota((positions, model), 0)
    for r in range(rows):
        here = slice(r * positions, (r + 1) * positions)
        x_out[here] = nn(x_ref[r], place).astype(BF16)
        seed = jnp.where(at < scalars[r], seed_ref[r].astype(F32), 0.0).astype(BF16)
        seed_out[here] = nn(seed, place).astype(BF16)
    gains_out[...] = sum(nn(part, place) for part in three_parts(gains_ref[...]))


def project_kernel(
    core_ref, offs, x_ref, bias_ref, gain_ref, w0, w1, w2, w3, w4, w5, w6, w7,
    first_ref, qkv_ref, slot_ref, out_ref, lse_ref, weights, score_scr, first_scr, qkv_scr,
    sems,
):
    _, positions = bias_ref.shape[:2]
    model = x_ref.shape[1]
    width = weights.shape[2] // 3
    heads = model // HD
    per_group = heads // 2
    groups = positions // DILATION_SMALL
    r = pl.program_id(0)

    @pl.when(r == 0)
    def _():
        pieces = (w0, w1, w2, w3, w4, w5, w6, w7)
        copies = stream_copies(pieces, slice(None), weights, sems, core_ref[0])
        start_all(copies)
        normal, _ = row_norm(x_ref[...].astype(F32))
        first_scr[...] = (normal * gain_ref[...]).astype(BF16)
        wait_all(copies)
        for hh in range(2):
            columns = slice(hh * 3 * width, (hh + 1) * 3 * width)
            qkv_scr[:, columns] = nn(first_scr[...], weights[hh]).astype(BF16)

    low, high = side_masks()
    side = iota((positions, 2 * HD), 1) < HD
    here = pl.ds(pl.multiple_of(r * positions, positions), positions)
    first_ref[...] = first_scr[here]
    qkv_ref[...] = qkv_scr[here]
    bias = bias_ref[0]
    bias = jnp.concatenate([bias, bias], axis=0)
    for pair in range(heads // 2):
        cq, ck, cv = pair_columns(pair, per_group, width)
        query, key = qkv_ref[:, cq], qkv_ref[:, ck]
        both = jnp.concatenate([query * low, query * high], axis=0)
        score_scr[pair] = nt(both, key) * SCALE + bias
        every = jnp.concatenate([query, key, qkv_ref[:, cv]], axis=1)
        for inside in range(2):
            chosen = slot_select(offs[2 * pair + inside], groups, positions)
            slots = nn(chosen, every).astype(BF16)
            starts = [2 * HD * e + HD * inside for e in range(3)]
            slot_ref[2 * pair + inside] = jnp.concatenate(
                [slots[:, start : start + HD] for start in starts], axis=1
            )
    for pair in range(heads // 2):
        value = qkv_ref[:, pair_columns(pair, per_group, width)[2]]
        score = score_scr[pair]
        peak = jnp.max(score, axis=-1, keepdims=True)
        expo = jnp.exp(score - peak)
        total = jnp.sum(expo, axis=-1, keepdims=True)
        expo = expo.astype(BF16)
        out = nn(
            jnp.concatenate([expo[:positions], expo[positions:]], axis=1),
            jnp.concatenate([value * low, value * high], axis=0),
        )
        columns = slice(2 * pair * HD, 2 * (pair + 1) * HD)
        log, scale = peak + jnp.log(total), 1.0 / total
        out_ref[:, columns] = out * jnp.where(side, scale[:positions], scale[positions:])
        lse_ref[:, columns] = jnp.where(side, log[:positions], log[positions:])


def far_masks(parity, row_start, row_count, slots):
    row = row_start + iota((row_count, slots), 0)
    column = iota((row_count, slots), 1)
    live_row = (parity == 0) | ((row & 1) == parity - 1)
    live_column = (parity == 0) | ((column & 1) == parity - 1)
    return (column <= row) & live_column, live_row


def for_blocks(count, body):
    if count == 1:
        body(0)
    else:
        lax.fori_loop(0, count, lambda b, carry: (body(b), carry)[1], 0)


def far_kernel(parity_ref, qkv_ref, out_ref, kv_scr):
    devices, _, groups, _ = qkv_ref.shape
    slots = devices * groups
    block = min(slots, 256)
    per_block = block // groups
    parity = parity_ref[pl.program_id(0)]
    kv_scr[...] = qkv_ref[:, 0].reshape(slots, 3 * HD)[:, HD:]

    def body(index):
        piece = pl.ds(index * per_block, per_block)
        query = qkv_ref[piece, 0].reshape(block, 3 * HD)[:, :HD]
        key, value = kv_scr[:, :HD], kv_scr[:, HD:]
        allowed, live = far_masks(parity, index * block, block, slots)
        score = jnp.where(allowed, nt(query, key) * SCALE, MASKED_SCORE)
        peak = jnp.max(score, axis=-1, keepdims=True)
        expo = jnp.exp(score - peak)
        total = jnp.sum(expo, axis=-1, keepdims=True)
        out = nn(expo.astype(BF16), value) / total
        log = jnp.where(live[:, :1], peak + jnp.log(total), MASKED_SCORE)
        high, middle, low = three_parts(log)
        lane = iota((block, 2 * HD), 1)
        tile = jnp.concatenate([out, out], axis=1)
        tile = jnp.where(lane == HD, high.astype(F32), tile)
        tile = jnp.where(lane == HD + 1, middle.astype(F32), tile)
        tile = jnp.where(lane == HD + 2, low.astype(F32), tile)
        out_ref[piece, 0] = tile.astype(BF16).reshape(per_block, groups, 2 * HD)

    for_blocks(slots // block, body)


HIDDEN_BLOCKS = 4


def hidden_kernel(
    core_ref, offs, gain_heads, gain_second, gain_hidden, far_ref, near_any, log_any, x_any,
    seed_any, place_any, a0, a1, a2, a3, b0, b1, b2, b3, c0, c1, c2, c3,
    block_ref, hidden_out, pre_out, left_ref, resid_ref, grad_ref, stats_ref, slot_ref,
    grad_heads, grad_second, grad_hidden,
    x_ref, att_ref, lse_ref, seed_ref, place_ref, merge_w, expand_w, reduce_w,
    second_ref, act_scr, slope_scr, grad_scr, hidden_ref, pre_ref, tile_scr, sems, in_sems, out_sems,
):
    tokens, model = x_ref.shape
    hidden_here = expand_w.shape[2]
    half_model = model // 2
    width = merge_w.shape[2]
    heads = model // HD
    groups = slot_ref.shape[1]
    positions = groups * DILATION_SMALL
    hidden_width = 2 * hidden_here
    block = hidden_width // HIDDEN_BLOCKS
    core = core_ref[0]
    chunks = ((a0, a1, a2, a3), (b0, b1, b2, b3), (c0, c1, c2, c3))
    third = a0.shape[1]

    def chunk_copies(target, first_column, size, at):
        copies = []
        for chunk, pieces in enumerate(chunks):
            low = max(first_column, chunk * third)
            high = min(first_column + size, (chunk + 1) * third)
            if low < high:
                copies += stream_copies(
                    pieces,
                    pl.ds(low - chunk * third, high - low),
                    target.at[:, :, pl.ds(low - first_column, high - low)],
                    sems.at[at + len(copies) // 8],
                    core,
                )
        return copies

    expand_copies = chunk_copies(expand_w, 0, hidden_here, 0)
    merge_copies = chunk_copies(merge_w, hidden_here, width, 2)
    reduce_copies = chunk_copies(reduce_w, hidden_here + width, hidden_here, 3)
    inputs = [
        pltpu.make_async_copy(source, target, in_sems.at[i])
        for i, (source, target) in enumerate(
            (
                (near_any, att_ref), (log_any, lse_ref), (x_any, x_ref), (seed_any, seed_ref),
                (place_any, place_ref),
            )
        )
    ]
    start_all(inputs[:3])
    start_all(merge_copies)
    start_all(expand_copies)
    start_all(inputs[3:4])
    start_all(reduce_copies)
    start_all(inputs[4:])

    def columns_of(index):
        return pl.ds(pl.multiple_of(index * block, block), block)

    def weight_block(weights, index):
        per_group = hidden_here // block
        return weights[lax.div(index, per_group), :, columns_of(lax.rem(index, per_group))]

    def send(source, target, index, columns):
        return pltpu.make_async_copy(
            source.at[:, columns], target.at[:, columns], out_sems.at[index]
        )

    nothing = jnp.zeros((tokens, 1), F32)
    wait_all(inputs[:3])

    lane = iota((positions, 2 * HD), 1)
    side, inside_lane = lane < HD, lane & (HD - 1)
    place = iota((positions, 2 * HD), 0) & (DILATION_SMALL - 1)

    def join_row(r, carry):
        here = pl.ds(pl.multiple_of(r * positions, positions), positions)
        for pair in range(heads // 2):
            even, odd = far_ref[r * heads + 2 * pair], far_ref[r * heads + 2 * pair + 1]
            spread = slot_spread(offs, pair, groups, positions)
            far_out = nn(spread, beside(even[:, :HD], odd[:, :HD]))
            even, odd = even.astype(F32), odd.astype(F32)
            logs = [
                beside(
                    jnp.broadcast_to(even[:, HD + i : HD + i + 1], (groups, HD)),
                    jnp.broadcast_to(odd[:, HD + i : HD + i + 1], (groups, HD)),
                )
                for i in range(3)
            ]
            log_far = sum(nn(spread, log.astype(BF16)) for log in logs)
            slot = jnp.where(side, offs[2 * pair], offs[2 * pair + 1])
            log_far = jnp.where(place == slot, log_far, MASKED_SCORE)
            columns = slice(2 * pair * HD, 2 * (pair + 1) * HD)
            log_near = lse_ref[here, columns]
            peak = jnp.maximum(log_near, log_far)
            weight_near, weight_far = jnp.exp(log_near - peak), jnp.exp(log_far - peak)
            total = weight_near + weight_far
            lse_ref[here, columns] = pltpu.roll(peak + jnp.log(total), HD, 1)
            att_ref[here, columns] = (
                att_ref[here, columns] * weight_near + far_out * weight_far
            ) / total
        return carry

    lax.fori_loop(0, tokens // positions, join_row, 0)
    normal_heads, _ = row_norm(att_ref[...])
    heads_in = (normal_heads * gain_heads[...]).astype(BF16)
    wait_all(merge_copies)
    merged = [nt(heads_in[:, hh * width : (hh + 1) * width], merge_w[hh]) for hh in range(2)]
    residual = x_ref[...].astype(F32) + (merged[0] + merged[1])
    resid_ref[...] = residual
    normal_two, inverse_two = row_norm(residual)
    second_in = (normal_two * gain_second[...]).astype(BF16)
    second_ref[...] = second_in
    start = hidden_width + model
    pre_ref[:, hidden_width:start] = heads_in
    pre_ref[:, start : start + half_model] = second_in[:, half_model:]
    left_ref[:, :half_model] = second_in[:, :half_model]
    wait_all(expand_copies)

    def expand_step(index, totals):
        columns = columns_of(index)
        act, slope = gelu_parts(nn(second_ref[...], weight_block(expand_w, index)))
        act_scr[:, columns] = act
        slope_scr[:, columns] = slope
        return (
            totals[0] + jnp.sum(act, axis=-1, keepdims=True),
            totals[1] + jnp.sum(act * act, axis=-1, keepdims=True),
        )

    total_one, total_two = lax.fori_loop(0, HIDDEN_BLOCKS, expand_step, (nothing, nothing))
    center = total_one / hidden_width
    inverse = lax.rsqrt(total_two / hidden_width - center * center + NORM_EPSILON)
    wait_all(inputs[3:4])
    hidden_ref[:, hidden_width:] = seed_ref[:, half_model:]
    wait_all(reduce_copies)

    def reduce_step(index, totals):
        columns = columns_of(index)
        normal = (act_scr[:, columns] - center) * inverse
        act_scr[:, columns] = normal
        gain = gain_hidden[:, columns]
        scaled = normal * gain
        hidden_ref[:, columns] = scaled.astype(BF16)
        send(hidden_ref, hidden_out, index, columns).start()
        grad = nn(seed_ref[...], weight_block(reduce_w, index))
        grad_hidden[:, columns] = jnp.sum(grad * normal, axis=0, keepdims=True)
        grad_scr[:, columns] = grad * gain
        return (
            totals[0] + jnp.sum(grad * gain, axis=-1, keepdims=True),
            totals[1] + jnp.sum(grad * scaled, axis=-1, keepdims=True),
        )

    total_one, total_two = lax.fori_loop(0, HIDDEN_BLOCKS, reduce_step, (nothing, nothing))
    seed_columns = slice(hidden_width, hidden_width + half_model)
    send(hidden_ref, hidden_out, HIDDEN_BLOCKS, seed_columns).start()
    mean_one = total_one / hidden_width
    mean_two = total_two / hidden_width

    def pre_step(index, carry):
        columns = columns_of(index)
        grad = inverse * (grad_scr[:, columns] - mean_one - act_scr[:, columns] * mean_two)
        pre_ref[:, columns] = (grad * slope_scr[:, columns]).astype(BF16)
        send(pre_ref, pre_out, HIDDEN_BLOCKS + 1 + index, columns).start()
        return carry

    lax.fori_loop(0, HIDDEN_BLOCKS, pre_step, 0)
    grad_second_in = nt(pre_ref[:, :hidden_here], expand_w[0]) + nt(
        pre_ref[:, hidden_here:hidden_width], expand_w[1]
    )
    normal_two, inverse_two = row_norm(resid_ref[...])
    grad_second[...] = jnp.sum(grad_second_in * normal_two, axis=0, keepdims=True)
    resid = seed_ref[...].astype(F32) + row_norm_back(
        grad_second_in, normal_two, inverse_two, gain_second[...]
    )
    block_out = nt(hidden_ref[:, :hidden_here], reduce_w[0]) + nt(
        hidden_ref[:, hidden_here:hidden_width], reduce_w[1]
    )
    block_out = (resid_ref[...] + block_out).astype(BF16)
    resid_ref[...] = resid
    resid_low = resid.astype(BF16)
    left_ref[:, half_model:] = resid_low[:, :half_model]
    pre_ref[:, start + half_model :] = resid_low[:, half_model:]
    last_columns = slice(hidden_width, hidden_width + 2 * model)
    send(pre_ref, pre_out, 2 * HIDDEN_BLOCKS + 1, last_columns).start()
    grad_heads_in = jnp.concatenate([nn(resid_low, merge_w[hh]) for hh in range(2)], axis=1)
    wait_all(inputs[4:])
    block_ref[...] = nt(block_out, place_ref[...]).astype(BF16)
    normal_heads, inverse_heads = row_norm(att_ref[...])
    grad_heads[...] = jnp.sum(grad_heads_in * normal_heads, axis=0, keepdims=True)
    grad_att = row_norm_back(
        grad_heads_in, normal_heads, inverse_heads, gain_heads[...]
    ).astype(BF16)
    grad_ref[...] = grad_att
    grad_scr[:, :model] = grad_att.astype(F32) * att_ref[...]
    across = (iota((2 * HD, 2 * HD), 0) // HD != iota((2 * HD, 2 * HD), 1) // HD).astype(BF16)
    def for_row(r, carry):
        here = pl.ds(pl.multiple_of(r * positions, positions), positions)
        for pair in range(heads // 2):
            columns = slice(2 * pair * HD, 2 * (pair + 1) * HD)
            top, middle, _ = three_parts(grad_scr[here, columns])
            dots = nn(top, across) + nn(middle, across)
            stats = jnp.zeros((positions, 2 * HD), F32)
            for index, part in enumerate(three_parts(lse_ref[here, columns]) + three_parts(dots)):
                stats = jnp.where(inside_lane == index, part.astype(F32), stats)
            stats_ref[here, columns] = stats.astype(BF16)
            grad = grad_ref[here, columns].astype(F32)
            tile_scr[2 * pair] = jnp.where(side, grad, stats)
            tile_scr[2 * pair + 1] = jnp.where(side, stats, grad)
        for head in range(heads):
            tile = tile_scr[head, pl.ds(offs[head], groups, stride=DILATION_SMALL), :]
            if head % 2:
                tile = jnp.concatenate([tile[:, HD:], tile[:, :HD]], axis=1)
            slot_ref[r * heads + head] = tile.astype(BF16)
        return carry

    lax.fori_loop(0, tokens // positions, for_row, 0)
    for index in range(HIDDEN_BLOCKS):
        columns = slice(index * block, (index + 1) * block)
        send(hidden_ref, hidden_out, index, columns).wait()
        send(pre_ref, pre_out, HIDDEN_BLOCKS + 1 + index, columns).wait()
    send(hidden_ref, hidden_out, HIDDEN_BLOCKS, seed_columns).wait()
    send(pre_ref, pre_out, 2 * HIDDEN_BLOCKS + 1, last_columns).wait()


def far_back_kernel(parity_ref, qkv_ref, grad_ref, out_ref, kv_scr, total_scr):
    devices, _, groups, _ = qkv_ref.shape
    slots = devices * groups
    block = min(slots, 256)
    per_block = block // groups
    parity = parity_ref[pl.program_id(0)]
    kv_scr[...] = qkv_ref[:, 0].reshape(slots, 3 * HD)[:, HD:]
    total_scr[...] = jnp.zeros_like(total_scr)

    def body(index):
        piece = pl.ds(index * per_block, per_block)
        query = qkv_ref[piece, 0].reshape(block, 3 * HD)[:, :HD]
        tile = grad_ref[piece, 0].reshape(block, 2 * HD)
        key, value = kv_scr[:, :HD], kv_scr[:, HD:]
        grad = tile[:, :HD]
        stats = tile[:, HD:].astype(F32)
        log = stats[:, 0:1] + stats[:, 1:2] + stats[:, 2:3]
        dots = stats[:, 3:4] + stats[:, 4:5] + stats[:, 5:6]
        allowed, live = far_masks(parity, index * block, block, slots)
        score = jnp.where(allowed & live, nt(query, key) * SCALE - log, MASKED_SCORE)
        weight = jnp.exp(score)
        grad_score = (weight * (nt(grad, value) - dots)).astype(BF16)
        grad_query = nn(grad_score, key) * SCALE
        total_scr[:, :HD] += tn(grad_score, query) * SCALE
        total_scr[:, HD:] += tn(weight.astype(BF16), grad)
        out_ref[piece, 0, :, :HD] = grad_query.astype(BF16).reshape(per_block, groups, HD)

    for_blocks(slots // block, body)
    out_ref[:, 0, :, HD:] = total_scr[...].astype(BF16).reshape(devices, groups, 2 * HD)


def near_back_kernel(bias_ref, qkv_ref, grad_ref, stats_ref, out_ref, weight_scr, score_scr):
    positions, model = grad_ref.shape
    heads = model // HD
    per_group = heads // 2
    width = per_group * HD
    low, high = side_masks()
    inside = iota((1, 2 * HD), 1) & (HD - 1)
    less_log = jnp.where(inside < 3, -1.0 / SCALE, 0.0).astype(BF16)
    less_dots = jnp.where((inside >= 3) & (inside < 6), -1.0, 0.0).astype(BF16)

    bias = bias_ref[0]
    for pair in range(heads // 2):
        cq, ck, cv = pair_columns(pair, per_group, width)
        own = slice(2 * pair * HD, 2 * (pair + 1) * HD)
        query, key, value = qkv_ref[:, cq], qkv_ref[:, ck], qkv_ref[:, cv]
        grad, stats = grad_ref[:, own], stats_ref[:, own]
        for side, (mine, other) in enumerate(((low, high), (high, low))):
            more = stats * other
            score = nt(query * mine + more, key * mine + less_log * other)
            weight = jnp.exp(score * SCALE + bias)
            through = nt(grad * mine + more, value * mine + less_dots * other)
            weight_scr[2 * pair + side] = weight.astype(BF16)
            score_scr[2 * pair + side] = (weight * through).astype(BF16)
    for pair in range(heads // 2):
        cq, ck, cv = pair_columns(pair, per_group, width)
        own = slice(2 * pair * HD, 2 * (pair + 1) * HD)
        query, key, grad = qkv_ref[:, cq], qkv_ref[:, ck], grad_ref[:, own]
        even, odd = score_scr[2 * pair], score_scr[2 * pair + 1]
        out_ref[:, cq] = (SCALE * nn(
            jnp.concatenate([even, odd], axis=1),
            jnp.concatenate([key * low, key * high], axis=0),
        )).astype(BF16)
        out_ref[:, ck] = (SCALE * tn(
            jnp.concatenate([even, odd], axis=0),
            jnp.concatenate([query * low, query * high], axis=0),
        )).astype(BF16)
        out_ref[:, cv] = (tn(
            jnp.concatenate([weight_scr[2 * pair], weight_scr[2 * pair + 1]], axis=0),
            jnp.concatenate([grad * low, grad * high], axis=0),
        )).astype(BF16)


def join_back_kernel(offs, near_ref, far_ref, first_ref, out_ref):
    positions, model = first_ref.shape
    heads = model // HD
    per_group = heads // 2
    width = per_group * HD
    groups = far_ref.shape[1]
    out_ref[:, 3 * model :] = first_ref[:, model // 2 :]

    for pair in range(heads // 2):
        even, odd = far_ref[2 * pair], far_ref[2 * pair + 1]
        spread = slot_spread(offs, pair, groups, positions)
        for e, columns in enumerate(pair_columns(pair, per_group, width)):
            part = slice(e * HD, (e + 1) * HD)
            far = nn(spread, beside(even[:, part], odd[:, part]))
            out_ref[:, columns] = (near_ref[:, columns].astype(F32) + far).astype(BF16)


def weight_grad_kernel(
    change, core_ref, left, right_0, right_1, left_got, right_0_got, right_1_got,
    *refs,
):
    kept_ref, sent_ref, left_scr = refs[-3:]
    block = kept_ref.shape[1]
    if len(refs) > 3:
        sent_ref[2 * block :] = refs[0][...]
    step = pl.program_id(0)

    @pl.when((step == 0) | (step == change))
    def _():
        left_scr[0] = left[...].T
        left_scr[1] = left_got[...].T

    product = [
        nn(left_scr[0], right[...]) + nn(left_scr[1], got[...])
        for right, got in ((right_0, right_0_got), (right_1, right_1_got))
    ]
    kept_ref[0] = product[0][:block].astype(BF16)
    sent_ref[block : 2 * block] = product[1][block:].astype(BF16)
    low, high = product[0][block:], product[1][:block]

    @pl.when(core_ref[0] == 0)
    def _():
        kept_ref[1] = high.astype(BF16)
        sent_ref[:block] = low.astype(BF16)

    @pl.when(core_ref[0] != 0)
    def _():
        kept_ref[1] = low.astype(BF16)
        sent_ref[:block] = high.astype(BF16)


def input_grad_kernel(
    core_ref, x_ref, pack_ref, resid_ref, gain_ref, second_ref, place_ref, w0, w1, w2, w3, w4, w5, w6, w7,
    grad_ref, gain_grad, weights, sems,
):
    span = weights.shape[2]
    copies = stream_copies((w0, w1, w2, w3, w4, w5, w6, w7), slice(None), weights, sems, core_ref[0])
    start_all(copies)
    normal, inverse = row_norm(x_ref[...].astype(F32))
    wait_all(copies)
    grad_first = nt(pack_ref[:, :span], weights[0]) + nt(pack_ref[:, span : 2 * span], weights[1])
    first = jnp.sum(grad_first * normal, axis=0, keepdims=True)
    parts = three_parts(jnp.concatenate([first, second_ref[...]] + [jnp.zeros_like(first)] * 6))
    gain_grad[...] = sum(nt(part, place_ref[...]) for part in parts)
    grad = resid_ref[...] + row_norm_back(grad_first, normal, inverse, gain_ref[...])
    grad_ref[...] = nt(grad.astype(BF16), place_ref[...]).astype(BF16)


def finish_kernel(
    core_ref, kept_ref, got_ref, attend_ref, merge_ref, expand_ref, reduce_ref, gain_ref
):
    rows = attend_ref.shape[1] // 2
    width, hidden = merge_ref.shape[1], expand_ref.shape[1]
    gain_ref[...] = kept_ref[rows:, : 3 * width] + got_ref[rows:, : 3 * width]

    def place_halves(first, second):
        for half, source in enumerate((first, second)):
            here = slice(half * rows, (half + 1) * rows)
            for e in range(3):
                attend_ref[e, here] = source[:rows, e * width : (e + 1) * width]
            start = 3 * width
            expand_ref[here] = source[:rows, start : start + hidden]
            merge_ref[here] = source[:rows, start + hidden : start + hidden + width]
            reduce_ref[here] = source[:rows, start + hidden + width :]

    @pl.when(core_ref[0] == 0)
    def _():
        place_halves(kept_ref, got_ref)

    @pl.when(core_ref[0] != 0)
    def _():
        place_halves(got_ref, kept_ref)


def whole(*shape):
    return pl.BlockSpec(shape, lambda *_: tuple(0 for _ in shape))


def sds(shape, dtype):
    return jax.ShapeDtypeStruct(shape, dtype)


def call(
    kernel, grid, in_specs, out_specs, out_shape, scratch=(), earlier=(), cost=5
):
    def body(*refs):
        kernel(*refs[len(earlier) :])

    return partial(
        pl.pallas_call(
            body,
            grid=grid,
            in_specs=[ANY] * len(earlier) + in_specs,
            out_specs=out_specs,
            out_shape=out_shape,
            scratch_shapes=list(scratch),
            compiler_params=pltpu.CompilerParams(
                dimension_semantics=("arbitrary",) * len(grid), vmem_limit_bytes=VMEM_LIMIT
            ),
            cost_estimate=pl.CostEstimate(
                flops=cost * 1_150_000_000, bytes_accessed=0, transcendentals=0
            ),
        ),
        *earlier,
    )


def per_device(
    inputs,
    attend_weight,
    merge_weight,
    expand_weight,
    reduce_weight,
    gain_first,
    gain_heads,
    gain_second,
    gain_hidden,
    cotangent,
    lengths,
    local_span,
    dilation,
):
    seq_size, head_size = lax.axis_size("seq"), lax.axis_size("head")
    row_count, positions, model = inputs.shape
    rows = row_count // head_size
    tokens = rows * positions
    shard_rows, width = attend_weight.shape[1:]
    heads = width * head_size // HD
    group_heads = heads // head_size
    hidden_here = expand_weight.shape[1]
    hidden_width = hidden_here * head_size
    quarter = model // 4
    groups = positions // DILATION_SMALL
    pairs = rows * heads
    owned = -(-pairs // seq_size)
    padded = owned * seq_size
    seq_index, head_index = lax.axis_index("seq"), lax.axis_index("head")
    core = seq_index & 1
    core_ref = core.reshape(1)

    attend_shard = gather_core(jnp.concatenate(list(attend_weight), axis=1))
    attend_far = jnp.concatenate(gather_far(attend_shard))
    other_shard = jnp.concatenate([expand_weight, merge_weight.T, reduce_weight.T], axis=1)
    other_shard = gather_core(after(other_shard, attend_shard))
    third = other_shard.shape[1] // 3
    other_shards = [
        gate(other_shard[:, i * third : (i + 1) * third], attend_far) for i in range(3)
    ]
    attend_got = exchange_near(attend_far, 0)
    attend_more = exchange_near(attend_far, 1)
    other_pieces = [gather_far(other_shards[0])]
    attend_last = exchange_near(attend_got, 1)
    other_pieces.append(gather_far(gate(other_shards[1], attend_got)))
    other_far = [jnp.concatenate(pieces) for pieces in other_pieces]
    other_got = [exchange_near(other_far[0], 0)]
    attend_last = gate(attend_last, other_got[0])
    other_pieces.append(gather_far(gate(other_shards[2], attend_last)))
    attend_all = (attend_far, attend_got, attend_more, attend_last)
    attend_all = attend_all + tuple(exchange(piece, 1, 0) for piece in attend_all)
    both_gains = jnp.concatenate([gain_heads, gain_hidden])
    partner_gains = exchange(both_gains.reshape(-1, 128), 0, 1).reshape(-1)
    gain_heads_all = jnp.concatenate([gain_heads, partner_gains[:width]])[None]
    gain_hidden_all = jnp.concatenate([gain_hidden, partner_gains[width:]])[None]

    half_rows = shard_rows // 2
    part, near, far, beside, inside = jnp.meshgrid(
        *[jnp.arange(n) for n in (2, 2, seq_size // 4, 2, half_rows)], indexing="ij"
    )
    shard_of = seq_index ^ (4 * far + 2 * near + (beside ^ part))
    feature_of = (shard_of * shard_rows + (core ^ part) * half_rows + inside).reshape(-1)
    feature_of = gate(feature_of, attend_far)

    row_start = head_index * rows
    lengths, local_span, dilation = gate(
        jnp.stack([lengths, local_span, dilation]), attend_far
    )

    def own_rows(tensor):
        return lax.dynamic_slice_in_dim(tensor, row_start, rows, axis=0)

    scalars = jnp.concatenate([own_rows(lengths), (seq_index * positions).reshape(1)])
    both_rows_gains = jnp.pad(jnp.stack([gain_first, gain_second]), ((0, 6), (0, 0)))
    own_block = pl.BlockSpec((rows, positions, model), lambda i, head: (head[0], 0, 0))

    def fixed(*shape):
        return pl.BlockSpec(shape, lambda i, head: tuple(0 for _ in shape))

    place, x_own, seed, own_gains = pl.pallas_call(
        prepare_kernel,
        grid_spec=pltpu.PrefetchScalarGridSpec(
            num_scalar_prefetch=1,
            grid=(1,),
            in_specs=[SMEM, fixed(1, model), fixed(8, model), own_block, own_block],
            out_specs=[
                fixed(model, model), fixed(tokens, model), fixed(tokens, model), fixed(8, model)
            ],
        ),
        out_shape=[
            sds((model, model), BF16), sds((tokens, model), BF16), sds((tokens, model), BF16),
            sds((8, model), F32),
        ],
        compiler_params=pltpu.CompilerParams(vmem_limit_bytes=VMEM_LIMIT),
        cost_estimate=pl.CostEstimate(flops=0, bytes_accessed=0, transcendentals=0),
    )(
        head_index.reshape(1), scalars, feature_of[None], both_rows_gains, inputs, cotangent
    )
    gain_one, gain_two = own_gains[:1], own_gains[1:2]
    places = jnp.arange(positions)
    span_block = places[None, :] // own_rows(local_span)[:, None]
    within = (span_block[:, :, None] == span_block[:, None, :]) & (
        places[None, :] <= places[:, None]
    )
    bias = jnp.where(within, 0.0, MASKED_SCORE).astype(F32)

    local_head = jnp.arange(heads)
    head_ids = (head_index ^ (local_head // group_heads)) * group_heads + local_head % group_heads
    offsets = gate((head_ids % DILATION_SMALL).astype(jnp.int32), attend_far)
    pair_ids = jnp.minimum(seq_index * owned + jnp.arange(owned), pairs - 1)
    pair_rate = own_rows(dilation)[pair_ids // heads]
    pair_head = head_ids[pair_ids % heads]
    parity = jnp.where(
        pair_rate == DILATION_SMALL, 0, 1 + (pair_head % pair_rate) // DILATION_SMALL
    ).astype(jnp.int32)

    model_spec, model_shape = whole(tokens, model), (tokens, model)
    attend_scratch = pltpu.VMEM((2, model, 3 * width), BF16)

    def by_row(size):
        return pl.BlockSpec((positions, size), lambda r: (r, 0))

    def of_row(size):
        return pl.BlockSpec((heads, groups, size), lambda r: (r, 0, 0))

    model_row, qkv_row = by_row(model), by_row(3 * model)
    bias_row = pl.BlockSpec((1, positions, positions), lambda r: (r, 0, 0))
    first_in, qkv, slots, near_out, log_near = call(
        project_kernel,
        (rows,),
        [SMEM, SMEM, model_spec, bias_row, whole(1, model)] + [ANY] * 8,
        [model_row, qkv_row, of_row(3 * HD), model_row, model_row],
        [
            sds(model_shape, BF16),
            sds((tokens, 3 * model), BF16),
            sds((padded, groups, 3 * HD), BF16),
            sds(model_shape, F32),
            sds(model_shape, F32),
        ],
        [
            attend_scratch,
            pltpu.VMEM((heads // 2, 2 * positions, positions), F32),
            pltpu.VMEM((tokens, model), BF16),
            pltpu.VMEM((tokens, 3 * model), BF16),
            pltpu.SemaphoreType.DMA((8,)),
        ],
        cost=20,
    )(core_ref, offsets, x_own, bias, gain_one, *attend_all)
    other_held = [jnp.concatenate([other_far[0], other_got[0]])]
    other_more = [exchange_near(other_held[0], 1)]
    other_got.append(exchange_near(other_far[1], 0))
    other_far.append(gate(jnp.concatenate(other_pieces[2]), other_more[0]))
    other_got.append(exchange_near(other_far[2], 0))
    other_held.append(jnp.concatenate([other_far[1], other_got[1]]))
    other_more.append(exchange_near(other_held[1], 1))
    other_core = [(exchange(other_held[0], 1, 0), exchange(other_more[0], 1, 0))]

    def to_owners(value):
        value = value.reshape(seq_size, owned, groups, value.shape[-1])
        return lax.all_to_all(value, "seq", 0, 0, tiled=True)

    def from_owners(value):
        value = lax.all_to_all(value, "seq", 0, 0, tiled=True)
        return value.reshape(padded, groups, value.shape[-1])

    def by_pair(size):
        return pl.BlockSpec((seq_size, 1, groups, size), lambda i: (0, i, 0, 0))

    def owned_shape(size):
        return sds((seq_size, owned, groups, size), BF16)

    slot_count = seq_size * groups
    kv_scratch = pltpu.VMEM((slot_count, 2 * HD), BF16)
    far_qkv = to_owners(slots)
    far_out = call(
        far_kernel,
        (owned,),
        [SMEM, by_pair(3 * HD)],
        by_pair(2 * HD),
        owned_shape(2 * HD),
        [kv_scratch],
        cost=4,
        earlier=(seed, place, gain_two),
    )(parity, far_qkv)
    far_here = from_owners(far_out)
    other_held.append(
        gate(jnp.concatenate([other_far[2], other_got[2]]), far_out)
    )
    other_more.append(exchange_near(other_held[2], 1))
    other_core.append((exchange(other_held[1], 1, 0), exchange(other_more[1], 1, 0)))
    held_core = exchange(other_held[2], 1, 0)

    other_core.append((held_core, exchange(other_more[2], 1, 0)))
    weights_all = [
        piece for i in range(3) for piece in (other_held[i], other_more[i], *other_core[i])
    ]
    hidden_pack = (tokens, hidden_width + model // 2)
    pre_pack = (tokens, hidden_width + 2 * model)
    low_scratch = pltpu.VMEM(model_shape, BF16)
    full_scratch = pltpu.VMEM(model_shape, F32)
    hidden_scratch = pltpu.VMEM((tokens, hidden_width), F32)
    weight_scratch = pltpu.VMEM((2, model, hidden_here), BF16)
    (
        block_mine, hidden_in, grad_pre, lefts, grad_resid, grad_att, stats, grad_slots,
        grad_heads, grad_second, grad_hidden,
    ) = call(
        hidden_kernel,
        (),
        [SMEM, SMEM, whole(1, model), whole(1, model), whole(1, hidden_width),
         whole(padded, groups, 2 * HD)] + [ANY] * 17,
        [
            model_spec, ANY, ANY, model_spec, model_spec, model_spec, model_spec,
            whole(padded, groups, 2 * HD), whole(1, model), whole(1, model),
            whole(1, hidden_width),
        ],
        [
            sds(model_shape, BF16), sds(hidden_pack, BF16), sds(pre_pack, BF16),
            sds(model_shape, BF16), sds(model_shape, F32), sds(model_shape, BF16),
            sds(model_shape, BF16), sds((padded, groups, 2 * HD), BF16), sds((1, model), F32),
            sds((1, model), F32), sds((1, hidden_width), F32),
        ],
        [
            low_scratch, full_scratch, full_scratch, low_scratch,
            pltpu.VMEM((model, model), BF16), pltpu.VMEM((2, model, width), BF16),
            weight_scratch, weight_scratch, low_scratch, hidden_scratch, hidden_scratch, hidden_scratch,
            pltpu.VMEM(hidden_pack, BF16), pltpu.VMEM(pre_pack, BF16),
            pltpu.VMEM((heads, positions, 2 * HD), F32), pltpu.SemaphoreType.DMA((5, 8)),
            pltpu.SemaphoreType.DMA((5,)), pltpu.SemaphoreType.DMA((2 * HIDDEN_BLOCKS + 2,)),
        ],
        cost=8,
    )(
        core_ref, offsets, gain_heads_all, gain_two, gain_hidden_all, far_here, near_out,
        log_near, x_own, seed, place, *weights_all,
    )

    def weight_grad(
        size, left, left_at, right, right_at, left_got_at, earlier=(), change=0, extra=None
    ):
        got = exchange(right, 1, 0)

        def spec(at):
            return pl.BlockSpec((tokens, width), lambda j: (0, at(j)))

        def rights():
            return [spec(lambda j, x=x: right_at(x, j)) for x in range(2)]

        sent_rows = 2 * quarter
        extras = []
        if extra is not None:
            sent_rows += GAIN_ROWS
            extras = [extra]
        return call(
            partial(weight_grad_kernel, change),
            (size // width,),
            [SMEM, spec(left_at)] + rights() + [spec(left_got_at)] + rights()
            + [pl.BlockSpec((GAIN_ROWS, width), lambda j: (0, j))] * len(extras),
            [
                pl.BlockSpec((2, quarter, width), lambda j: (0, 0, j)),
                pl.BlockSpec((sent_rows, width), lambda j: (0, j)),
            ],
            [sds((2, quarter, size), BF16), sds((sent_rows, size), BF16)],
            [pltpu.VMEM((2, model // 2, tokens), BF16)],
            earlier=earlier,
            cost=7,
        )(core_ref, left, right, right, got, got, got, *extras)

    per_half = hidden_here // width
    hidden_blocks = hidden_width // width

    def both_rows(mine, earlier=None):
        mine = mine.reshape(rows, positions, model)
        other = exchange(mine, 0, 1)
        if earlier is not None:
            other = gate(other, earlier)
        both = jnp.concatenate([other, other])
        return lax.dynamic_update_slice_in_dim(both, mine, row_start, axis=0)

    far_grads = to_owners(grad_slots)
    near_grad = call(
        near_back_kernel,
        (rows,),
        [bias_row, qkv_row, model_row, model_row],
        qkv_row,
        sds((tokens, 3 * model), BF16),
        [pltpu.VMEM((heads, positions, positions), BF16)] * 2,
        cost=60,
    )(bias, qkv, grad_att, stats)
    reduce_kept, reduce_sent = weight_grad(
        hidden_here, seed, lambda j: 0, hidden_in, lambda x, j: x * per_half + j,
        lambda j: hidden_blocks, earlier=(near_grad,),
    )
    far_back = call(
        far_back_kernel,
        (owned,),
        [SMEM, by_pair(3 * HD), by_pair(2 * HD)],
        by_pair(3 * HD),
        owned_shape(3 * HD),
        [kv_scratch, pltpu.VMEM((slot_count, 2 * HD), F32)],
        earlier=(reduce_sent,),
        cost=0,
    )(parity, far_qkv, far_grads)
    expand_kept, expand_sent = weight_grad(
        hidden_here + width, lefts, lambda j: jnp.where(j < per_half, 0, 1), grad_pre,
        lambda x, j: jnp.where(j < per_half, x * per_half + j, hidden_blocks + x),
        lambda j: hidden_blocks + 2 + jnp.where(j < per_half, 0, 1),
        earlier=(far_back,), change=per_half,
    )
    back_here = from_owners(far_back)
    block_out = both_rows(block_mine, expand_sent)
    reduce_kept, reduce_sent, _ = scatter_first(reduce_kept, reduce_sent)
    grad_pack_shape = (tokens, 3 * model + model // 2)
    grad_pack = call(
        join_back_kernel,
        (rows,),
        [SMEM, qkv_row, of_row(3 * HD), model_row],
        by_row(grad_pack_shape[1]),
        sds(grad_pack_shape, BF16),
        earlier=(reduce_sent, block_out),
        cost=1,
    )(offsets, near_grad, back_here, first_in)
    grad_mine, grad_shared = call(
        input_grad_kernel,
        (),
        [
            SMEM, model_spec, whole(*grad_pack_shape), model_spec, whole(1, model),
            whole(1, model), whole(model, model),
        ]
        + [ANY] * 8,
        [model_spec, whole(8, model)],
        [sds(model_shape, BF16), sds((8, model), F32)],
        [attend_scratch, pltpu.SemaphoreType.DMA((8,))],
        cost=3,
    )(core_ref, x_own, grad_pack, grad_resid, gain_one, grad_second, place, *attend_all)

    expand_kept, expand_sent, _ = scatter_first(
        gate(expand_kept, grad_mine), expand_sent
    )
    def by_head(grad):
        size = grad.shape[1] // 2
        return jnp.where(head_index == 0, grad[0], jnp.roll(grad[0], size))

    grad_shared = gate(grad_shared, expand_sent)
    gains = jnp.concatenate(
        [
            grad_shared[0], grad_shared[1], by_head(grad_heads), by_head(grad_hidden),
        ]
    )
    gain_rows = -(-gains.shape[0] // (3 * width))
    gains = jnp.pad(gains, (0, gain_rows * 3 * width - gains.shape[0])).reshape(gain_rows, -1)
    gain_sent = to_rows(gains)
    reduce_kept, reduce_sent, _ = scatter_second(reduce_kept, reduce_sent)
    attend_kept, attend_sent = weight_grad(
        3 * width, first_in, lambda j: 0, grad_pack, lambda x, j: 3 * x + j, lambda j: 6,
        earlier=(grad_mine, *reduce_sent), extra=gain_sent,
    )
    attend_kept, attend_sent, attend_near = scatter_first(attend_kept, attend_sent)
    gains = from_rows(gain_sent, gain_rows) + from_rows(attend_near[2 * quarter :], gain_rows)
    gain_sent = to_rows(gains)
    reduce_total = scatter_far(reduce_kept, reduce_sent)
    expand_kept, expand_sent, _ = scatter_second(expand_kept, expand_sent)
    attend_sent = after(after(attend_sent, reduce_total), expand_sent[0])
    attend_kept, attend_sent, attend_got = scatter_second(
        attend_kept, jnp.concatenate([attend_sent, gain_sent])
    )
    gains = from_rows(gain_sent, gain_rows) + from_rows(attend_got[quarter:], gain_rows)
    stages = far_stages(seq_size)
    for stage in reversed(range(len(stages))):
        unit, radix = stages[stage]
        gain_sent = to_rows(gains)
        everyone = [from_rows(gain_sent, gain_rows)]
        rows_sent = attend_sent[0].shape[0]
        for i, piece in enumerate(attend_sent):
            got = exchange(jnp.concatenate([piece, gain_sent]), unit * (i + 1), 0)
            attend_kept = attend_kept + got[:rows_sent].astype(F32)
            everyone.append(from_rows(got[rows_sent:], gain_rows))
        while len(everyone) > 1:
            everyone = [one + two for one, two in zip(everyone[::2], everyone[1::2])]
        gains = everyone[0]
        if stage:
            held = attend_kept.reshape(stages[stage - 1][1], -1, 3 * width)
            attend_kept, attend_sent = held[0], [piece.astype(BF16) for piece in held[1:]]
    grad_inputs = both_rows(gate(grad_mine, attend_got))
    expand_total = scatter_far(gate(expand_kept, attend_got), expand_sent)
    totals = jnp.concatenate([attend_kept, expand_total, reduce_total], axis=1)
    gains = jnp.pad(gains, ((0, 8 - gain_rows), (0, totals.shape[1] - gains.shape[1])))
    last_kept = jnp.concatenate([totals[:half_rows], gains])
    last_got = exchange(jnp.concatenate([totals[half_rows:], gains]), 1, 0)
    last_shape = last_kept.shape
    grad_attend, grad_merge, grad_expand, grad_reduce, gains = call(
        finish_kernel,
        (),
        [SMEM, whole(*last_shape), whole(*last_shape)],
        [
            whole(3, shard_rows, width), whole(shard_rows, width), whole(shard_rows, hidden_here),
            whole(shard_rows, hidden_here), whole(8, 3 * width),
        ],
        [
            sds((3, shard_rows, width), F32), sds((shard_rows, width), F32),
            sds((shard_rows, hidden_here), F32), sds((shard_rows, hidden_here), F32),
            sds((8, 3 * width), F32),
        ],
        cost=1,
    )(core_ref, last_kept, last_got)
    gains = gains[:gain_rows].reshape(-1)

    def own_half(start, size):
        return jnp.where(
            head_index == 0, gains[start : start + size], gains[start + size : start + 2 * size]
        )

    return (
        block_out,
        grad_inputs,
        grad_attend,
        grad_merge.T,
        grad_expand,
        grad_reduce.T,
        gains[:model],
        own_half(2 * model, width),
        gains[model : 2 * model],
        own_half(3 * model, hidden_here),
    )


def solution(mesh):
    placed = (
        P(None, "seq", None),
        P(None, "seq", "head"),
        P("head", "seq"),
        P("seq", "head"),
        P("head", "seq"),
        P(),
        P("head"),
        P(),
        P("head"),
        P(None, "seq", None),
        P(),
        P(),
        P(),
    )
    return jax.shard_map(
        per_device,
        mesh=mesh,
        in_specs=placed,
        out_specs=(
            P(None, "seq", None),
            P(None, "seq", None),
            P(None, "seq", "head"),
            P("head", "seq"),
            P("seq", "head"),
            P("head", "seq"),
            P(),
            P("head"),
            P(),
            P("head"),
        ),
        check_vma=False,
    )
```

```python
from functools import partial

import jax
import jax.numpy as jnp
from jax import lax
from jax.experimental import pallas as pl
from jax.experimental.pallas import tpu as pltpu
from jax.sharding import PartitionSpec as P

HD = 64
DILATION_SMALL = 8
NORM_EPSILON = 1e-05
MASKED_SCORE = -1e30
SCALE = HD ** (-0.5)
F32 = jnp.float32
BF16 = jnp.bfloat16
ANY = pl.BlockSpec(memory_space=pl.ANY)
SMEM = pl.BlockSpec(memory_space=pltpu.SMEM)
VMEM_LIMIT = 56 * 1024 * 1024


def nn(left, right):
    return lax.dot_general(left, right, (((1,), (0,)), ((), ())), preferred_element_type=F32)


def nt(left, right):
    return lax.dot_general(left, right, (((1,), (1,)), ((), ())), preferred_element_type=F32)


def tn(left, right):
    return lax.dot_general(left, right, (((0,), (0,)), ((), ())), preferred_element_type=F32)


def row_norm(values):
    center = jnp.mean(values, axis=-1, keepdims=True)
    spread = jnp.mean(values * values, axis=-1, keepdims=True) - center * center
    inverse = lax.rsqrt(spread + NORM_EPSILON)
    return (values - center) * inverse, inverse


def row_norm_back(incoming, normal, inverse, gain_row):
    scaled = incoming * gain_row
    first_mean = jnp.mean(scaled, axis=-1, keepdims=True)
    second_mean = jnp.mean(scaled * normal, axis=-1, keepdims=True)
    return inverse * (scaled - first_mean - normal * second_mean)


def three_parts(values):
    high = values.astype(BF16)
    rest = values - high.astype(F32)
    middle = rest.astype(BF16)
    low = (rest - middle.astype(F32)).astype(BF16)
    return high, middle, low


def gelu_parts(values):
    expo = jnp.exp(values * values * -0.5)
    term = 1.0 / (1.0 + (0.3275911 * 0.7071067811865476) * jnp.abs(values))
    poly = term * (
        0.254829592
        + term
        * (-0.284496736 + term * (1.421413741 + term * (-1.453152027 + term * 1.061405429)))
    )
    tail = 0.5 * poly * expo
    phi = jnp.where(values >= 0.0, 1.0 - tail, tail)
    return values * phi, phi + values * expo * 0.3989422804014327


def iota(shape, dim):
    return lax.broadcasted_iota(jnp.int32, shape, dim)


def permute(value, target):
    seq_size, head_size = lax.axis_size("seq"), lax.axis_size("head")
    pairs = []
    for s in range(seq_size):
        for h in range(head_size):
            to_seq, to_head = target(s, h)
            pairs.append((s * head_size + h, to_seq * head_size + to_head))
    return lax.ppermute(value, ("seq", "head"), pairs)


def exchange(value, seq_mask, head_mask):
    return permute(value, lambda s, h: (s ^ seq_mask, h ^ head_mask))


def exchange_near(value, turn):
    return permute(value, lambda s, h: (s, h ^ 1) if (s & 1) == turn else (s ^ 2, h))


def far_stages(seq_size):
    unit, left, stages = 4, seq_size // 4, []
    while left > 1:
        radix = 4 if left % 4 == 0 else 2
        stages.append((unit, radix))
        unit, left = unit * radix, left // radix
    return stages


def gate(value, *earlier):
    def kernel(*refs):
        pass

    return pl.pallas_call(
        kernel,
        in_specs=[ANY] * (len(earlier) + 1),
        out_specs=ANY,
        out_shape=jax.ShapeDtypeStruct(value.shape, value.dtype),
        input_output_aliases={len(earlier): 0},
        cost_estimate=pl.CostEstimate(flops=0, bytes_accessed=0, transcendentals=0),
    )(*earlier, value)


def after(value, earlier):
    zero = earlier[(0,) * earlier.ndim].astype(F32) * 0.0
    return value + zero.astype(value.dtype)


def gather_core(shard):
    core = lax.axis_index("seq") & 1
    half = shard.shape[0] // 2
    kept = lax.dynamic_slice_in_dim(shard, core * half, half)
    sent = lax.dynamic_slice_in_dim(shard, (1 - core) * half, half)
    return jnp.concatenate([kept, exchange(sent, 1, 0)])


def gather_far(held):
    stages = far_stages(lax.axis_size("seq"))
    for unit, radix in stages:
        pieces = [held] + [exchange(held, unit * i, 0) for i in range(1, radix)]
        held = jnp.concatenate(pieces) if (unit, radix) != stages[-1] else None
    return pieces


def scatter_first(kept, sent):
    got = exchange_near(sent, 1)
    block = kept.shape[1]

    def total(index):
        return kept[index].astype(F32) + got[index * block : (index + 1) * block].astype(F32)

    return total(0), total(1).astype(BF16), got


def scatter_second(kept, sent):
    got = exchange_near(sent, 0)
    total = kept + got[: kept.shape[0]].astype(F32)
    unit, radix = far_stages(lax.axis_size("seq"))[-1]
    total = total.reshape(radix, -1, total.shape[-1])
    return total[0], [total[i].astype(BF16) for i in range(1, radix)], got


def scatter_far(kept, sent):
    stages = far_stages(lax.axis_size("seq"))
    for stage in reversed(range(len(stages))):
        unit, radix = stages[stage]
        for i, piece in enumerate(sent):
            kept = kept + exchange(piece, unit * (i + 1), 0).astype(F32)
        if stage:
            held = kept.reshape(stages[stage - 1][1], -1, kept.shape[-1])
            kept, sent = held[0], [piece.astype(BF16) for piece in held[1:]]
    return kept


def to_rows(sums):
    high = lax.reduce_precision(sums, 8, 7)
    low = sums - high
    spare = jnp.zeros((GAIN_ROWS - 2 * sums.shape[0], sums.shape[1]), F32)
    return jnp.concatenate([high, low, spare]).astype(BF16)


def from_rows(rows, count):
    return rows[:count].astype(F32) + rows[count : 2 * count].astype(F32)


GAIN_ROWS = 16


def stream_copies(pieces, columns, target, sems, core):
    block = target.shape[1] // 4
    blocks = [
        piece.at[pl.ds(start, block), columns]
        for piece in pieces
        for start in range(0, piece.shape[0], block)
    ]
    copies = []
    for index, source in enumerate(blocks):
        part, second, first = index // 4, index // 2 % 2, index % 2
        straight = (core ^ part) == 0
        x = jnp.where(straight, first, second)
        y = jnp.where(straight, second, first)
        row = pl.multiple_of((2 * part + y) * block, block)
        copies.append(
            pltpu.make_async_copy(source, target.at[x, pl.ds(row, block)], sems.at[index])
        )
    return copies


def start_all(copies):
    for copy in copies:
        copy.start()


def wait_all(copies):
    for copy in copies:
        copy.wait()


def pair_columns(pair, per_group, width):
    group, inside = divmod(2 * pair, per_group)
    start = group * 3 * width + inside * HD
    return [slice(start + e * width, start + e * width + 2 * HD) for e in range(3)]


def slot_select(offset, groups, positions):
    shape = (groups, positions)
    return (iota(shape, 1) == DILATION_SMALL * iota(shape, 0) + offset).astype(BF16)


def slot_spread(offs, pair, groups, positions, times=1):
    shape = (positions, 2 * groups * times)
    slot = iota(shape, 1) & (2 * groups - 1)
    offset = jnp.where(slot < groups, offs[2 * pair], offs[2 * pair + 1])
    return (iota(shape, 0) == DILATION_SMALL * (slot & (groups - 1)) + offset).astype(BF16)


def side_masks():
    lane = iota((1, 2 * HD), 1)
    return (lane < HD).astype(BF16), (lane >= HD).astype(BF16)


def beside(even, odd):
    nothing = jnp.zeros_like(even)
    return jnp.concatenate(
        [jnp.concatenate([even, nothing], axis=1), jnp.concatenate([nothing, odd], axis=1)], axis=0
    )


def prepare_kernel(
    head_ref, scalars, feature_ref, gains_ref, x_ref, seed_ref, place_out, x_out, seed_out, gains_out
):
    rows, positions, model = x_ref.shape
    feature = feature_ref[...]
    place = (iota((model, model), 0) == feature).astype(BF16)
    place_out[...] = place
    at = scalars[rows] + iota((positions, model), 0)
    for r in range(rows):
        here = slice(r * positions, (r + 1) * positions)
        x_out[here] = nn(x_ref[r], place).astype(BF16)
        seed = jnp.where(at < scalars[r], seed_ref[r].astype(F32), 0.0).astype(BF16)
        seed_out[here] = nn(seed, place).astype(BF16)
    gains_out[...] = sum(nn(part, place) for part in three_parts(gains_ref[...]))


def project_kernel(
    core_ref, offs, x_ref, bias_ref, gain_ref, w0, w1, w2, w3, w4, w5, w6, w7,
    first_ref, qkv_ref, slot_ref, out_ref, lse_ref, weights, score_scr, first_scr, qkv_scr,
    sems,
):
    _, positions = bias_ref.shape[:2]
    model = x_ref.shape[1]
    width = weights.shape[2] // 3
    heads = model // HD
    per_group = heads // 2
    groups = positions // DILATION_SMALL
    r = pl.program_id(0)

    @pl.when(r == 0)
    def _():
        pieces = (w0, w1, w2, w3, w4, w5, w6, w7)
        copies = stream_copies(pieces, slice(None), weights, sems, core_ref[0])
        start_all(copies)
        normal, _ = row_norm(x_ref[...].astype(F32))
        first_scr[...] = (normal * gain_ref[...]).astype(BF16)
        wait_all(copies)
        for hh in range(2):
            columns = slice(hh * 3 * width, (hh + 1) * 3 * width)
            qkv_scr[:, columns] = nn(first_scr[...], weights[hh]).astype(BF16)

    low, high = side_masks()
    side = iota((positions, 2 * HD), 1) < HD
    here = pl.ds(pl.multiple_of(r * positions, positions), positions)
    first_ref[...] = first_scr[here]
    qkv_ref[...] = qkv_scr[here]
    bias = bias_ref[0]
    bias = jnp.concatenate([bias, bias], axis=0)
    for pair in range(heads // 2):
        cq, ck, cv = pair_columns(pair, per_group, width)
        query, key = qkv_ref[:, cq], qkv_ref[:, ck]
        both = jnp.concatenate([query * low, query * high], axis=0)
        score_scr[pair] = nt(both, key) * SCALE + bias
        every = jnp.concatenate([query, key, qkv_ref[:, cv]], axis=1)
        for inside in range(2):
            chosen = slot_select(offs[2 * pair + inside], groups, positions)
            slots = nn(chosen, every).astype(BF16)
            starts = [2 * HD * e + HD * inside for e in range(3)]
            slot_ref[2 * pair + inside] = jnp.concatenate(
                [slots[:, start : start + HD] for start in starts], axis=1
            )
    for pair in range(heads // 2):
        value = qkv_ref[:, pair_columns(pair, per_group, width)[2]]
        score = score_scr[pair]
        peak = jnp.max(score, axis=-1, keepdims=True)
        expo = jnp.exp(score - peak)
        total = jnp.sum(expo, axis=-1, keepdims=True)
        expo = expo.astype(BF16)
        out = nn(
            jnp.concatenate([expo[:positions], expo[positions:]], axis=1),
            jnp.concatenate([value * low, value * high], axis=0),
        )
        columns = slice(2 * pair * HD, 2 * (pair + 1) * HD)
        log, scale = peak + jnp.log(total), 1.0 / total
        out_ref[:, columns] = out * jnp.where(side, scale[:positions], scale[positions:])
        lse_ref[:, columns] = jnp.where(side, log[:positions], log[positions:])


def far_masks(parity, row_start, row_count, slots):
    row = row_start + iota((row_count, slots), 0)
    column = iota((row_count, slots), 1)
    live_row = (parity == 0) | ((row & 1) == parity - 1)
    live_column = (parity == 0) | ((column & 1) == parity - 1)
    return (column <= row) & live_column, live_row


def for_blocks(count, body):
    if count == 1:
        body(0)
    else:
        lax.fori_loop(0, count, lambda b, carry: (body(b), carry)[1], 0)


def far_kernel(parity_ref, qkv_ref, out_ref, kv_scr):
    devices, _, groups, _ = qkv_ref.shape
    slots = devices * groups
    block = min(slots, 256)
    per_block = block // groups
    parity = parity_ref[pl.program_id(0)]
    kv_scr[...] = qkv_ref[:, 0].reshape(slots, 3 * HD)[:, HD:]

    def body(index):
        piece = pl.ds(index * per_block, per_block)
        query = qkv_ref[piece, 0].reshape(block, 3 * HD)[:, :HD]
        key, value = kv_scr[:, :HD], kv_scr[:, HD:]
        allowed, live = far_masks(parity, index * block, block, slots)
        score = jnp.where(allowed, nt(query, key) * SCALE, MASKED_SCORE)
        peak = jnp.max(score, axis=-1, keepdims=True)
        expo = jnp.exp(score - peak)
        total = jnp.sum(expo, axis=-1, keepdims=True)
        out = nn(expo.astype(BF16), value) / total
        log = jnp.where(live[:, :1], peak + jnp.log(total), MASKED_SCORE)
        high, middle, low = three_parts(log)
        lane = iota((block, 2 * HD), 1)
        tile = jnp.concatenate([out, out], axis=1)
        tile = jnp.where(lane == HD, high.astype(F32), tile)
        tile = jnp.where(lane == HD + 1, middle.astype(F32), tile)
        tile = jnp.where(lane == HD + 2, low.astype(F32), tile)
        out_ref[piece, 0] = tile.astype(BF16).reshape(per_block, groups, 2 * HD)

    for_blocks(slots // block, body)


HIDDEN_BLOCKS = 4


def hidden_kernel(
    core_ref, offs, gain_heads, gain_second, gain_hidden, far_ref, near_any, log_any, x_any,
    seed_any, place_any, a0, a1, a2, a3, b0, b1, b2, b3, c0, c1, c2, c3,
    block_ref, hidden_out, pre_out, left_ref, resid_ref, grad_ref, stats_ref, slot_ref,
    grad_heads, grad_second, grad_hidden,
    x_ref, att_ref, lse_ref, seed_ref, place_ref, merge_w, expand_w, reduce_w,
    second_ref, act_scr, slope_scr, grad_scr, hidden_ref, pre_ref, tile_scr, sems, in_sems, out_sems,
):
    tokens, model = x_ref.shape
    hidden_here = expand_w.shape[2]
    half_model = model // 2
    width = merge_w.shape[2]
    heads = model // HD
    groups = slot_ref.shape[1]
    positions = groups * DILATION_SMALL
    hidden_width = 2 * hidden_here
    block = hidden_width // HIDDEN_BLOCKS
    core = core_ref[0]
    chunks = ((a0, a1, a2, a3), (b0, b1, b2, b3), (c0, c1, c2, c3))
    third = a0.shape[1]

    def chunk_copies(target, first_column, size, at):
        copies = []
        for chunk, pieces in enumerate(chunks):
            low = max(first_column, chunk * third)
            high = min(first_column + size, (chunk + 1) * third)
            if low < high:
                copies += stream_copies(
                    pieces,
                    pl.ds(low - chunk * third, high - low),
                    target.at[:, :, pl.ds(low - first_column, high - low)],
                    sems.at[at + len(copies) // 8],
                    core,
                )
        return copies

    expand_copies = chunk_copies(expand_w, 0, hidden_here, 0)
    merge_copies = chunk_copies(merge_w, hidden_here, width, 2)
    reduce_copies = chunk_copies(reduce_w, hidden_here + width, hidden_here, 3)
    inputs = [
        pltpu.make_async_copy(source, target, in_sems.at[i])
        for i, (source, target) in enumerate(
            (
                (near_any, att_ref), (log_any, lse_ref), (x_any, x_ref), (seed_any, seed_ref),
                (place_any, place_ref),
            )
        )
    ]
    start_all(inputs[:3])
    start_all(merge_copies)
    start_all(expand_copies)
    start_all(inputs[3:4])
    start_all(reduce_copies)
    start_all(inputs[4:])

    def columns_of(index):
        return pl.ds(pl.multiple_of(index * block, block), block)

    def weight_block(weights, index):
        per_group = hidden_here // block
        return weights[lax.div(index, per_group), :, columns_of(lax.rem(index, per_group))]

    def send(source, target, index, columns):
        return pltpu.make_async_copy(
            source.at[:, columns], target.at[:, columns], out_sems.at[index]
        )

    nothing = jnp.zeros((tokens, 1), F32)
    wait_all(inputs[:3])

    lane = iota((positions, 2 * HD), 1)
    side, inside_lane = lane < HD, lane & (HD - 1)
    place = iota((positions, 2 * HD), 0) & (DILATION_SMALL - 1)

    def join_row(r, carry):
        here = pl.ds(pl.multiple_of(r * positions, positions), positions)
        for pair in range(heads // 2):
            even, odd = far_ref[r * heads + 2 * pair], far_ref[r * heads + 2 * pair + 1]
            spread = slot_spread(offs, pair, groups, positions)
            far_out = nn(spread, beside(even[:, :HD], odd[:, :HD]))
            even, odd = even.astype(F32), odd.astype(F32)
            logs = [
                beside(
                    jnp.broadcast_to(even[:, HD + i : HD + i + 1], (groups, HD)),
                    jnp.broadcast_to(odd[:, HD + i : HD + i + 1], (groups, HD)),
                )
                for i in range(3)
            ]
            log_far = sum(nn(spread, log.astype(BF16)) for log in logs)
            slot = jnp.where(side, offs[2 * pair], offs[2 * pair + 1])
            log_far = jnp.where(place == slot, log_far, MASKED_SCORE)
            columns = slice(2 * pair * HD, 2 * (pair + 1) * HD)
            log_near = lse_ref[here, columns]
            peak = jnp.maximum(log_near, log_far)
            weight_near, weight_far = jnp.exp(log_near - peak), jnp.exp(log_far - peak)
            total = weight_near + weight_far
            lse_ref[here, columns] = pltpu.roll(peak + jnp.log(total), HD, 1)
            att_ref[here, columns] = (
                att_ref[here, columns] * weight_near + far_out * weight_far
            ) / total
        return carry

    lax.fori_loop(0, tokens // positions, join_row, 0)
    normal_heads, _ = row_norm(att_ref[...])
    heads_in = (normal_heads * gain_heads[...]).astype(BF16)
    wait_all(merge_copies)
    merged = [nt(heads_in[:, hh * width : (hh + 1) * width], merge_w[hh]) for hh in range(2)]
    residual = x_ref[...].astype(F32) + (merged[0] + merged[1])
    resid_ref[...] = residual
    normal_two, inverse_two = row_norm(residual)
    second_in = (normal_two * gain_second[...]).astype(BF16)
    second_ref[...] = second_in
    start = hidden_width + model
    pre_ref[:, hidden_width:start] = heads_in
    pre_ref[:, start : start + half_model] = second_in[:, half_model:]
    left_ref[:, :half_model] = second_in[:, :half_model]
    wait_all(expand_copies)

    def expand_step(index, totals):
        columns = columns_of(index)
        act, slope = gelu_parts(nn(second_ref[...], weight_block(expand_w, index)))
        act_scr[:, columns] = act
        slope_scr[:, columns] = slope
        return (
            totals[0] + jnp.sum(act, axis=-1, keepdims=True),
            totals[1] + jnp.sum(act * act, axis=-1, keepdims=True),
        )

    total_one, total_two = lax.fori_loop(
        0, HIDDEN_BLOCKS, expand_step, (nothing, nothing), unroll=True
    )
    center = total_one / hidden_width
    inverse = lax.rsqrt(total_two / hidden_width - center * center + NORM_EPSILON)
    wait_all(inputs[3:4])
    hidden_ref[:, hidden_width:] = seed_ref[:, half_model:]
    wait_all(reduce_copies)

    def reduce_step(index, totals):
        columns = columns_of(index)
        normal = (act_scr[:, columns] - center) * inverse
        act_scr[:, columns] = normal
        gain = gain_hidden[:, columns]
        scaled = normal * gain
        hidden_ref[:, columns] = scaled.astype(BF16)
        send(hidden_ref, hidden_out, index, columns).start()
        grad = nn(seed_ref[...], weight_block(reduce_w, index))
        grad_hidden[:, columns] = jnp.sum(grad * normal, axis=0, keepdims=True)
        grad_scr[:, columns] = grad * gain
        return (
            totals[0] + jnp.sum(grad * gain, axis=-1, keepdims=True),
            totals[1] + jnp.sum(grad * scaled, axis=-1, keepdims=True),
        )

    total_one, total_two = lax.fori_loop(0, HIDDEN_BLOCKS, reduce_step, (nothing, nothing))
    seed_columns = slice(hidden_width, hidden_width + half_model)
    send(hidden_ref, hidden_out, HIDDEN_BLOCKS, seed_columns).start()
    mean_one = total_one / hidden_width
    mean_two = total_two / hidden_width

    def pre_step(index, carry):
        columns = columns_of(index)
        grad = inverse * (grad_scr[:, columns] - mean_one - act_scr[:, columns] * mean_two)
        pre_ref[:, columns] = (grad * slope_scr[:, columns]).astype(BF16)
        send(pre_ref, pre_out, HIDDEN_BLOCKS + 1 + index, columns).start()
        return carry

    lax.fori_loop(0, HIDDEN_BLOCKS, pre_step, 0)
    grad_second_in = nt(pre_ref[:, :hidden_here], expand_w[0]) + nt(
        pre_ref[:, hidden_here:hidden_width], expand_w[1]
    )
    normal_two, inverse_two = row_norm(resid_ref[...])
    grad_second[...] = jnp.sum(grad_second_in * normal_two, axis=0, keepdims=True)
    resid = seed_ref[...].astype(F32) + row_norm_back(
        grad_second_in, normal_two, inverse_two, gain_second[...]
    )
    block_out = nt(hidden_ref[:, :hidden_here], reduce_w[0]) + nt(
        hidden_ref[:, hidden_here:hidden_width], reduce_w[1]
    )
    block_out = (resid_ref[...] + block_out).astype(BF16)
    resid_ref[...] = resid
    resid_low = resid.astype(BF16)
    left_ref[:, half_model:] = resid_low[:, :half_model]
    pre_ref[:, start + half_model :] = resid_low[:, half_model:]
    last_columns = slice(hidden_width, hidden_width + 2 * model)
    send(pre_ref, pre_out, 2 * HIDDEN_BLOCKS + 1, last_columns).start()
    grad_heads_in = jnp.concatenate([nn(resid_low, merge_w[hh]) for hh in range(2)], axis=1)
    wait_all(inputs[4:])
    block_ref[...] = nt(block_out, place_ref[...]).astype(BF16)
    normal_heads, inverse_heads = row_norm(att_ref[...])
    grad_heads[...] = jnp.sum(grad_heads_in * normal_heads, axis=0, keepdims=True)
    grad_att = row_norm_back(
        grad_heads_in, normal_heads, inverse_heads, gain_heads[...]
    ).astype(BF16)
    grad_ref[...] = grad_att
    grad_scr[:, :model] = grad_att.astype(F32) * att_ref[...]
    across = (iota((2 * HD, 2 * HD), 0) // HD != iota((2 * HD, 2 * HD), 1) // HD).astype(BF16)
    def for_row(r, carry):
        here = pl.ds(pl.multiple_of(r * positions, positions), positions)
        for pair in range(heads // 2):
            columns = slice(2 * pair * HD, 2 * (pair + 1) * HD)
            top, middle, _ = three_parts(grad_scr[here, columns])
            dots = nn(top, across) + nn(middle, across)
            stats = jnp.zeros((positions, 2 * HD), F32)
            for index, part in enumerate(three_parts(lse_ref[here, columns]) + three_parts(dots)):
                stats = jnp.where(inside_lane == index, part.astype(F32), stats)
            stats_ref[here, columns] = stats.astype(BF16)
            grad = grad_ref[here, columns].astype(F32)
            tile_scr[2 * pair] = jnp.where(side, grad, stats)
            tile_scr[2 * pair + 1] = jnp.where(side, stats, grad)
        for head in range(heads):
            tile = tile_scr[head, pl.ds(offs[head], groups, stride=DILATION_SMALL), :]
            if head % 2:
                tile = jnp.concatenate([tile[:, HD:], tile[:, :HD]], axis=1)
            slot_ref[r * heads + head] = tile.astype(BF16)
        return carry

    lax.fori_loop(0, tokens // positions, for_row, 0)
    for index in range(HIDDEN_BLOCKS):
        columns = slice(index * block, (index + 1) * block)
        send(hidden_ref, hidden_out, index, columns).wait()
        send(pre_ref, pre_out, HIDDEN_BLOCKS + 1 + index, columns).wait()
    send(hidden_ref, hidden_out, HIDDEN_BLOCKS, seed_columns).wait()
    send(pre_ref, pre_out, 2 * HIDDEN_BLOCKS + 1, last_columns).wait()


def far_back_kernel(parity_ref, qkv_ref, grad_ref, out_ref, kv_scr, total_scr):
    devices, _, groups, _ = qkv_ref.shape
    slots = devices * groups
    block = min(slots, 256)
    per_block = block // groups
    parity = parity_ref[pl.program_id(0)]
    kv_scr[...] = qkv_ref[:, 0].reshape(slots, 3 * HD)[:, HD:]
    total_scr[...] = jnp.zeros_like(total_scr)

    def body(index):
        piece = pl.ds(index * per_block, per_block)
        query = qkv_ref[piece, 0].reshape(block, 3 * HD)[:, :HD]
        tile = grad_ref[piece, 0].reshape(block, 2 * HD)
        key, value = kv_scr[:, :HD], kv_scr[:, HD:]
        grad = tile[:, :HD]
        stats = tile[:, HD:].astype(F32)
        log = stats[:, 0:1] + stats[:, 1:2] + stats[:, 2:3]
        dots = stats[:, 3:4] + stats[:, 4:5] + stats[:, 5:6]
        allowed, live = far_masks(parity, index * block, block, slots)
        score = jnp.where(allowed & live, nt(query, key) * SCALE - log, MASKED_SCORE)
        weight = jnp.exp(score)
        grad_score = (weight * (nt(grad, value) - dots)).astype(BF16)
        grad_query = nn(grad_score, key) * SCALE
        total_scr[:, :HD] += tn(grad_score, query) * SCALE
        total_scr[:, HD:] += tn(weight.astype(BF16), grad)
        out_ref[piece, 0, :, :HD] = grad_query.astype(BF16).reshape(per_block, groups, HD)

    for_blocks(slots // block, body)
    out_ref[:, 0, :, HD:] = total_scr[...].astype(BF16).reshape(devices, groups, 2 * HD)


def near_back_kernel(bias_ref, qkv_ref, grad_ref, stats_ref, out_ref, weight_scr, score_scr):
    positions, model = grad_ref.shape
    heads = model // HD
    per_group = heads // 2
    width = per_group * HD
    low, high = side_masks()
    inside = iota((1, 2 * HD), 1) & (HD - 1)
    less_log = jnp.where(inside < 3, -1.0 / SCALE, 0.0).astype(BF16)
    less_dots = jnp.where((inside >= 3) & (inside < 6), -1.0, 0.0).astype(BF16)

    bias = bias_ref[0]
    for pair in range(heads // 2):
        cq, ck, cv = pair_columns(pair, per_group, width)
        own = slice(2 * pair * HD, 2 * (pair + 1) * HD)
        query, key, value = qkv_ref[:, cq], qkv_ref[:, ck], qkv_ref[:, cv]
        grad, stats = grad_ref[:, own], stats_ref[:, own]
        for side, (mine, other) in enumerate(((low, high), (high, low))):
            more = stats * other
            score = nt(query * mine + more, key * mine + less_log * other)
            weight = jnp.exp(score * SCALE + bias)
            through = nt(grad * mine + more, value * mine + less_dots * other)
            weight_scr[2 * pair + side] = weight.astype(BF16)
            score_scr[2 * pair + side] = (weight * through).astype(BF16)
    for pair in range(heads // 2):
        cq, ck, cv = pair_columns(pair, per_group, width)
        own = slice(2 * pair * HD, 2 * (pair + 1) * HD)
        query, key, grad = qkv_ref[:, cq], qkv_ref[:, ck], grad_ref[:, own]
        even, odd = score_scr[2 * pair], score_scr[2 * pair + 1]
        out_ref[:, cq] = (SCALE * nn(
            jnp.concatenate([even, odd], axis=1),
            jnp.concatenate([key * low, key * high], axis=0),
        )).astype(BF16)
        out_ref[:, ck] = (SCALE * tn(
            jnp.concatenate([even, odd], axis=0),
            jnp.concatenate([query * low, query * high], axis=0),
        )).astype(BF16)
        out_ref[:, cv] = (tn(
            jnp.concatenate([weight_scr[2 * pair], weight_scr[2 * pair + 1]], axis=0),
            jnp.concatenate([grad * low, grad * high], axis=0),
        )).astype(BF16)


def join_back_kernel(offs, near_ref, far_ref, first_ref, out_ref):
    positions, model = first_ref.shape
    heads = model // HD
    per_group = heads // 2
    width = per_group * HD
    groups = far_ref.shape[1]
    out_ref[:, 3 * model :] = first_ref[:, model // 2 :]

    for pair in range(heads // 2):
        even, odd = far_ref[2 * pair], far_ref[2 * pair + 1]
        spread = slot_spread(offs, pair, groups, positions)
        for e, columns in enumerate(pair_columns(pair, per_group, width)):
            part = slice(e * HD, (e + 1) * HD)
            far = nn(spread, beside(even[:, part], odd[:, part]))
            out_ref[:, columns] = (near_ref[:, columns].astype(F32) + far).astype(BF16)


def weight_grad_kernel(
    change, core_ref, left, right_0, right_1, left_got, right_0_got, right_1_got,
    *refs,
):
    kept_ref, sent_ref, left_scr = refs[-3:]
    block = kept_ref.shape[1]
    if len(refs) > 3:
        sent_ref[2 * block :] = refs[0][...]
    step = pl.program_id(0)

    @pl.when((step == 0) | (step == change))
    def _():
        left_scr[0] = left[...].T
        left_scr[1] = left_got[...].T

    product = [
        nn(left_scr[0], right[...]) + nn(left_scr[1], got[...])
        for right, got in ((right_0, right_0_got), (right_1, right_1_got))
    ]
    kept_ref[0] = product[0][:block].astype(BF16)
    sent_ref[block : 2 * block] = product[1][block:].astype(BF16)
    low, high = product[0][block:], product[1][:block]

    @pl.when(core_ref[0] == 0)
    def _():
        kept_ref[1] = high.astype(BF16)
        sent_ref[:block] = low.astype(BF16)

    @pl.when(core_ref[0] != 0)
    def _():
        kept_ref[1] = low.astype(BF16)
        sent_ref[:block] = high.astype(BF16)


def input_grad_kernel(
    core_ref, x_ref, pack_ref, resid_ref, gain_ref, second_ref, place_ref, w0, w1, w2, w3, w4, w5, w6, w7,
    grad_ref, gain_grad, weights, sems,
):
    span = weights.shape[2]
    copies = stream_copies((w0, w1, w2, w3, w4, w5, w6, w7), slice(None), weights, sems, core_ref[0])
    start_all(copies)
    normal, inverse = row_norm(x_ref[...].astype(F32))
    wait_all(copies)
    grad_first = nt(pack_ref[:, :span], weights[0]) + nt(pack_ref[:, span : 2 * span], weights[1])
    first = jnp.sum(grad_first * normal, axis=0, keepdims=True)
    parts = three_parts(jnp.concatenate([first, second_ref[...]] + [jnp.zeros_like(first)] * 6))
    gain_grad[...] = sum(nt(part, place_ref[...]) for part in parts)
    grad = resid_ref[...] + row_norm_back(grad_first, normal, inverse, gain_ref[...])
    grad_ref[...] = nt(grad.astype(BF16), place_ref[...]).astype(BF16)


def finish_kernel(
    core_ref, kept_ref, got_ref, attend_ref, merge_ref, expand_ref, reduce_ref, gain_ref
):
    rows = attend_ref.shape[1] // 2
    width, hidden = merge_ref.shape[1], expand_ref.shape[1]
    gain_ref[...] = kept_ref[rows:, : 3 * width] + got_ref[rows:, : 3 * width]

    def place_halves(first, second):
        for half, source in enumerate((first, second)):
            here = slice(half * rows, (half + 1) * rows)
            for e in range(3):
                attend_ref[e, here] = source[:rows, e * width : (e + 1) * width]
            start = 3 * width
            expand_ref[here] = source[:rows, start : start + hidden]
            merge_ref[here] = source[:rows, start + hidden : start + hidden + width]
            reduce_ref[here] = source[:rows, start + hidden + width :]

    @pl.when(core_ref[0] == 0)
    def _():
        place_halves(kept_ref, got_ref)

    @pl.when(core_ref[0] != 0)
    def _():
        place_halves(got_ref, kept_ref)


def whole(*shape):
    return pl.BlockSpec(shape, lambda *_: tuple(0 for _ in shape))


def sds(shape, dtype):
    return jax.ShapeDtypeStruct(shape, dtype)


def call(
    kernel, grid, in_specs, out_specs, out_shape, scratch=(), earlier=(), cost=5
):
    def body(*refs):
        kernel(*refs[len(earlier) :])

    return partial(
        pl.pallas_call(
            body,
            grid=grid,
            in_specs=[ANY] * len(earlier) + in_specs,
            out_specs=out_specs,
            out_shape=out_shape,
            scratch_shapes=list(scratch),
            compiler_params=pltpu.CompilerParams(
                dimension_semantics=("arbitrary",) * len(grid), vmem_limit_bytes=VMEM_LIMIT
            ),
            cost_estimate=pl.CostEstimate(
                flops=cost * 1_150_000_000, bytes_accessed=0, transcendentals=0
            ),
        ),
        *earlier,
    )


def per_device(
    inputs,
    attend_weight,
    merge_weight,
    expand_weight,
    reduce_weight,
    gain_first,
    gain_heads,
    gain_second,
    gain_hidden,
    cotangent,
    lengths,
    local_span,
    dilation,
):
    seq_size, head_size = lax.axis_size("seq"), lax.axis_size("head")
    row_count, positions, model = inputs.shape
    rows = row_count // head_size
    tokens = rows * positions
    shard_rows, width = attend_weight.shape[1:]
    heads = width * head_size // HD
    group_heads = heads // head_size
    hidden_here = expand_weight.shape[1]
    hidden_width = hidden_here * head_size
    quarter = model // 4
    groups = positions // DILATION_SMALL
    pairs = rows * heads
    owned = -(-pairs // seq_size)
    padded = owned * seq_size
    seq_index, head_index = lax.axis_index("seq"), lax.axis_index("head")
    core = seq_index & 1
    core_ref = core.reshape(1)

    attend_shard = gather_core(jnp.concatenate(list(attend_weight), axis=1))
    attend_far = jnp.concatenate(gather_far(attend_shard))
    other_shard = jnp.concatenate([expand_weight, merge_weight.T, reduce_weight.T], axis=1)
    other_shard = gather_core(after(other_shard, attend_shard))
    third = other_shard.shape[1] // 3
    other_shards = [
        gate(other_shard[:, i * third : (i + 1) * third], attend_far) for i in range(3)
    ]
    attend_got = exchange_near(attend_far, 0)
    attend_more = exchange_near(attend_far, 1)
    other_pieces = [gather_far(other_shards[0])]
    attend_last = exchange_near(attend_got, 1)
    other_pieces.append(gather_far(gate(other_shards[1], attend_got)))
    other_far = [jnp.concatenate(pieces) for pieces in other_pieces]
    other_got = [exchange_near(other_far[0], 0)]
    attend_last = gate(attend_last, other_got[0])
    other_pieces.append(gather_far(gate(other_shards[2], attend_last)))
    attend_all = (attend_far, attend_got, attend_more, attend_last)
    attend_all = attend_all + tuple(exchange(piece, 1, 0) for piece in attend_all)
    both_gains = jnp.concatenate([gain_heads, gain_hidden])
    partner_gains = exchange(both_gains.reshape(-1, 128), 0, 1).reshape(-1)
    gain_heads_all = jnp.concatenate([gain_heads, partner_gains[:width]])[None]
    gain_hidden_all = jnp.concatenate([gain_hidden, partner_gains[width:]])[None]

    half_rows = shard_rows // 2
    part, near, far, beside, inside = jnp.meshgrid(
        *[jnp.arange(n) for n in (2, 2, seq_size // 4, 2, half_rows)], indexing="ij"
    )
    shard_of = seq_index ^ (4 * far + 2 * near + (beside ^ part))
    feature_of = (shard_of * shard_rows + (core ^ part) * half_rows + inside).reshape(-1)
    feature_of = gate(feature_of, attend_far)

    row_start = head_index * rows
    lengths, local_span, dilation = gate(
        jnp.stack([lengths, local_span, dilation]), attend_far
    )

    def own_rows(tensor):
        return lax.dynamic_slice_in_dim(tensor, row_start, rows, axis=0)

    scalars = jnp.concatenate([own_rows(lengths), (seq_index * positions).reshape(1)])
    both_rows_gains = jnp.pad(jnp.stack([gain_first, gain_second]), ((0, 6), (0, 0)))
    own_block = pl.BlockSpec((rows, positions, model), lambda i, head: (head[0], 0, 0))

    def fixed(*shape):
        return pl.BlockSpec(shape, lambda i, head: tuple(0 for _ in shape))

    place, x_own, seed, own_gains = pl.pallas_call(
        prepare_kernel,
        grid_spec=pltpu.PrefetchScalarGridSpec(
            num_scalar_prefetch=1,
            grid=(1,),
            in_specs=[SMEM, fixed(1, model), fixed(8, model), own_block, own_block],
            out_specs=[
                fixed(model, model), fixed(tokens, model), fixed(tokens, model), fixed(8, model)
            ],
        ),
        out_shape=[
            sds((model, model), BF16), sds((tokens, model), BF16), sds((tokens, model), BF16),
            sds((8, model), F32),
        ],
        compiler_params=pltpu.CompilerParams(vmem_limit_bytes=VMEM_LIMIT),
        cost_estimate=pl.CostEstimate(flops=0, bytes_accessed=0, transcendentals=0),
    )(
        head_index.reshape(1), scalars, feature_of[None], both_rows_gains, inputs, cotangent
    )
    gain_one, gain_two = own_gains[:1], own_gains[1:2]
    places = jnp.arange(positions)
    span_block = places[None, :] // own_rows(local_span)[:, None]
    within = (span_block[:, :, None] == span_block[:, None, :]) & (
        places[None, :] <= places[:, None]
    )
    bias = jnp.where(within, 0.0, MASKED_SCORE).astype(F32)

    local_head = jnp.arange(heads)
    head_ids = (head_index ^ (local_head // group_heads)) * group_heads + local_head % group_heads
    offsets = gate((head_ids % DILATION_SMALL).astype(jnp.int32), attend_far)
    pair_ids = jnp.minimum(seq_index * owned + jnp.arange(owned), pairs - 1)
    pair_rate = own_rows(dilation)[pair_ids // heads]
    pair_head = head_ids[pair_ids % heads]
    parity = jnp.where(
        pair_rate == DILATION_SMALL, 0, 1 + (pair_head % pair_rate) // DILATION_SMALL
    ).astype(jnp.int32)

    model_spec, model_shape = whole(tokens, model), (tokens, model)
    attend_scratch = pltpu.VMEM((2, model, 3 * width), BF16)

    def by_row(size):
        return pl.BlockSpec((positions, size), lambda r: (r, 0))

    def of_row(size):
        return pl.BlockSpec((heads, groups, size), lambda r: (r, 0, 0))

    model_row, qkv_row = by_row(model), by_row(3 * model)
    bias_row = pl.BlockSpec((1, positions, positions), lambda r: (r, 0, 0))
    first_in, qkv, slots, near_out, log_near = call(
        project_kernel,
        (rows,),
        [SMEM, SMEM, model_spec, bias_row, whole(1, model)] + [ANY] * 8,
        [model_row, qkv_row, of_row(3 * HD), model_row, model_row],
        [
            sds(model_shape, BF16),
            sds((tokens, 3 * model), BF16),
            sds((padded, groups, 3 * HD), BF16),
            sds(model_shape, F32),
            sds(model_shape, F32),
        ],
        [
            attend_scratch,
            pltpu.VMEM((heads // 2, 2 * positions, positions), F32),
            pltpu.VMEM((tokens, model), BF16),
            pltpu.VMEM((tokens, 3 * model), BF16),
            pltpu.SemaphoreType.DMA((8,)),
        ],
        cost=20,
    )(core_ref, offsets, x_own, bias, gain_one, *attend_all)
    other_held = [jnp.concatenate([other_far[0], other_got[0]])]
    other_more = [exchange_near(other_held[0], 1)]
    other_got.append(exchange_near(other_far[1], 0))
    other_far.append(gate(jnp.concatenate(other_pieces[2]), other_more[0]))
    other_got.append(exchange_near(other_far[2], 0))
    other_held.append(jnp.concatenate([other_far[1], other_got[1]]))
    other_more.append(exchange_near(other_held[1], 1))
    other_core = [(exchange(other_held[0], 1, 0), exchange(other_more[0], 1, 0))]

    def to_owners(value):
        value = value.reshape(seq_size, owned, groups, value.shape[-1])
        return lax.all_to_all(value, "seq", 0, 0, tiled=True)

    def from_owners(value):
        value = lax.all_to_all(value, "seq", 0, 0, tiled=True)
        return value.reshape(padded, groups, value.shape[-1])

    def by_pair(size):
        return pl.BlockSpec((seq_size, 1, groups, size), lambda i: (0, i, 0, 0))

    def owned_shape(size):
        return sds((seq_size, owned, groups, size), BF16)

    slot_count = seq_size * groups
    kv_scratch = pltpu.VMEM((slot_count, 2 * HD), BF16)
    far_qkv = to_owners(slots)
    far_out = call(
        far_kernel,
        (owned,),
        [SMEM, by_pair(3 * HD)],
        by_pair(2 * HD),
        owned_shape(2 * HD),
        [kv_scratch],
        cost=4,
        earlier=(seed, place, gain_two),
    )(parity, far_qkv)
    far_here = from_owners(far_out)
    other_held.append(
        gate(jnp.concatenate([other_far[2], other_got[2]]), far_out)
    )
    other_more.append(exchange_near(other_held[2], 1))
    other_core.append((exchange(other_held[1], 1, 0), exchange(other_more[1], 1, 0)))
    held_core = exchange(other_held[2], 1, 0)

    other_core.append((held_core, exchange(other_more[2], 1, 0)))
    weights_all = [
        piece for i in range(3) for piece in (other_held[i], other_more[i], *other_core[i])
    ]
    hidden_pack = (tokens, hidden_width + model // 2)
    pre_pack = (tokens, hidden_width + 2 * model)
    low_scratch = pltpu.VMEM(model_shape, BF16)
    full_scratch = pltpu.VMEM(model_shape, F32)
    hidden_scratch = pltpu.VMEM((tokens, hidden_width), F32)
    weight_scratch = pltpu.VMEM((2, model, hidden_here), BF16)
    (
        block_mine, hidden_in, grad_pre, lefts, grad_resid, grad_att, stats, grad_slots,
        grad_heads, grad_second, grad_hidden,
    ) = call(
        hidden_kernel,
        (),
        [SMEM, SMEM, whole(1, model), whole(1, model), whole(1, hidden_width),
         whole(padded, groups, 2 * HD)] + [ANY] * 17,
        [
            model_spec, ANY, ANY, model_spec, model_spec, model_spec, model_spec,
            whole(padded, groups, 2 * HD), whole(1, model), whole(1, model),
            whole(1, hidden_width),
        ],
        [
            sds(model_shape, BF16), sds(hidden_pack, BF16), sds(pre_pack, BF16),
            sds(model_shape, BF16), sds(model_shape, F32), sds(model_shape, BF16),
            sds(model_shape, BF16), sds((padded, groups, 2 * HD), BF16), sds((1, model), F32),
            sds((1, model), F32), sds((1, hidden_width), F32),
        ],
        [
            low_scratch, full_scratch, full_scratch, low_scratch,
            pltpu.VMEM((model, model), BF16), pltpu.VMEM((2, model, width), BF16),
            weight_scratch, weight_scratch, low_scratch, hidden_scratch, hidden_scratch, hidden_scratch,
            pltpu.VMEM(hidden_pack, BF16), pltpu.VMEM(pre_pack, BF16),
            pltpu.VMEM((heads, positions, 2 * HD), F32), pltpu.SemaphoreType.DMA((5, 8)),
            pltpu.SemaphoreType.DMA((5,)), pltpu.SemaphoreType.DMA((2 * HIDDEN_BLOCKS + 2,)),
        ],
        cost=8,
    )(
        core_ref, offsets, gain_heads_all, gain_two, gain_hidden_all, far_here, near_out,
        log_near, x_own, seed, place, *weights_all,
    )

    def weight_grad(
        size, left, left_at, right, right_at, left_got_at, earlier=(), change=0, extra=None
    ):
        got = exchange(right, 1, 0)

        def spec(at):
            return pl.BlockSpec((tokens, width), lambda j: (0, at(j)))

        def rights():
            return [spec(lambda j, x=x: right_at(x, j)) for x in range(2)]

        sent_rows = 2 * quarter
        extras = []
        if extra is not None:
            sent_rows += GAIN_ROWS
            extras = [extra]
        return call(
            partial(weight_grad_kernel, change),
            (size // width,),
            [SMEM, spec(left_at)] + rights() + [spec(left_got_at)] + rights()
            + [pl.BlockSpec((GAIN_ROWS, width), lambda j: (0, j))] * len(extras),
            [
                pl.BlockSpec((2, quarter, width), lambda j: (0, 0, j)),
                pl.BlockSpec((sent_rows, width), lambda j: (0, j)),
            ],
            [sds((2, quarter, size), BF16), sds((sent_rows, size), BF16)],
            [pltpu.VMEM((2, model // 2, tokens), BF16)],
            earlier=earlier,
            cost=7,
        )(core_ref, left, right, right, got, got, got, *extras)

    per_half = hidden_here // width
    hidden_blocks = hidden_width // width

    def both_rows(mine, earlier=None):
        mine = mine.reshape(rows, positions, model)
        other = exchange(mine, 0, 1)
        if earlier is not None:
            other = gate(other, earlier)
        both = jnp.concatenate([other, other])
        return lax.dynamic_update_slice_in_dim(both, mine, row_start, axis=0)

    far_grads = to_owners(grad_slots)
    near_grad = call(
        near_back_kernel,
        (rows,),
        [bias_row, qkv_row, model_row, model_row],
        qkv_row,
        sds((tokens, 3 * model), BF16),
        [pltpu.VMEM((heads, positions, positions), BF16)] * 2,
        cost=60,
    )(bias, qkv, grad_att, stats)
    reduce_kept, reduce_sent = weight_grad(
        hidden_here, seed, lambda j: 0, hidden_in, lambda x, j: x * per_half + j,
        lambda j: hidden_blocks, earlier=(near_grad,),
    )
    far_back = call(
        far_back_kernel,
        (owned,),
        [SMEM, by_pair(3 * HD), by_pair(2 * HD)],
        by_pair(3 * HD),
        owned_shape(3 * HD),
        [kv_scratch, pltpu.VMEM((slot_count, 2 * HD), F32)],
        earlier=(reduce_sent,),
        cost=0,
    )(parity, far_qkv, far_grads)
    expand_kept, expand_sent = weight_grad(
        hidden_here + width, lefts, lambda j: jnp.where(j < per_half, 0, 1), grad_pre,
        lambda x, j: jnp.where(j < per_half, x * per_half + j, hidden_blocks + x),
        lambda j: hidden_blocks + 2 + jnp.where(j < per_half, 0, 1),
        earlier=(far_back,), change=per_half,
    )
    back_here = from_owners(far_back)
    block_out = both_rows(block_mine, expand_sent)
    reduce_kept, reduce_sent, _ = scatter_first(reduce_kept, reduce_sent)
    grad_pack_shape = (tokens, 3 * model + model // 2)
    grad_pack = call(
        join_back_kernel,
        (rows,),
        [SMEM, qkv_row, of_row(3 * HD), model_row],
        by_row(grad_pack_shape[1]),
        sds(grad_pack_shape, BF16),
        earlier=(reduce_sent, block_out),
        cost=1,
    )(offsets, near_grad, back_here, first_in)
    grad_mine, grad_shared = call(
        input_grad_kernel,
        (),
        [
            SMEM, model_spec, whole(*grad_pack_shape), model_spec, whole(1, model),
            whole(1, model), whole(model, model),
        ]
        + [ANY] * 8,
        [model_spec, whole(8, model)],
        [sds(model_shape, BF16), sds((8, model), F32)],
        [attend_scratch, pltpu.SemaphoreType.DMA((8,))],
        cost=3,
    )(core_ref, x_own, grad_pack, grad_resid, gain_one, grad_second, place, *attend_all)

    expand_kept, expand_sent, _ = scatter_first(
        gate(expand_kept, grad_mine), expand_sent
    )
    def by_head(grad):
        size = grad.shape[1] // 2
        return jnp.where(head_index == 0, grad[0], jnp.roll(grad[0], size))

    grad_shared = gate(grad_shared, expand_sent)
    gains = jnp.concatenate(
        [
            grad_shared[0], grad_shared[1], by_head(grad_heads), by_head(grad_hidden),
        ]
    )
    gain_rows = -(-gains.shape[0] // (3 * width))
    gains = jnp.pad(gains, (0, gain_rows * 3 * width - gains.shape[0])).reshape(gain_rows, -1)
    gain_sent = to_rows(gains)
    reduce_kept, reduce_sent, _ = scatter_second(reduce_kept, reduce_sent)
    attend_kept, attend_sent = weight_grad(
        3 * width, first_in, lambda j: 0, grad_pack, lambda x, j: 3 * x + j, lambda j: 6,
        earlier=(grad_mine, *reduce_sent), extra=gain_sent,
    )
    attend_kept, attend_sent, attend_near = scatter_first(attend_kept, attend_sent)
    gains = from_rows(gain_sent, gain_rows) + from_rows(attend_near[2 * quarter :], gain_rows)
    gain_sent = to_rows(gains)
    reduce_total = scatter_far(reduce_kept, reduce_sent)
    expand_kept, expand_sent, _ = scatter_second(expand_kept, expand_sent)
    attend_sent = after(after(attend_sent, reduce_total), expand_sent[0])
    attend_kept, attend_sent, attend_got = scatter_second(
        attend_kept, jnp.concatenate([attend_sent, gain_sent])
    )
    gains = from_rows(gain_sent, gain_rows) + from_rows(attend_got[quarter:], gain_rows)
    stages = far_stages(seq_size)
    for stage in reversed(range(len(stages))):
        unit, radix = stages[stage]
        gain_sent = to_rows(gains)
        everyone = [from_rows(gain_sent, gain_rows)]
        rows_sent = attend_sent[0].shape[0]
        for i, piece in enumerate(attend_sent):
            got = exchange(jnp.concatenate([piece, gain_sent]), unit * (i + 1), 0)
            attend_kept = attend_kept + got[:rows_sent].astype(F32)
            everyone.append(from_rows(got[rows_sent:], gain_rows))
        while len(everyone) > 1:
            everyone = [one + two for one, two in zip(everyone[::2], everyone[1::2])]
        gains = everyone[0]
        if stage:
            held = attend_kept.reshape(stages[stage - 1][1], -1, 3 * width)
            attend_kept, attend_sent = held[0], [piece.astype(BF16) for piece in held[1:]]
    grad_inputs = both_rows(gate(grad_mine, attend_got))
    expand_total = scatter_far(gate(expand_kept, attend_got), expand_sent)
    totals = jnp.concatenate([attend_kept, expand_total, reduce_total], axis=1)
    gains = jnp.pad(gains, ((0, 8 - gain_rows), (0, totals.shape[1] - gains.shape[1])))
    last_kept = jnp.concatenate([totals[:half_rows], gains])
    last_got = exchange(jnp.concatenate([totals[half_rows:], gains]), 1, 0)
    last_shape = last_kept.shape
    grad_attend, grad_merge, grad_expand, grad_reduce, gains = call(
        finish_kernel,
        (),
        [SMEM, whole(*last_shape), whole(*last_shape)],
        [
            whole(3, shard_rows, width), whole(shard_rows, width), whole(shard_rows, hidden_here),
            whole(shard_rows, hidden_here), whole(8, 3 * width),
        ],
        [
            sds((3, shard_rows, width), F32), sds((shard_rows, width), F32),
            sds((shard_rows, hidden_here), F32), sds((shard_rows, hidden_here), F32),
            sds((8, 3 * width), F32),
        ],
        cost=1,
    )(core_ref, last_kept, last_got)
    gains = gains[:gain_rows].reshape(-1)

    def own_half(start, size):
        return jnp.where(
            head_index == 0, gains[start : start + size], gains[start + size : start + 2 * size]
        )

    return (
        block_out,
        grad_inputs,
        grad_attend,
        grad_merge.T,
        grad_expand,
        grad_reduce.T,
        gains[:model],
        own_half(2 * model, width),
        gains[model : 2 * model],
        own_half(3 * model, hidden_here),
    )


def solution(mesh):
    placed = (
        P(None, "seq", None),
        P(None, "seq", "head"),
        P("head", "seq"),
        P("seq", "head"),
        P("head", "seq"),
        P(),
        P("head"),
        P(),
        P("head"),
        P(None, "seq", None),
        P(),
        P(),
        P(),
    )
    return jax.shard_map(
        per_device,
        mesh=mesh,
        in_specs=placed,
        out_specs=(
            P(None, "seq", None),
            P(None, "seq", None),
            P(None, "seq", "head"),
            P("head", "seq"),
            P("seq", "head"),
            P("head", "seq"),
            P(),
            P("head"),
            P(),
            P("head"),
        ),
        check_vma=False,
    )
```
